32 devices in a mesh: lon: 8 (over z, core), lat: 4 (over y, x).
Axes of the slice: x: 2, y: 2, z: 4, core: 2. Of those that a mesh axis runs over, the one named last changes fastest.
Arguments:
- state: float32 [150, 128, 1024], P(None, 'lat', 'lon'), may hold values from -6 to 6
- diffusivity: float32 [150, 128, 1024], P(None, 'lat', 'lon'), may hold values from 0.02 to 0.24
- sea_mask: int32 [75, 128, 1024], P(None, 'lat', 'lon'), may hold values 0 or 1
- send_cols: int32 [32, 768], P(('lon', 'lat')), may hold values from 0 to 4096, as said below
- obs_slots: int32 [4, 65536], P(None, ('lon', 'lat')), may hold values from 0 to 767, as said below
- obs_weights: float32 [4, 65536], P(None, ('lon', 'lat')), may hold values from 0.05 to 0.5
- obs_precision: float32 [150, 65536], P(None, ('lon', 'lat')), may hold values from 0.25 to 4
Outputs:
- product: float32 [150, 128, 1024], P(None, 'lat', 'lon')
- equivalents: float32 [150, 65536], P(None, ('lon', 'lat'))
The draws below stay inside these ranges and needn't reach their ends.
Inputs may be any that keep to these rules, and one draw needn't show every extreme that they name: `send_cols`: for each device s and owner o the first n entries of the owner's 24 entries are local column indices below 4096, the rest are 4096; n is at least 1 and at most 24; every device has some owner with n = 24, and some owner receives 24 columns from every device. `obs_slots`: every slot named refers to a live entry: for owner o, slot s * 24 + p with p below the number of live entries of device s for owner o.
All inputs are finite; a program needn't handle non-finite values. No bound on the sum of `sea_mask` on one device may be relied on, other than what follows from the above.
Results may differ from the reference program's by a relative error of at most 0.00002.
Values sent between devices are 32-bit elements; how exact they have to be, the bound alone decides.
No kernel may reach another device: no remote copies, remote signals or barrier semaphores. Data moves between devices by JAX's collectives and lax.ppermute only.
A program may use at most 128 MiB of HBM per device.

```python
import math
import jax
import jax.numpy as jnp
from jax import lax

LEVELS = 75
VALS = 150
CLAT = 32
CLON = 128
SWEEPS = 2
CAP = 24
OBS_DEV = 2048
OWNERS = 32
CELLS = 4096
NLAT = 128
NLON = 1024
NOBS = 65536
N_LON = 8
N_LAT = 4


def pair_counts(key):
    base = jax.random.fold_in(key, 11)
    first, second, third = jax.random.split(base, 3)
    counts = jax.random.randint(first, (OWNERS, OWNERS), CAP // 3, CAP + 1)
    order = jax.random.permutation(second, OWNERS)
    counts = counts.at[jnp.arange(OWNERS), order].set(CAP)
    full_owner = jax.random.randint(third, (), 0, OWNERS)
    counts = counts.at[:, full_owner].set(CAP)
    sparse_owner = jnp.where(order[1] == full_owner, order[2], order[1])
    counts = counts.at[0, sparse_owner].set(1)
    return counts


def draw_send_cols(key, part):
    counts = pair_counts(key)
    cell_ids = jax.random.randint(jax.random.fold_in(key, 12), (OWNERS, OWNERS, CAP), 0, CELLS)
    cell_ids = cell_ids.at[0, :, 0].set(0)
    position = jnp.arange(CAP)
    live = position[None, None, :] < counts[:, :, None]
    return jnp.where(live, cell_ids, CELLS).reshape(OWNERS, OWNERS * CAP).astype(jnp.int32)


def draw_obs_slots(key, part):
    counts = pair_counts(key)
    base = jax.random.fold_in(key, 13)
    first, second = jax.random.split(base, 2)
    source = jax.random.randint(first, (4, OWNERS, OBS_DEV), 0, OWNERS)
    owner_ids = jnp.arange(OWNERS)[None, :, None]
    limits = counts[source, owner_ids]
    position = jax.random.randint(second, (4, OWNERS, OBS_DEV), 0, limits)
    slot_ids = source * CAP + position
    slot_ids = slot_ids.at[0, :, 0].set((OWNERS - 1) * CAP + counts[OWNERS - 1, :] - 1)
    slot_ids = slot_ids.at[1, :, 0].set(0)
    return slot_ids.reshape(4, OWNERS * OBS_DEV).astype(jnp.int32)


def touch_ends(values, rng, least, largest):
    longest = values.shape.index(max(values.shape))
    spots = []
    for shift in (0, 1):
        where = [jax.random.randint(jax.random.fold_in(rng, axis), (), 0, length) for axis, length in enumerate(values.shape)]
        where[longest] = (where[longest] + shift) % values.shape[longest]
        spots.append(tuple(where))
    return values.at[spots[0]].set(least).at[spots[1]].set(largest)


def block_scale(own_key, extent, cuts, smallest, high):
    def one(dim, parts):
        steps = jax.random.uniform(jax.random.fold_in(jax.random.fold_in(own_key, 6), dim), (parts,), jnp.float32, smallest / len(cuts), high / len(cuts))
        return jnp.repeat(jnp.exp(steps), extent[dim] // parts).reshape((-1,) + (1,) * (len(extent) - dim - 1))

    loudness = one(*cuts[0])
    for cut in cuts[1:]:
        loudness = loudness * one(*cut)
    return loudness


def noise(own_key, extent, deviation, bound, cuts=(), held_as=jnp.bfloat16):
    array = deviation * jax.random.normal(own_key, extent, jnp.float32)
    if cuts:
        array = array * block_scale(own_key, extent, cuts, -0.22, 0.18)
    return jnp.clip(array, -bound, bound).astype(held_as)


def setup_inputs(seed: int = 0) -> dict:
    arg_keys = jax.random.split(jax.random.key(seed), 8)
    return {
        "state": noise(arg_keys[0], (VALS, NLAT, NLON), 1.0, 6.0, ((1, 4), (2, 8)), jnp.float32),
        "diffusivity": jnp.clip(0.02 + 0.22 * jax.random.uniform(arg_keys[1], (VALS, NLAT, NLON), jnp.float32) ** block_scale(arg_keys[1], (VALS, NLAT, NLON), ((1, 4), (2, 8)), -0.2, 0.2), 0.02, 0.24),
        "sea_mask": touch_ends((jax.random.randint(arg_keys[2], (LEVELS, NLAT, NLON), 0, 10) < 9).astype(jnp.int32), jax.random.fold_in(arg_keys[2], 1), 0, 1),
        "send_cols": draw_send_cols(jax.random.fold_in(arg_keys[7], 71), 0),
        "obs_slots": draw_obs_slots(jax.random.fold_in(arg_keys[7], 71), 0),
        "obs_weights": jnp.clip(0.05 + 0.45 * jax.random.uniform(arg_keys[5], (4, NOBS), jnp.float32) ** block_scale(arg_keys[5], (4, NOBS), ((1, 32),), -0.2, 0.2), 0.05, 0.5),
        "obs_precision": jnp.clip(jnp.exp(math.log(4.0) - 2.7725887 * jax.random.uniform(arg_keys[6], (VALS, NOBS), jnp.float32) ** block_scale(arg_keys[6], (VALS, NOBS), ((1, 32),), -0.2, 0.2)), 0.25, 4.0),
    }


def widen(field):
    field = jnp.concatenate([field[:, :, -1:], field, field[:, :, :1]], axis=2)
    return jnp.pad(field, ((0, 0), (1, 1), (0, 0)))


def relax_step(wide_field, wide_coef):
    centre = wide_field[:, 1:-1, 1:-1]
    centre_coef = wide_coef[:, 1:-1, 1:-1]
    total = jnp.minimum(centre_coef, wide_coef[:, 2:, 1:-1]) * (wide_field[:, 2:, 1:-1] - centre)
    total = total + jnp.minimum(centre_coef, wide_coef[:, :-2, 1:-1]) * (wide_field[:, :-2, 1:-1] - centre)
    total = total + jnp.minimum(centre_coef, wide_coef[:, 1:-1, :-2]) * (wide_field[:, 1:-1, :-2] - centre)
    total = total + jnp.minimum(centre_coef, wide_coef[:, 1:-1, 2:]) * (wide_field[:, 1:-1, 2:] - centre)
    return centre + total


def diffuse(field, conduct):
    wide_coef = widen(conduct)
    for sweep in range(SWEEPS):
        field = relax_step(widen(field), wide_coef)
    return field


def to_blocks(field):
    vals = field.shape[0]
    shaped = field.reshape(vals, N_LAT, CLAT, N_LON, CLON).transpose(0, 3, 1, 2, 4)
    return shaped.reshape(vals, OWNERS, CLAT * CLON)


def from_blocks(blocks):
    vals = blocks.shape[0]
    shaped = blocks.reshape(vals, N_LON, N_LAT, CLAT, CLON).transpose(0, 2, 3, 1, 4)
    return shaped.reshape(vals, NLAT, NLON)


def reference(state, diffusivity, sea_mask, send_cols, obs_slots, obs_weights, obs_precision):
    vals = state.shape[0]
    sea_float = sea_mask.astype(jnp.float32)
    conduct = diffusivity * jnp.concatenate([sea_float, sea_float], axis=0)
    smooth = diffuse(state, conduct)
    blocks = to_blocks(smooth)
    padded = jnp.concatenate([blocks, jnp.zeros((vals, OWNERS, 1), jnp.float32)], axis=2)
    sources = jnp.arange(OWNERS, dtype=jnp.int32)[:, None]

    def per_owner(adjoint_sum, owner):
        picked = lax.dynamic_slice_in_dim(send_cols, owner * CAP, CAP, 1)
        gathered = padded[:, sources, picked].reshape(vals, OWNERS * CAP)
        slot_ids = lax.dynamic_slice_in_dim(obs_slots, owner * OBS_DEV, OBS_DEV, 1)
        weights = lax.dynamic_slice_in_dim(obs_weights, owner * OBS_DEV, OBS_DEV, 1)
        inverse_var = lax.dynamic_slice_in_dim(obs_precision, owner * OBS_DEV, OBS_DEV, 1)
        equivalent = jnp.zeros((vals, OBS_DEV), jnp.float32)
        for tap in range(obs_slots.shape[0]):
            equivalent = equivalent + weights[tap][None, :] * gathered[:, slot_ids[tap]]
        weighted = inverse_var * equivalent
        returned = jnp.zeros((vals, OWNERS * CAP), jnp.float32)
        for tap in range(obs_slots.shape[0]):
            returned = returned.at[:, slot_ids[tap]].add(weights[tap][None, :] * weighted)
        adjoint_sum = adjoint_sum.at[:, sources, picked].add(returned.reshape(vals, OWNERS, CAP))
        return adjoint_sum, equivalent

    start_sum = jnp.zeros((vals, OWNERS, CLAT * CLON + 1), jnp.float32)
    adjoint_sum, stacked = lax.scan(per_owner, start_sum, jnp.arange(OWNERS, dtype=jnp.int32))
    equivalents = stacked.transpose(1, 0, 2).reshape(vals, OWNERS * OBS_DEV)
    adjoint = from_blocks(adjoint_sum[:, :, :CLAT * CLON])
    product = state + diffuse(adjoint, conduct)
    return product, equivalents
```

```python
import functools

import jax
import jax.numpy as jnp
from jax import lax
from jax.experimental import pallas as pl
from jax.experimental.pallas import tpu as pltpu
from jax.sharding import PartitionSpec as P

CAP = 24
LANES = 128
GROUPS = 5
ROWS = 32
OBS_BLOCK = 256
F32, BF16 = jnp.float32, jnp.bfloat16
MIB = 1 << 20


def up(n, k):
    return -(-n // k) * k


def roll(x, k):
    k %= LANES
    return x if k == 0 else pltpu.roll(x, k, axis=1)


def lane_of(x):
    return lax.broadcasted_iota(jnp.int32, x.shape, 1)


def tall(x, rows):
    return jnp.concatenate([x, jnp.zeros((rows - x.shape[0], x.shape[1]), x.dtype)], axis=0)


def halves(x):
    hi = x.astype(BF16)
    return hi, (x - hi.astype(F32)).astype(BF16)


def dot(a, b):
    return lax.dot_general(a, b, (((1,), (0,)), ((), ())), preferred_element_type=F32)


def dot_nt(a, b):
    return lax.dot_general(a, b, (((1,), (1,)), ((), ())), preferred_element_type=F32)


def stacked(x):
    return jnp.concatenate(halves(x), axis=0)


def folded(x):
    n = x.shape[0] // 2
    return x[:n] + x[n:]


def row_edges(c):
    east = jnp.where(lane_of(c) == LANES - 1, 0.0, jnp.minimum(c, roll(c, -1)))
    return east, roll(east, 1)


def pack_edges(cp):
    lane = lane_of(cp)
    kind = lane & 3
    inner = jnp.where(kind == 1, roll(cp, 1), roll(cp, -1))
    inner = jnp.where((kind == 1) | (kind == 2), jnp.minimum(cp, inner), 0.0)
    south = jnp.where(lane >= LANES - 4, 0.0, jnp.minimum(cp, roll(cp, -4)))
    return kind, inner, south, roll(south, 4)


def rim_rows(v0, v1, v30, v31, c0, c1, c30, c31):
    out = []
    for v, w, c, d in ((v0, v1, c0, c1), (v31, v30, c31, c30)):
        east, west = row_edges(c)
        out.append(v + east * (roll(v, -1) - v) + west * (roll(v, 1) - v) + jnp.minimum(c, d) * (w - v))
    return out


def rim_pack(vp, cp):
    kind, inner, south, north = pack_edges(cp)
    beside = jnp.where(kind == 1, roll(vp, 1), roll(vp, -1))
    return vp + inner * (beside - vp) + south * (roll(vp, -4) - vp) + north * (roll(vp, 4) - vp)


def pack_messages(vp, cp, pp):
    kind = lane_of(vp) & 3
    east = jnp.where(kind == 0, roll(vp, -1), jnp.where(kind == 1, cp, roll(pp, 1)))
    west = jnp.where(kind == 0, roll(vp, -2), jnp.where(kind == 1, roll(cp, -1), pp))
    return east, west


def ghost_pack(from_w, from_e):
    one = (lane_of(from_w) & 3) == 1
    v = jnp.where(one, roll(from_e, 1), roll(from_w, 2))
    c = jnp.where(one, from_e, roll(from_w, 1))
    p = jnp.where(one, roll(from_e, -1), from_w)
    return v, c, p


CORNER_LANES = (1, 2, LANES - 3, LANES - 2)


def corner_messages(vp, cp):
    vt, ct = tall(vp, 256).T, tall(cp, 256).T
    row = lax.broadcasted_iota(jnp.int32, (8, 256), 0)
    return [jnp.where(row == 0, vt[k : k + 1], jnp.where(row == 1, ct[k : k + 1], 0.0)) for k in CORNER_LANES]


def corner_pack(messages, which, rows):
    row = lax.broadcasted_iota(jnp.int32, (LANES, 256), 0)
    t = jnp.zeros((LANES, 256), F32)
    for k, m in zip(CORNER_LANES, messages):
        t = jnp.where(row == k, m[which : which + 1], t)
    return t.T[:rows]


def rim_correction(own, coef, ghosts):
    v0, v31, p0, p31, vp, pp = own
    c0, c1, c30, c31, cp = coef
    (gvn, gcn, gpn), (gvs, gcs, gps), (gv, gc, gp), (kv, kc) = ghosts
    lane = lane_of(v0)
    ends = (lane == 0) | (lane == LANES - 1)
    kind, inner, south, north = pack_edges(cp)
    mid = (kind == 1) | (kind == 2)
    mg = jnp.where(mid, jnp.minimum(cp, gc), 0.0)
    f = mg * (gv - vp)
    mn, ms = jnp.minimum(c0, gcn), jnp.minimum(c31, gcs)
    fn, fs = mn * (gvn - v0), ms * (gvs - v31)
    ghost = gp - f + jnp.where(mid, jnp.minimum(gc, kc), 0.0) * (kv - gv)
    ghost_n = gpn - fn + jnp.where(ends, jnp.minimum(gcn, roll(kc, -2)), 0.0) * (roll(kv, -2) - gvn)
    ghost_s = gps - fs + jnp.where(ends, jnp.minimum(gcs, roll(kc, 2)), 0.0) * (roll(kv, 2) - gvs)
    whole = pp + f + jnp.where((lane == 1) | (lane == 2), roll(fn, 2), 0.0)
    whole = whole + jnp.where((lane == LANES - 3) | (lane == LANES - 2), roll(fs, -2), 0.0)
    whole_n = p0 + fn + jnp.where(ends, roll(f, -2), 0.0)
    whole_s = p31 + fs + jnp.where(ends, roll(f, 2), 0.0)
    qf = inner * f
    rp = f - qf + south * (roll(f, -4) - f) + north * (roll(f, 4) - f) + mg * (ghost - whole)
    rp = jnp.where(mid, rp, jnp.where(kind == 0, roll(qf, -1), roll(qf, 1)))
    rows = []
    for c, d, m, g, w, x in ((c0, c1, mn, ghost_n, whole_n, fn), (c31, c30, ms, ghost_s, whole_s, fs)):
        east, west = row_edges(c)
        across = jnp.minimum(c, d)
        rows.append(x + east * (roll(x, -1) - x) + west * (roll(x, 1) - x) - across * x + m * (g - w))
        rows.append(across * x)
    return rows[0], rows[1], rows[3], rows[2], rp


def two_sweeps(load_v, load_c, store):
    x, c = load_v(0), load_c(0)
    last = lane_of(x) == LANES - 1
    zero = jnp.zeros_like(x)
    f_up, g_up = zero, zero
    before = None
    for i in range(ROWS):
        if i < ROWS - 1:
            xn, cn = load_v(i + 1), load_c(i + 1)
            across = jnp.minimum(c, cn)
            f = across * (xn - x)
        else:
            f = zero
        east = jnp.where(last, 0.0, jnp.minimum(c, roll(c, -1)))
        e = east * (roll(x, -1) - x)
        y = x + (e - roll(e, 1)) + (f - f_up)
        if before is not None:
            yb, hb, across_b = before
            g = across_b * (y - yb)
            store(i - 1, yb + hb + (g - g_up))
            g_up = g
        h = east * (roll(y, -1) - y)
        before = (y, h - roll(h, 1), across)
        f_up = f
        if i < ROWS - 1:
            x, c = xn, cn
    yb, hb, _ = before
    store(ROWS - 1, yb + hb - g_up)


def chosen(cells, ids):
    return jnp.where(ids == cells, 1.0, 0.0).astype(BF16)


def rim_ids(n):
    line = lax.broadcasted_iota(jnp.int32, (LANES, n), 0)
    rows = [line + i * LANES for i in (0, 1, ROWS - 2, ROWS - 1)]
    k = line & 3
    pack = (line >> 2) * LANES + jnp.where(k < 2, LANES - 2 + k, k - 2)
    return jnp.concatenate(rows + [pack], axis=0)


def pack_payload(x, out_ref, owners):
    lane = lax.broadcasted_iota(jnp.int32, (ROWS, LANES), 1)
    for o in range(owners):
        a, b = divmod(o, GROUPS)
        block = jnp.zeros((ROWS, LANES), F32)
        for g in range(GROUPS):
            piece = roll(x[ROWS * g : ROWS * (g + 1), LANES * a : LANES * (a + 1)], CAP * (g - b))
            block = jnp.where((lane >= CAP * g) & (lane < CAP * (g + 1)), piece, block)
        out_ref[ROWS * o : ROWS * (o + 1), :] = block


def unpack_payload(in_ref, owners, slots):
    lane = lax.broadcasted_iota(jnp.int32, (ROWS, LANES), 1)
    columns = []
    for a in range(slots // LANES):
        pieces = []
        for g in range(GROUPS):
            piece = jnp.zeros((ROWS, LANES), F32)
            for b in range(GROUPS):
                o = GROUPS * a + b
                if o < owners:
                    block = roll(in_ref[ROWS * o : ROWS * (o + 1), :], CAP * (b - g))
                    piece = jnp.where((lane >= CAP * b) & (lane < CAP * (b + 1)), block, piece)
            pieces.append(piece)
        columns.append(jnp.concatenate(pieces, axis=0))
    return jnp.concatenate(columns, axis=1)


def call(kernel, outs, *args, in_specs=None, scratch=(), vmem=48, flops=0, nbytes=0, **kw):
    any_spec = pl.BlockSpec(memory_space=pltpu.VMEM)
    return pl.pallas_call(
        kernel,
        out_shape=[jax.ShapeDtypeStruct(s, d) for s, d in outs],
        in_specs=in_specs or [any_spec] * len(args),
        scratch_shapes=list(scratch),
        compiler_params=pltpu.CompilerParams(vmem_limit_bytes=vmem * MIB),
        cost_estimate=pl.CostEstimate(flops=flops, bytes_accessed=nbytes, transcendentals=0),
        **kw,
    )(*args)


HBM = pl.BlockSpec(memory_space=pl.ANY)
VMEM = pl.BlockSpec(memory_space=pltpu.VMEM)


def load_fields(vals, refs, scratch, sems):
    state, diff, mask = refs
    sv, sd, sm = scratch
    n = vals * ROWS
    copies = [
        pltpu.make_async_copy(state, sv.at[pl.ds(0, n)], sems.at[0]),
        pltpu.make_async_copy(diff, sd.at[pl.ds(0, n)], sems.at[1]),
        pltpu.make_async_copy(mask, sm.at[pl.ds(0, n // 2)], sems.at[2]),
        pltpu.make_async_copy(mask, sm.at[pl.ds(n // 2, n // 2)], sems.at[3]),
    ]
    for c in copies:
        c.start()
    rest = sv.shape[0] - n
    sv[pl.ds(n, rest), :] = jnp.zeros((rest, LANES), F32)
    sd[pl.ds(n, rest), :] = jnp.zeros((rest, LANES), F32)
    sm[pl.ds(n, rest), :] = jnp.zeros((rest, LANES), jnp.int32)
    for c in copies:
        c.wait()


def grid_row(ref, i, vp):
    return ref[pl.ds(i, vp, stride=ROWS), :]


def prepare_kernel(vals, vp, mp, state, diff, mask, m_n, m_s, m_e, m_w, k_ne, k_nw, k_se, k_sw, rv, rc, pk, sv, sd, sm, sems):
    load_fields(vals, (state, diff, mask), (sv, sd, sm), sems)

    def coef(i):
        return grid_row(sd, i, vp) * grid_row(sm, i, vp).astype(F32)

    lane = lax.broadcasted_iota(jnp.int32, (vp, LANES), 1)
    pv = jnp.zeros((vp, LANES), F32)
    pc = jnp.zeros((vp, LANES), F32)
    for i in range(ROWS):
        here = (lane >> 2) == i
        pv = jnp.where(here, roll(grid_row(sv, i, vp), 4 * i + 2), pv)
        pc = jnp.where(here, roll(coef(i), 4 * i + 2), pc)
    v0, v1, v30, v31 = (grid_row(sv, i, vp) for i in (0, 1, ROWS - 2, ROWS - 1))
    c0, c1, c30, c31 = (coef(i) for i in (0, 1, ROWS - 2, ROWS - 1))
    p0, p31 = rim_rows(v0, v1, v30, v31, c0, c1, c30, c31)
    pp = rim_pack(pv, pc)
    east, west = pack_messages(pv, pc, pp)
    for ref, parts in ((m_n, (v0, c0, p0)), (m_s, (v31, c31, p31)), (m_e, (east,)), (m_w, (west,))):
        for k, x in enumerate(parts):
            ref[mp * k : mp * (k + 1), :] = x[:mp]
    for ref, m in zip((k_ne, k_nw, k_se, k_sw), corner_messages(pv, pc)):
        ref[...] = m
    for ref, parts in ((rv, (v0, v31, p0, p31)), (rc, (c0, c1, c30, c31)), (pk, (pv, pc, pp))):
        for k, x in enumerate(parts):
            ref[vp * k : vp * (k + 1), :] = x


def inner_kernel(vals, vp, state, diff, mask, cells, out, sv, sd, sm, smooth, hot, sems):
    load_fields(vals, (state, diff, mask), (sv, sd, sm), sems)

    def step(t, carry):
        def load(ref, i):
            return ref[pl.ds(t * (16 * ROWS) + i, 16, stride=ROWS), :]

        def store(i, x):
            smooth[pl.ds(t * 16, 16), LANES * i : LANES * (i + 1)] = x

        two_sweeps(lambda i: load(sv, i), lambda i: load(sd, i) * load(sm, i).astype(F32), store)
        return carry

    lax.fori_loop(0, vp // 16, step, 0)
    chunk = hot.shape[1]
    wide = 4 * LANES
    for base in range(0, cells.shape[1], chunk):
        total = jnp.zeros((2 * vp, chunk), F32)
        for k in range(0, ROWS * LANES, wide):
            ids = lax.broadcasted_iota(jnp.int32, (wide, chunk), 0) + k
            hot[k : k + wide, :] = chosen(cells[:, base : base + chunk], ids)
        for k in range(0, ROWS * LANES, wide):
            total = total + dot(stacked(smooth[:, k : k + wide]), hot[k : k + wide, :])
        out[:, base : base + chunk] = folded(total)


def weights_kernel(slots, weights, hi, lo):
    s = slots[...]
    place = s + 8 * jnp.floor((s.astype(F32) + 0.5) * (1.0 / (CAP * GROUPS))).astype(jnp.int32)
    row = lax.broadcasted_iota(jnp.int32, hi.shape, 0)
    total = jnp.zeros(hi.shape, F32)
    for k in range(slots.shape[0]):
        total = total + jnp.where(row == place[k : k + 1], weights[k : k + 1, :], 0.0)
    hi[...], lo[...] = halves(total)


def read_ghosts(vp, mp, f_n, f_s, f_e, f_w, corners):
    def part(ref, k):
        return tall(ref[mp * k : mp * (k + 1), :], vp)

    gn = [part(f_n, k) for k in range(3)]
    gs = [part(f_s, k) for k in range(3)]
    gp = ghost_pack(part(f_w, 0), part(f_e, 0))
    k = [corner_pack([m[...] for m in corners], i, vp) for i in (0, 1)]
    return gn, gs, gp, k


def parts_of(ref, vp):
    return [ref[vp * k : vp * (k + 1), :] for k in range(ref.shape[0] // vp)]


def send_kernel(owners, vp, mp, f_n, f_s, f_e, f_w, k_ne, k_nw, k_se, k_sw, rv, rc, pk, inner, cells, out):
    ghosts = read_ghosts(vp, mp, f_n, f_s, f_e, f_w, (k_ne, k_nw, k_se, k_sw))
    v0, v31, p0, p31 = parts_of(rv, vp)
    pv, pc, pp = parts_of(pk, vp)
    fix = rim_correction((v0, v31, p0, p31, pv, pp), parts_of(rc, vp) + [pc], ghosts)
    slots = cells.shape[1]
    total = folded(dot(stacked(jnp.concatenate(fix, axis=1)), chosen(cells[...], rim_ids(slots))))
    pack_payload(inner[...] + total, out, owners)


def owner_kernel(vals, vp, owners, got, w_hi, w_lo, prec, equiv, back, r2, w2, acc):
    step = pl.program_id(0)

    @pl.when(step == 0)
    def _():
        r2[...] = stacked(unpack_payload(got, owners, acc.shape[1]))
        w2[...] = jnp.zeros(w2.shape, F32)
        acc[...] = jnp.zeros(acc.shape, F32)

    hi, lo = w_hi[...], w_lo[...]
    e = folded(dot(r2[...], hi)) + dot(r2[:vp, :], lo)
    equiv[...] = e[:vals]
    w2[:vals, :] = prec[...] * e[:vals]
    w = stacked(w2[...])
    acc[...] += folded(dot_nt(w, hi)) + dot_nt(w[:vp], lo)

    @pl.when(step == pl.num_programs(0) - 1)
    def _():
        pack_payload(acc[...], back, owners)


def back_kernel(owners, vp, mp, got, cells, rc, pk, m_n, m_s, m_e, m_w, k_ne, k_nw, k_se, k_sw, inc, ra, pa):
    slots = cells.shape[1]
    x = stacked(unpack_payload(got, owners, slots))
    inc[...] = x
    rims = folded(dot_nt(x, chosen(cells[...], rim_ids(slots))))
    v0, v1, v30, v31, pv = (rims[:, LANES * k : LANES * (k + 1)] for k in range(5))
    pc = pk[vp : 2 * vp, :]
    p0, p31 = rim_rows(v0, v1, v30, v31, *parts_of(rc, vp))
    pp = rim_pack(pv, pc)
    east, west = pack_messages(pv, pc, pp)
    for ref, parts in ((m_n, (v0, p0)), (m_s, (v31, p31)), (m_e, (east,)), (m_w, (west,))):
        for k, y in enumerate(parts):
            ref[mp * k : mp * (k + 1), :] = y[:mp]
    for ref, m in zip((k_ne, k_nw, k_se, k_sw), corner_messages(pv, pc)):
        ref[...] = m
    for ref, parts in ((ra, (v0, v31, p0, p31)), (pa, (pv, pp))):
        for k, y in enumerate(parts):
            ref[vp * k : vp * (k + 1), :] = y


def adjoint_kernel(vals, vp, state, diff, mask, inc, cells, out, sv, sd, sm, adj, sems, sem):
    load_fields(vals, (state, diff, mask), (sv, sd, sm), sems)
    wide = 2 * LANES
    slots = cells.shape[1]

    def scatter(k, carry):
        ids = lax.broadcasted_iota(jnp.int32, (wide, slots), 0) + k * wide
        x = folded(dot_nt(inc[...], chosen(cells[...], ids)))
        for j in range(2):
            adj[pl.ds((2 * k + j) * vp, vp), :] = x[:, LANES * j : LANES * (j + 1)]
        return carry

    lax.fori_loop(0, ROWS // 2, scatter, 0)

    def step(t, carry):
        def rows(i):
            return pl.ds(t * (16 * ROWS) + i, 16, stride=ROWS)

        def store(i, x):
            sv[rows(i), :] = sv[rows(i), :] + x

        two_sweeps(
            lambda i: adj[pl.ds(i * vp + t * 16, 16), :],
            lambda i: sd[rows(i), :] * sm[rows(i), :].astype(F32),
            store,
        )
        return carry

    lax.fori_loop(0, vp // 16, step, 0)
    copy = pltpu.make_async_copy(sv.at[pl.ds(0, vals * ROWS)], out, sem)
    copy.start()
    copy.wait()


def final_kernel(vals, vp, mp, f_n, f_s, f_e, f_w, k_ne, k_nw, k_se, k_sw, a_n, a_s, a_e, a_w, j_ne, j_nw, j_se, j_sw, ra, rc, pk, pa, part, out, buf, rp, sem):
    n = vals * ROWS
    copy = pltpu.make_async_copy(part, buf.at[pl.ds(0, n)], sem)
    copy.start()
    (_, gcn, _), (_, gcs, _), (_, gc, _), (_, kc) = read_ghosts(vp, mp, f_n, f_s, f_e, f_w, (k_ne, k_nw, k_se, k_sw))

    def piece(ref, k):
        return tall(ref[mp * k : mp * (k + 1), :], vp)

    gv, _, gp = ghost_pack(piece(a_w, 0), piece(a_e, 0))
    kv = corner_pack([m[...] for m in (j_ne, j_nw, j_se, j_sw)], 0, vp)
    ghosts = (piece(a_n, 0), gcn, piece(a_n, 1)), (piece(a_s, 0), gcs, piece(a_s, 1)), (gv, gc, gp), (kv, kc)
    v0, v31, p0, p31 = parts_of(ra, vp)
    pv, pp = parts_of(pa, vp)
    r0, r1, r30, r31, fix = rim_correction((v0, v31, p0, p31, pv, pp), parts_of(rc, vp) + [pk[vp : 2 * vp, :]], ghosts)
    rp[...] = fix
    copy.wait()
    lane = lax.broadcasted_iota(jnp.int32, (vp, LANES), 1)
    outer = (lane < 2) | (lane >= LANES - 2)
    for i in range(ROWS):
        x = grid_row(buf, i, vp) + jnp.where(outer, roll(rp[...], -(4 * i + 2)), 0.0)
        row = {0: r0, 1: r1, ROWS - 2: r30, ROWS - 1: r31}.get(i)
        buf[pl.ds(i, vp, stride=ROWS), :] = x if row is None else x + row
    copy = pltpu.make_async_copy(buf.at[pl.ds(0, n)], out, sem)
    copy.start()
    copy.wait()


def neighbour(x, dlon, dlat):
    nlon, nlat = lax.axis_size("lon"), lax.axis_size("lat")
    pairs = [
        (a * nlat + b, (a + dlon) % nlon * nlat + b + dlat)
        for a in range(nlon)
        for b in range(nlat)
        if 0 <= b + dlat < nlat
    ]
    return lax.ppermute(x, ("lon", "lat"), pairs)


def exchange(m_n, m_s, m_e, m_w, k_ne, k_nw, k_se, k_sw):
    f_s = neighbour(m_n, 0, -1)
    f_n = neighbour(m_s, 0, 1)
    f_w = neighbour(m_e, 1, 0)
    f_e = neighbour(m_w, -1, 0)
    g_sw = neighbour(k_ne, 1, -1)
    g_se = neighbour(k_nw, -1, -1)
    g_nw = neighbour(k_se, 1, 1)
    g_ne = neighbour(k_sw, -1, 1)
    return f_n, f_s, f_e, f_w, g_ne, g_nw, g_se, g_sw


def across(x):
    return lax.all_to_all(x, ("lon", "lat"), split_axis=0, concat_axis=0, tiled=True)


def on_device(state, diffusivity, sea_mask, send_cols, obs_slots, obs_weights, obs_precision):
    vals, taps, obs = state.shape[0], obs_slots.shape[0], obs_slots.shape[1]
    owners = send_cols.shape[1] // CAP
    vp, mp = up(vals, ROWS), up(vals, 8)
    tiles = up(owners, 7 * GROUPS) // GROUPS
    slots = tiles * LANES
    cell_count = ROWS * LANES
    flat = [x.reshape(-1, LANES) for x in (state, diffusivity, sea_mask)]
    cells = jnp.pad(send_cols, ((0, 0), (0, tiles * GROUPS * CAP - owners * CAP)), constant_values=cell_count)
    cells = jnp.pad(cells.reshape(tiles, GROUPS * CAP), ((0, 0), (0, LANES - GROUPS * CAP)), constant_values=cell_count)
    cells = cells.reshape(1, slots)

    fields = [pltpu.VMEM((vp * ROWS, LANES), d) for d in (F32, F32, jnp.int32)]
    dma4 = pltpu.SemaphoreType.DMA((4,))
    line = (vp, LANES)
    corner = [((8, 256), F32)] * 4

    def messages(n):
        return [((n * mp, LANES), F32)] * 2 + [((mp, LANES), F32)] * 2 + corner

    *sent, rv, rc, pk = call(
        functools.partial(prepare_kernel, vals, vp, mp),
        messages(3) + [((4 * vp, LANES), F32)] * 2 + [((3 * vp, LANES), F32)],
        *flat,
        in_specs=[HBM] * 3,
        scratch=fields + [dma4],
    )
    ghosts = exchange(*sent)
    w_hi, w_lo = pl.pallas_call(
        weights_kernel,
        grid=(obs // OBS_BLOCK,),
        out_shape=[jax.ShapeDtypeStruct((slots, obs), BF16)] * 2,
        in_specs=[pl.BlockSpec((taps, OBS_BLOCK), lambda j: (0, j))] * 2,
        out_specs=[pl.BlockSpec((slots, OBS_BLOCK), lambda j: (0, j))] * 2,
        compiler_params=pltpu.CompilerParams(vmem_limit_bytes=48 * MIB),
        cost_estimate=pl.CostEstimate(flops=10 * slots * obs, bytes_accessed=4 * slots * obs, transcendentals=0),
    )(obs_slots, obs_weights)
    (inner,) = call(
        functools.partial(inner_kernel, vals, vp),
        [((vp, slots), F32)],
        *flat,
        cells,
        in_specs=[HBM] * 3 + [VMEM],
        scratch=fields + [pltpu.VMEM((vp, cell_count), F32), pltpu.VMEM((cell_count, 7 * LANES), BF16), dma4],
        flops=4 * vp * cell_count * slots,
        nbytes=8 * MIB,
    )
    (payload,) = call(
        functools.partial(send_kernel, owners, vp, mp),
        [((owners * ROWS, LANES), F32)],
        *ghosts, rv, rc, pk, inner, cells,
    )
    received = across(payload)
    equivalents, payload = pl.pallas_call(
        functools.partial(owner_kernel, vals, vp, owners),
        grid=(obs // OBS_BLOCK,),
        out_shape=[jax.ShapeDtypeStruct((vals, obs), F32), jax.ShapeDtypeStruct((owners * ROWS, LANES), F32)],
        in_specs=[
            pl.BlockSpec((owners * ROWS, LANES), lambda j: (0, 0)),
            pl.BlockSpec((slots, OBS_BLOCK), lambda j: (0, j)),
            pl.BlockSpec((slots, OBS_BLOCK), lambda j: (0, j)),
            pl.BlockSpec((vals, OBS_BLOCK), lambda j: (0, j)),
        ],
        out_specs=[
            pl.BlockSpec((vals, OBS_BLOCK), lambda j: (0, j)),
            pl.BlockSpec((owners * ROWS, LANES), lambda j: (0, 0)),
        ],
        scratch_shapes=[pltpu.VMEM((2 * vp, slots), BF16), pltpu.VMEM((vp, OBS_BLOCK), F32), pltpu.VMEM((vp, slots), F32)],
        compiler_params=pltpu.CompilerParams(vmem_limit_bytes=48 * MIB),
    )(received, w_hi, w_lo, obs_precision)
    incoming = across(payload)
    *sent, inc, ra, pa = call(
        functools.partial(back_kernel, owners, vp, mp),
        messages(2) + [((2 * vp, slots), BF16), ((4 * vp, LANES), F32), ((2 * vp, LANES), F32)],
        incoming, cells, rc, pk,
    )
    adjoint_ghosts = exchange(*sent)
    (part,) = call(
        functools.partial(adjoint_kernel, vals, vp),
        [((vals * ROWS, LANES), F32)],
        *flat, inc, cells,
        in_specs=[HBM] * 3 + [VMEM] * 2,
        scratch=fields + [pltpu.VMEM((ROWS * vp, LANES), F32), dma4, pltpu.SemaphoreType.DMA(())],
        out_specs=[HBM],
        flops=4 * vp * cell_count * slots,
        nbytes=10 * MIB,
    )
    (product,) = call(
        functools.partial(final_kernel, vals, vp, mp),
        [((vals * ROWS, LANES), F32)],
        *ghosts, *adjoint_ghosts, ra, rc, pk, pa, part,
        in_specs=[VMEM] * 20 + [HBM],
        scratch=[pltpu.VMEM((vp * ROWS, LANES), F32), pltpu.VMEM(line, F32), pltpu.SemaphoreType.DMA(())],
        out_specs=[HBM],
    )
    return product.reshape(state.shape), equivalents


def solution(mesh):
    placed = (
        P(None, "lat", "lon"),
        P(None, "lat", "lon"),
        P(None, "lat", "lon"),
        P(("lon", "lat"), None),
        P(None, ("lon", "lat")),
        P(None, ("lon", "lat")),
        P(None, ("lon", "lat")),
    )
    return jax.shard_map(
        on_device,
        mesh=mesh,
        in_specs=placed,
        out_specs=(P(None, "lat", "lon"), P(None, ("lon", "lat"))),
        check_vma=False,
    )
```

```python
import functools

import jax
import jax.numpy as jnp
from jax import lax
from jax.experimental import pallas as pl
from jax.experimental.pallas import tpu as pltpu
from jax.sharding import PartitionSpec as P

CAP = 24
LANES = 128
GROUPS = 5
ROWS = 32
OBS_BLOCK = 256
F32, BF16 = jnp.float32, jnp.bfloat16
MIB = 1 << 20


def up(n, k):
    return -(-n // k) * k


def roll(x, k):
    k %= LANES
    return x if k == 0 else pltpu.roll(x, k, axis=1)


def lane_of(x):
    return lax.broadcasted_iota(jnp.int32, x.shape, 1)


def tall(x, rows):
    return jnp.concatenate([x, jnp.zeros((rows - x.shape[0], x.shape[1]), x.dtype)], axis=0)


def halves(x):
    hi = x.astype(BF16)
    return hi, (x - hi.astype(F32)).astype(BF16)


def dot(a, b):
    return lax.dot_general(a, b, (((1,), (0,)), ((), ())), preferred_element_type=F32)


def dot_nt(a, b):
    return lax.dot_general(a, b, (((1,), (1,)), ((), ())), preferred_element_type=F32)


def stacked(x):
    return jnp.concatenate(halves(x), axis=0)


def folded(x):
    n = x.shape[0] // 2
    return x[:n] + x[n:]


def row_edges(c):
    east = jnp.where(lane_of(c) == LANES - 1, 0.0, jnp.minimum(c, roll(c, -1)))
    return east, roll(east, 1)


def pack_edges(cp):
    lane = lane_of(cp)
    kind = lane & 3
    inner = jnp.where(kind == 1, roll(cp, 1), roll(cp, -1))
    inner = jnp.where((kind == 1) | (kind == 2), jnp.minimum(cp, inner), 0.0)
    south = jnp.where(lane >= LANES - 4, 0.0, jnp.minimum(cp, roll(cp, -4)))
    return kind, inner, south, roll(south, 4)


def rim_rows(v0, v1, v30, v31, c0, c1, c30, c31):
    out = []
    for v, w, c, d in ((v0, v1, c0, c1), (v31, v30, c31, c30)):
        east, west = row_edges(c)
        out.append(v + east * (roll(v, -1) - v) + west * (roll(v, 1) - v) + jnp.minimum(c, d) * (w - v))
    return out


def rim_pack(vp, cp):
    kind, inner, south, north = pack_edges(cp)
    beside = jnp.where(kind == 1, roll(vp, 1), roll(vp, -1))
    return vp + inner * (beside - vp) + south * (roll(vp, -4) - vp) + north * (roll(vp, 4) - vp)


def pack_messages(vp, cp, pp, north, south):
    lane = lane_of(vp)
    kind = lane & 3
    east = jnp.where(kind == 0, roll(vp, -1), jnp.where(kind == 1, cp, roll(pp, 1)))
    west = jnp.where(kind == 0, roll(vp, -2), jnp.where(kind == 1, roll(cp, -1), pp))
    for k, x in zip((3, 7, 11, 15), (*north, *south)):
        east = jnp.where(lane == k, roll(x, k + 1), east)
        west = jnp.where(lane == k, roll(x, k), west)
    return east, west


def ghost_pack(from_w, from_e):
    one = (lane_of(from_w) & 3) == 1
    v = jnp.where(one, roll(from_e, 1), roll(from_w, 2))
    c = jnp.where(one, from_e, roll(from_w, 1))
    p = jnp.where(one, roll(from_e, -1), from_w)
    return v, c, p


def corner_pack(from_w, from_e):
    lane = lane_of(from_w)
    out = []
    for n, s in ((3, 11), (7, 15)):
        x = jnp.zeros_like(from_w)
        for at, src, k in ((1, from_e, n), (2, from_w, n), (LANES - 3, from_e, s), (LANES - 2, from_w, s)):
            x = jnp.where(lane == at, roll(src, at - k), x)
        out.append(x)
    return out


def rim_correction(own, coef, ghosts):
    v0, v31, p0, p31, vp, pp = own
    c0, c1, c30, c31, cp = coef
    (gvn, gcn, gpn), (gvs, gcs, gps), (gv, gc, gp), (kv, kc) = ghosts
    lane = lane_of(v0)
    ends = (lane == 0) | (lane == LANES - 1)
    kind, inner, south, north = pack_edges(cp)
    mid = (kind == 1) | (kind == 2)
    mg = jnp.where(mid, jnp.minimum(cp, gc), 0.0)
    f = mg * (gv - vp)
    mn, ms = jnp.minimum(c0, gcn), jnp.minimum(c31, gcs)
    fn, fs = mn * (gvn - v0), ms * (gvs - v31)
    ghost = gp - f + jnp.where(mid, jnp.minimum(gc, kc), 0.0) * (kv - gv)
    ghost_n = gpn - fn + jnp.where(ends, jnp.minimum(gcn, roll(kc, -2)), 0.0) * (roll(kv, -2) - gvn)
    ghost_s = gps - fs + jnp.where(ends, jnp.minimum(gcs, roll(kc, 2)), 0.0) * (roll(kv, 2) - gvs)
    whole = pp + f + jnp.where((lane == 1) | (lane == 2), roll(fn, 2), 0.0)
    whole = whole + jnp.where((lane == LANES - 3) | (lane == LANES - 2), roll(fs, -2), 0.0)
    whole_n = p0 + fn + jnp.where(ends, roll(f, -2), 0.0)
    whole_s = p31 + fs + jnp.where(ends, roll(f, 2), 0.0)
    qf = inner * f
    rp = f - qf + south * (roll(f, -4) - f) + north * (roll(f, 4) - f) + mg * (ghost - whole)
    rp = jnp.where(mid, rp, jnp.where(kind == 0, roll(qf, -1), roll(qf, 1)))
    rows = []
    for c, d, m, g, w, x in ((c0, c1, mn, ghost_n, whole_n, fn), (c31, c30, ms, ghost_s, whole_s, fs)):
        east, west = row_edges(c)
        across = jnp.minimum(c, d)
        rows.append(x + east * (roll(x, -1) - x) + west * (roll(x, 1) - x) - across * x + m * (g - w))
        rows.append(across * x)
    return rows[0], rows[1], rows[3], rows[2], rp


def sweep(src, edges, emit):
    east, west, south = edges
    for i in range(ROWS):
        x = src[i]
        y = x + east[i] * (roll(x, -1) - x) + west[i] * (roll(x, 1) - x)
        if i < ROWS - 1:
            y = y + south[i] * (src[i + 1] - x)
        if i > 0:
            y = y + south[i - 1] * (src[i - 1] - x)
        emit(i, y)


def chosen(cells, ids):
    return jnp.where(ids == cells, 1.0, 0.0).astype(BF16)


def rim_ids(n):
    line = lax.broadcasted_iota(jnp.int32, (LANES, n), 0)
    rows = [line + i * LANES for i in (0, 1, ROWS - 2, ROWS - 1)]
    k = line & 3
    pack = (line >> 2) * LANES + jnp.where(k < 2, LANES - 2 + k, k - 2)
    return jnp.concatenate(rows + [pack], axis=0)


def pack_payload(x, out_ref, owners):
    lane = lax.broadcasted_iota(jnp.int32, (ROWS, LANES), 1)
    for o in range(owners):
        a, b = divmod(o, GROUPS)
        block = jnp.zeros((ROWS, LANES), F32)
        for g in range(GROUPS):
            piece = roll(x[ROWS * g : ROWS * (g + 1), LANES * a : LANES * (a + 1)], CAP * (g - b))
            block = jnp.where((lane >= CAP * g) & (lane < CAP * (g + 1)), piece, block)
        out_ref[ROWS * o : ROWS * (o + 1), :] = block


def unpack_payload(in_ref, owners, slots):
    lane = lax.broadcasted_iota(jnp.int32, (ROWS, LANES), 1)
    columns = []
    for a in range(slots // LANES):
        pieces = []
        for g in range(GROUPS):
            piece = jnp.zeros((ROWS, LANES), F32)
            for b in range(GROUPS):
                o = GROUPS * a + b
                if o < owners:
                    block = roll(in_ref[ROWS * o : ROWS * (o + 1), :], CAP * (b - g))
                    piece = jnp.where((lane >= CAP * b) & (lane < CAP * (b + 1)), block, piece)
            pieces.append(piece)
        columns.append(jnp.concatenate(pieces, axis=0))
    return jnp.concatenate(columns, axis=1)


def call(kernel, outs, *args, in_specs=None, scratch=(), vmem=48, flops=0, nbytes=0, **kw):
    any_spec = pl.BlockSpec(memory_space=pltpu.VMEM)
    return pl.pallas_call(
        kernel,
        out_shape=[jax.ShapeDtypeStruct(s, d) for s, d in outs],
        in_specs=in_specs or [any_spec] * len(args),
        scratch_shapes=list(scratch),
        compiler_params=pltpu.CompilerParams(vmem_limit_bytes=vmem * MIB),
        cost_estimate=pl.CostEstimate(flops=flops, bytes_accessed=nbytes, transcendentals=0),
        **kw,
    )(*args)


HBM = pl.BlockSpec(memory_space=pl.ANY)
VMEM = pl.BlockSpec(memory_space=pltpu.VMEM)


def run(copies):
    for c in copies:
        c.start()
    for c in copies:
        c.wait()


def even(axis):
    return lax.rem(lax.axis_index(axis), 2) == 0


def write_parts(ref, parts, rows):
    for k, x in enumerate(parts):
        ref[rows * k : rows * (k + 1), :] = x[:rows]


def parts_of(ref, rows, vp=None):
    out = [ref[rows * k : rows * (k + 1), :] for k in range(ref.shape[0] // rows)]
    return out if vp is None else [tall(x, vp) for x in out]


def write_pair(axis, first, second, up_parts, down_parts, rows):
    for ref, e, o in ((first, down_parts, up_parts), (second, up_parts, down_parts)):
        write_parts(ref, [jnp.where(even(axis), x, y) for x, y in zip(e, o)], rows)


def read_pair(axis, first, second, rows, vp):
    f, s = parts_of(first, rows, vp), parts_of(second, rows, vp)
    before = [jnp.where(even(axis), y, x) for x, y in zip(f, s)]
    after = [jnp.where(even(axis), x, y) for x, y in zip(f, s)]
    return before, after


def prepare_kernel(vals, vp, mp, state, diff, mask, field, coef, m_1, m_2, rv, rc, sv, sd, sm, dt, mt, sems):
    run([pltpu.make_async_copy(r, t, sems.at[k]) for k, (r, t) in enumerate(((state, sv), (diff, sd), (mask, sm)))])
    half = vals // 2
    copies = []
    for i in range(ROWS):
        copies.append(pltpu.make_async_copy(sv.at[:, i], field.at[i, pl.ds(0, vals)], sems.at[3 + 4 * i]))
        copies.append(pltpu.make_async_copy(sd.at[:, i], dt.at[i, pl.ds(0, vals)], sems.at[4 + 4 * i]))
        copies.append(pltpu.make_async_copy(sm.at[:, i], mt.at[i, pl.ds(0, half)], sems.at[5 + 4 * i]))
        copies.append(pltpu.make_async_copy(sm.at[:, i], mt.at[i, pl.ds(half, half)], sems.at[6 + 4 * i]))
    for c in copies:
        c.start()
    for ref in (field, dt, mt):
        ref[:, vals:, :] = jnp.zeros((ROWS, vp - vals, LANES), ref.dtype)
    for c in copies:
        c.wait()
    for i in range(ROWS):
        coef[i] = dt[i] * mt[i].astype(F32)
    ends = (0, 1, ROWS - 2, ROWS - 1)
    v0, v1, v30, v31 = (field[i] for i in ends)
    c0, c1, c30, c31 = (coef[i] for i in ends)
    p0, p31 = rim_rows(v0, v1, v30, v31, c0, c1, c30, c31)
    write_pair("lat", m_1, m_2, (v0, c0, p0), (v31, c31, p31), mp)
    write_parts(rv, (v0, v31, p0, p31), vp)
    write_parts(rc, (c0, c1, c30, c31), vp)


def sweeps_kernel(vp, field, coef, out, east, west, south, pk, mid):
    lane = lax.broadcasted_iota(jnp.int32, (vp, LANES), 1)
    pv = jnp.zeros((vp, LANES), F32)
    pc = jnp.zeros((vp, LANES), F32)
    for i in range(ROWS):
        c = coef[i]
        e = jnp.where(lane == LANES - 1, 0.0, jnp.minimum(c, roll(c, -1)))
        east[i] = e
        west[i] = roll(e, 1)
        south[i] = jnp.minimum(c, coef[i + 1]) if i < ROWS - 1 else jnp.zeros_like(c)
        here = (lane >> 2) == i
        pv = jnp.where(here, roll(field[i], 4 * i + 2), pv)
        pc = jnp.where(here, roll(c, 4 * i + 2), pc)
    write_parts(pk, (pv, pc, rim_pack(pv, pc)), vp)
    edges = (east, west, south)

    def keep(i, y):
        mid[i] = y

    def split(i, y):
        out[:, LANES * i : LANES * (i + 1)] = stacked(y)

    sweep(field, edges, keep)
    sweep(mid, edges, split)


def lon_kernel(vp, mp, g_1, g_2, coefs, pk, m_1, m_2):
    north, south = read_pair("lat", g_1, g_2, mp, vp)
    if coefs:
        pv, pc, pp = parts_of(pk, vp)
        north, south = north[:2], south[:2]
    else:
        pv, pp = parts_of(pk, vp)
        pc = pv
        north, south = (north[0], north[0]), (south[0], south[0])
    east, west = pack_messages(pv, pc, pp, north, south)
    write_pair("lon", m_1, m_2, (west,), (east,), mp)


def select_kernel(smooth, cells, out, hot):
    chunk = hot.shape[1]
    wide = 4 * LANES
    for base in range(0, cells.shape[1], chunk):
        for k in range(0, ROWS * LANES, wide):
            ids = lax.broadcasted_iota(jnp.int32, (wide, chunk), 0) + k
            hot[k : k + wide, :] = chosen(cells[:, base : base + chunk], ids)
        total = jnp.zeros((smooth.shape[0], chunk), F32)
        for k in range(0, ROWS * LANES, wide):
            total = total + dot(smooth[:, k : k + wide], hot[k : k + wide, :])
        out[:, base : base + chunk] = folded(total)


def weights_kernel(slots, weights, hi, lo):
    s = slots[...]
    place = s + 8 * jnp.floor((s.astype(F32) + 0.5) * (1.0 / (CAP * GROUPS))).astype(jnp.int32)
    row = lax.broadcasted_iota(jnp.int32, hi.shape, 0)
    total = jnp.zeros(hi.shape, F32)
    for k in range(slots.shape[0]):
        total = total + jnp.where(row == place[k : k + 1], weights[k : k + 1, :], 0.0)
    hi[...], lo[...] = halves(total)


def read_ghosts(vp, mp, lat, lon):
    north, south = read_pair("lat", *lat, mp, vp)
    west, east = read_pair("lon", *lon, mp, vp)
    return north, south, ghost_pack(west[0], east[0]), corner_pack(west[0], east[0])


def send_kernel(owners, vp, mp, g_1, g_2, h_1, h_2, rv, rc, pk, inner, cells, out):
    ghosts = read_ghosts(vp, mp, (g_1, g_2), (h_1, h_2))
    v0, v31, p0, p31 = parts_of(rv, vp)
    pv, pc, pp = parts_of(pk, vp)
    fix = rim_correction((v0, v31, p0, p31, pv, pp), parts_of(rc, vp) + [pc], ghosts)
    slots = cells.shape[1]
    total = folded(dot(stacked(jnp.concatenate(fix, axis=1)), chosen(cells[...], rim_ids(slots))))
    pack_payload(inner[...] + total, out, owners)


def owner_kernel(vals, vp, owners, got, w_hi, w_lo, prec, equiv, back, r2, w2, acc):
    step = pl.program_id(0)

    @pl.when(step == 0)
    def _():
        r2[...] = stacked(unpack_payload(got, owners, acc.shape[1]))
        w2[...] = jnp.zeros(w2.shape, F32)
        acc[...] = jnp.zeros(acc.shape, F32)

    hi, lo = w_hi[...], w_lo[...]
    e = folded(dot(r2[...], hi)) + dot(r2[:vp, :], lo)
    equiv[...] = e[:vals]
    w2[:vals, :] = prec[...] * e[:vals]
    w = stacked(w2[...])
    acc[...] += folded(dot_nt(w, hi)) + dot_nt(w[:vp], lo)

    @pl.when(step == pl.num_programs(0) - 1)
    def _():
        pack_payload(acc[...], back, owners)


def back_kernel(owners, vp, mp, got, cells, rc, pk, m_1, m_2, inc, ra, pa):
    slots = cells.shape[1]
    x = stacked(unpack_payload(got, owners, slots))
    inc[...] = x
    rims = folded(dot_nt(x, chosen(cells[...], rim_ids(slots))))
    v0, v1, v30, v31, pv = (rims[:, LANES * k : LANES * (k + 1)] for k in range(5))
    p0, p31 = rim_rows(v0, v1, v30, v31, *parts_of(rc, vp))
    write_pair("lat", m_1, m_2, (v0, p0), (v31, p31), mp)
    write_parts(ra, (v0, v31, p0, p31), vp)
    write_parts(pa, (pv, rim_pack(pv, pk[vp : 2 * vp, :])), vp)


def adjoint_kernel(vp, inc, cells, east, west, south, out, adj):
    wide = 2 * LANES
    slots = cells.shape[1]
    for k in range(ROWS // 2):
        ids = lax.broadcasted_iota(jnp.int32, (wide, slots), 0) + k * wide
        x = folded(dot_nt(inc[...], chosen(cells[...], ids)))
        for j in range(2):
            adj[2 * k + j] = x[:, LANES * j : LANES * (j + 1)]

    def keep(i, y):
        out[i] = y

    sweep(adj, (east, west, south), keep)


def second_kernel(mid, east, west, south, field, out):
    def add(i, y):
        out[i] = y + field[i]

    sweep(mid, (east, west, south), add)


def final_kernel(vals, vp, mp, g_1, g_2, h_1, h_2, a_1, a_2, b_1, b_2, ra, rc, pk, pa, part, out, buf, sems):
    gn, gs, (_, gc, _), (_, kc) = read_ghosts(vp, mp, (g_1, g_2), (h_1, h_2))
    an, az, (gv, _, gp), (kv, _) = read_ghosts(vp, mp, (a_1, a_2), (b_1, b_2))
    ghosts = (an[0], gn[1], an[1]), (az[0], gs[1], az[1]), (gv, gc, gp), (kv, kc)
    v0, v31, p0, p31 = parts_of(ra, vp)
    pv, pp = parts_of(pa, vp)
    r0, r1, r30, r31, fix = rim_correction((v0, v31, p0, p31, pv, pp), parts_of(rc, vp) + [pk[vp : 2 * vp, :]], ghosts)
    lane = lax.broadcasted_iota(jnp.int32, (vp, LANES), 1)
    outer = (lane < 2) | (lane >= LANES - 2)
    copies = []
    for i in range(ROWS):
        x = part[i] + jnp.where(outer, roll(fix, -(4 * i + 2)), 0.0)
        row = {0: r0, 1: r1, ROWS - 2: r30, ROWS - 1: r31}.get(i)
        buf[i] = x if row is None else x + row
        copies.append(pltpu.make_async_copy(buf.at[i, pl.ds(0, vals)], out.at[:, i], sems.at[i]))
        copies[-1].start()
    for c in copies:
        c.wait()


def swap(axis, x, first):
    n = lax.axis_size(axis)
    pairs = []
    for i in range(n):
        j = i + 1 if (i % 2 == 0) == first else i - 1
        if axis == "lon":
            j %= n
        if 0 <= j < n:
            pairs.append((i, j))
    return lax.ppermute(x, axis, pairs)


def exchange(axis, m_1, m_2):
    g_2 = swap(axis, m_2, False)
    g_1 = swap(axis, m_1, True)
    return g_1, g_2


def across(x):
    return lax.all_to_all(x, ("lon", "lat"), split_axis=0, concat_axis=0, tiled=True)


def on_device(state, diffusivity, sea_mask, send_cols, obs_slots, obs_weights, obs_precision):
    vals, taps, obs = state.shape[0], obs_slots.shape[0], obs_slots.shape[1]
    owners = send_cols.shape[1] // CAP
    vp, mp = up(vals, ROWS), up(vals, 8)
    tiles = up(owners, 7 * GROUPS) // GROUPS
    slots = tiles * LANES
    cell_count = ROWS * LANES
    cells = jnp.pad(send_cols, ((0, 0), (0, tiles * GROUPS * CAP - owners * CAP)), constant_values=cell_count)
    cells = jnp.pad(cells.reshape(tiles, GROUPS * CAP), ((0, 0), (0, LANES - GROUPS * CAP)), constant_values=cell_count)
    cells = cells.reshape(1, slots)
    lines = lambda n, rows, dtype=F32: ((n * rows, LANES), dtype)
    field = ((ROWS, vp, LANES), F32)

    whole, coef, *lat_out, rv, rc = call(
        functools.partial(prepare_kernel, vals, vp, mp),
        [field, field, lines(3, mp), lines(3, mp), lines(4, vp), lines(4, vp)],
        state, diffusivity, sea_mask,
        in_specs=[HBM] * 3,
        scratch=[pltpu.VMEM(x.shape, x.dtype) for x in (state, diffusivity, sea_mask)]
        + [pltpu.VMEM((ROWS, vp, LANES), F32), pltpu.VMEM((ROWS, vp, LANES), jnp.int32), pltpu.SemaphoreType.DMA((3 + 4 * ROWS,))],
        vmem=24,
    )
    lat_in = exchange("lat", *lat_out)
    w_hi, w_lo = pl.pallas_call(
        weights_kernel,
        grid=(obs // OBS_BLOCK,),
        out_shape=[jax.ShapeDtypeStruct((slots, obs), BF16)] * 2,
        in_specs=[pl.BlockSpec((taps, OBS_BLOCK), lambda j: (0, j))] * 2,
        out_specs=[pl.BlockSpec((slots, OBS_BLOCK), lambda j: (0, j))] * 2,
        compiler_params=pltpu.CompilerParams(vmem_limit_bytes=40 * MIB),
        cost_estimate=pl.CostEstimate(flops=10 * slots * obs, bytes_accessed=4 * slots * obs, transcendentals=0),
    )(obs_slots, obs_weights)
    split, east, west, south, pk = call(
        functools.partial(sweeps_kernel, vp),
        [((2 * vp, cell_count), BF16), field, field, field, lines(3, vp)],
        whole, coef,
        scratch=[pltpu.VMEM((ROWS, vp, LANES), F32)],
        vmem=24,
        flops=10 * vp * cell_count,
        nbytes=24 * MIB,
    )
    lon_out = call(
        lambda g_1, g_2, *refs: lon_kernel(vp, mp, g_1, g_2, True, *refs),
        [lines(1, mp)] * 2, *lat_in, pk,
        vmem=8,
    )
    lon_in = exchange("lon", *lon_out)
    (inner,) = call(
        select_kernel,
        [((vp, slots), F32)],
        split, cells,
        scratch=[pltpu.VMEM((cell_count, 7 * LANES), BF16)],
        vmem=24,
        flops=4 * vp * cell_count * slots,
        nbytes=8 * MIB,
    )
    (payload,) = call(
        functools.partial(send_kernel, owners, vp, mp),
        [((owners * ROWS, LANES), F32)],
        *lat_in, *lon_in, rv, rc, pk, inner, cells,
        vmem=24,
    )
    payload, w_hi, w_lo = lax.optimization_barrier((payload, w_hi, w_lo))
    received = across(payload)
    wide = min(obs, 1024 if slots <= 1024 else 512)
    equivalents, payload = pl.pallas_call(
        functools.partial(owner_kernel, vals, vp, owners),
        grid=(obs // wide,),
        out_shape=[jax.ShapeDtypeStruct((vals, obs), F32), jax.ShapeDtypeStruct((owners * ROWS, LANES), F32)],
        in_specs=[
            pl.BlockSpec((owners * ROWS, LANES), lambda j: (0, 0)),
            pl.BlockSpec((slots, wide), lambda j: (0, j)),
            pl.BlockSpec((slots, wide), lambda j: (0, j)),
            pl.BlockSpec((vals, wide), lambda j: (0, j)),
        ],
        out_specs=[
            pl.BlockSpec((vals, wide), lambda j: (0, j)),
            pl.BlockSpec((owners * ROWS, LANES), lambda j: (0, 0)),
        ],
        scratch_shapes=[pltpu.VMEM((2 * vp, slots), BF16), pltpu.VMEM((vp, wide), F32), pltpu.VMEM((vp, slots), F32)],
        compiler_params=pltpu.CompilerParams(vmem_limit_bytes=48 * MIB),
    )(received, w_hi, w_lo, obs_precision)
    incoming = across(payload)
    *lat_out, inc, ra, pa = call(
        functools.partial(back_kernel, owners, vp, mp),
        [lines(2, mp)] * 2 + [((2 * vp, slots), BF16), lines(4, vp), lines(2, vp)],
        incoming, cells, rc, pk,
        vmem=24,
    )
    lat_back = exchange("lat", *lat_out)
    (mid,) = call(
        functools.partial(adjoint_kernel, vp),
        [field],
        inc, cells, east, west, south,
        scratch=[pltpu.VMEM((ROWS, vp, LANES), F32)],
        vmem=24,
        flops=4 * vp * cell_count * slots,
        nbytes=10 * MIB,
    )
    lon_out = call(
        lambda g_1, g_2, *refs: lon_kernel(vp, mp, g_1, g_2, False, *refs),
        [lines(1, mp)] * 2, *lat_back, pa,
        vmem=8,
    )
    lon_back = exchange("lon", *lon_out)
    (part,) = call(second_kernel, [field], mid, east, west, south, whole, vmem=24, flops=10 * vp * cell_count, nbytes=16 * MIB)
    (product,) = call(
        functools.partial(final_kernel, vals, vp, mp),
        [(state.shape, F32)],
        *lat_in, *lon_in, *lat_back, *lon_back, ra, rc, pk, pa, part,
        scratch=[pltpu.VMEM((ROWS, vp, LANES), F32), pltpu.SemaphoreType.DMA((ROWS,))],
        out_specs=[HBM],
        vmem=16,
    )
    return product, equivalents


def solution(mesh):
    placed = (
        P(None, "lat", "lon"),
        P(None, "lat", "lon"),
        P(None, "lat", "lon"),
        P(("lon", "lat"), None),
        P(None, ("lon", "lat")),
        P(None, ("lon", "lat")),
        P(None, ("lon", "lat")),
    )
    return jax.shard_map(
        on_device,
        mesh=mesh,
        in_specs=placed,
        out_specs=(P(None, "lat", "lon"), P(None, ("lon", "lat"))),
        check_vma=False,
    )
```

```python
import functools

import jax
import jax.numpy as jnp
from jax import lax
from jax.experimental import pallas as pl
from jax.experimental.pallas import tpu as pltpu
from jax.sharding import PartitionSpec as P

CAP = 24
LANES = 128
GROUPS = 5
ROWS = 32
OBS_BLOCK = 256
F32, BF16 = jnp.float32, jnp.bfloat16
MIB = 1 << 20


def up(n, k):
    return -(-n // k) * k


def roll(x, k):
    k %= LANES
    return x if k == 0 else pltpu.roll(x, k, axis=1)


def lane_of(x):
    return lax.broadcasted_iota(jnp.int32, x.shape, 1)


def tall(x, rows):
    return jnp.concatenate([x, jnp.zeros((rows - x.shape[0], x.shape[1]), x.dtype)], axis=0)


def halves(x):
    hi = x.astype(BF16)
    return hi, (x - hi.astype(F32)).astype(BF16)


def dot(a, b):
    return lax.dot_general(a, b, (((1,), (0,)), ((), ())), preferred_element_type=F32)


def dot_nt(a, b):
    return lax.dot_general(a, b, (((1,), (1,)), ((), ())), preferred_element_type=F32)


def stacked(x):
    return jnp.concatenate(halves(x), axis=0)


def folded(x):
    n = x.shape[0] // 2
    return x[:n] + x[n:]


def row_edges(c):
    east = jnp.where(lane_of(c) == LANES - 1, 0.0, jnp.minimum(c, roll(c, -1)))
    return east, roll(east, 1)


def pack_edges(cp):
    lane = lane_of(cp)
    kind = lane & 3
    inner = jnp.where(kind == 1, roll(cp, 1), roll(cp, -1))
    inner = jnp.where((kind == 1) | (kind == 2), jnp.minimum(cp, inner), 0.0)
    south = jnp.where(lane >= LANES - 4, 0.0, jnp.minimum(cp, roll(cp, -4)))
    return kind, inner, south, roll(south, 4)


def rim_rows(v0, v1, v30, v31, c0, c1, c30, c31):
    out = []
    for v, w, c, d in ((v0, v1, c0, c1), (v31, v30, c31, c30)):
        east, west = row_edges(c)
        out.append(v + east * (roll(v, -1) - v) + west * (roll(v, 1) - v) + jnp.minimum(c, d) * (w - v))
    return out


def rim_pack(vp, cp):
    kind, inner, south, north = pack_edges(cp)
    beside = jnp.where(kind == 1, roll(vp, 1), roll(vp, -1))
    return vp + inner * (beside - vp) + south * (roll(vp, -4) - vp) + north * (roll(vp, 4) - vp)


def pack_messages(vp, cp, pp, north, south):
    lane = lane_of(vp)
    kind = lane & 3
    east = jnp.where(kind == 0, roll(vp, -1), jnp.where(kind == 1, cp, roll(pp, 1)))
    west = jnp.where(kind == 0, roll(vp, -2), jnp.where(kind == 1, roll(cp, -1), pp))
    for k, x in zip((3, 7, 11, 15), (*north, *south)):
        east = jnp.where(lane == k, roll(x, k + 1), east)
        west = jnp.where(lane == k, roll(x, k), west)
    return east, west


def ghost_pack(from_w, from_e):
    one = (lane_of(from_w) & 3) == 1
    v = jnp.where(one, roll(from_e, 1), roll(from_w, 2))
    c = jnp.where(one, from_e, roll(from_w, 1))
    p = jnp.where(one, roll(from_e, -1), from_w)
    return v, c, p


def corner_pack(from_w, from_e):
    lane = lane_of(from_w)
    out = []
    for n, s in ((3, 11), (7, 15)):
        x = jnp.zeros_like(from_w)
        for at, src, k in ((1, from_e, n), (2, from_w, n), (LANES - 3, from_e, s), (LANES - 2, from_w, s)):
            x = jnp.where(lane == at, roll(src, at - k), x)
        out.append(x)
    return out


def rim_correction(own, coef, ghosts):
    v0, v31, p0, p31, vp, pp = own
    c0, c1, c30, c31, cp = coef
    (gvn, gcn, gpn), (gvs, gcs, gps), (gv, gc, gp), (kv, kc) = ghosts
    lane = lane_of(v0)
    ends = (lane == 0) | (lane == LANES - 1)
    kind, inner, south, north = pack_edges(cp)
    mid = (kind == 1) | (kind == 2)
    mg = jnp.where(mid, jnp.minimum(cp, gc), 0.0)
    f = mg * (gv - vp)
    mn, ms = jnp.minimum(c0, gcn), jnp.minimum(c31, gcs)
    fn, fs = mn * (gvn - v0), ms * (gvs - v31)
    ghost = gp - f + jnp.where(mid, jnp.minimum(gc, kc), 0.0) * (kv - gv)
    ghost_n = gpn - fn + jnp.where(ends, jnp.minimum(gcn, roll(kc, -2)), 0.0) * (roll(kv, -2) - gvn)
    ghost_s = gps - fs + jnp.where(ends, jnp.minimum(gcs, roll(kc, 2)), 0.0) * (roll(kv, 2) - gvs)
    whole = pp + f + jnp.where((lane == 1) | (lane == 2), roll(fn, 2), 0.0)
    whole = whole + jnp.where((lane == LANES - 3) | (lane == LANES - 2), roll(fs, -2), 0.0)
    whole_n = p0 + fn + jnp.where(ends, roll(f, -2), 0.0)
    whole_s = p31 + fs + jnp.where(ends, roll(f, 2), 0.0)
    qf = inner * f
    rp = f - qf + south * (roll(f, -4) - f) + north * (roll(f, 4) - f) + mg * (ghost - whole)
    rp = jnp.where(mid, rp, jnp.where(kind == 0, roll(qf, -1), roll(qf, 1)))
    rows = []
    for c, d, m, g, w, x in ((c0, c1, mn, ghost_n, whole_n, fn), (c31, c30, ms, ghost_s, whole_s, fs)):
        east, west = row_edges(c)
        across = jnp.minimum(c, d)
        rows.append(x + east * (roll(x, -1) - x) + west * (roll(x, 1) - x) - across * x + m * (g - w))
        rows.append(across * x)
    return rows[0], rows[1], rows[3], rows[2], rp


def sweep(src, edges, emit):
    east, west, south = edges
    for i in range(ROWS):
        x = src[i]
        y = x + east[i] * (roll(x, -1) - x) + west[i] * (roll(x, 1) - x)
        if i < ROWS - 1:
            y = y + south[i] * (src[i + 1] - x)
        if i > 0:
            y = y + south[i - 1] * (src[i - 1] - x)
        emit(i, y)


def chosen(cells, ids):
    return jnp.where(ids == cells, 1.0, 0.0).astype(BF16)


def rim_ids(n):
    line = lax.broadcasted_iota(jnp.int32, (LANES, n), 0)
    rows = [line + i * LANES for i in (0, 1, ROWS - 2, ROWS - 1)]
    k = line & 3
    pack = (line >> 2) * LANES + jnp.where(k < 2, LANES - 2 + k, k - 2)
    return jnp.concatenate(rows + [pack], axis=0)


def pack_payload(x, out_ref, first, last):
    lane = lax.broadcasted_iota(jnp.int32, (ROWS, LANES), 1)
    for o in range(first, last):
        a, b = divmod(o - first, GROUPS)
        block = jnp.zeros((ROWS, LANES), F32)
        for g in range(GROUPS):
            piece = roll(x[ROWS * g : ROWS * (g + 1), LANES * a : LANES * (a + 1)], CAP * (g - b))
            block = jnp.where((lane >= CAP * g) & (lane < CAP * (g + 1)), piece, block)
        out_ref[ROWS * o : ROWS * (o + 1), :] = block


def unpack_payload(in_ref, owners, slots):
    lane = lax.broadcasted_iota(jnp.int32, (ROWS, LANES), 1)
    columns = []
    for a in range(slots // LANES):
        pieces = []
        for g in range(GROUPS):
            piece = jnp.zeros((ROWS, LANES), F32)
            for b in range(GROUPS):
                o = GROUPS * a + b
                if o < owners:
                    block = roll(in_ref[ROWS * o : ROWS * (o + 1), :], CAP * (b - g))
                    piece = jnp.where((lane >= CAP * b) & (lane < CAP * (b + 1)), block, piece)
            pieces.append(piece)
        columns.append(jnp.concatenate(pieces, axis=0))
    return jnp.concatenate(columns, axis=1)


def takes(us):
    return pl.CostEstimate(flops=MIB, bytes_accessed=int(us * 3.3e6), transcendentals=0)


def call(kernel, outs, *args, in_specs=None, scratch=(), vmem=48, us=1, **kw):
    any_spec = pl.BlockSpec(memory_space=pltpu.VMEM)
    return pl.pallas_call(
        kernel,
        out_shape=[jax.ShapeDtypeStruct(s, d) for s, d in outs],
        in_specs=in_specs or [any_spec] * len(args),
        scratch_shapes=list(scratch),
        compiler_params=pltpu.CompilerParams(vmem_limit_bytes=vmem * MIB),
        cost_estimate=takes(us),
        **kw,
    )(*args)


HBM = pl.BlockSpec(memory_space=pl.ANY)
VMEM = pl.BlockSpec(memory_space=pltpu.VMEM)


def even(axis):
    return lax.rem(lax.axis_index(axis), 2) == 0


def write_parts(ref, parts, rows):
    for k, x in enumerate(parts):
        ref[rows * k : rows * (k + 1), :] = x[:rows]


def parts_of(ref, rows, vp=None):
    out = [ref[rows * k : rows * (k + 1), :] for k in range(ref.shape[0] // rows)]
    return out if vp is None else [tall(x, vp) for x in out]


def write_pair(axis, first, second, up_parts, down_parts, rows):
    for ref, e, o in ((first, down_parts, up_parts), (second, up_parts, down_parts)):
        write_parts(ref, [jnp.where(even(axis), x, y) for x, y in zip(e, o)], rows)


def read_pair(axis, first, second, rows, vp):
    f, s = parts_of(first, rows, vp), parts_of(second, rows, vp)
    before = [jnp.where(even(axis), y, x) for x, y in zip(f, s)]
    after = [jnp.where(even(axis), x, y) for x, y in zip(f, s)]
    return before, after


def start_loads(vals, state, diff, mask, sv, sd, sm, sems, rows):
    half = vals // 2
    copies = []
    for k, i in enumerate(rows):
        for src, dst in (
            (state, sv.at[k, pl.ds(0, vals)]),
            (diff, sd.at[k, pl.ds(0, vals)]),
            (mask, sm.at[k, pl.ds(0, half)]),
            (mask, sm.at[k, pl.ds(half, half)]),
        ):
            copies.append(pltpu.make_async_copy(src.at[:, i], dst, sems.at[len(copies)]))
            copies[-1].start()
    for ref in (sv, sd, sm):
        ref[:, vals:, :] = jnp.zeros((ref.shape[0], ref.shape[1] - vals, LANES), ref.dtype)
    return copies


ENDS = (0, 1, ROWS - 2, ROWS - 1)


def rows_kernel(vals, vp, mp, state, diff, mask, m_1, m_2, rv, rc, done, sv, sd, sm, sems):
    done[...] = jnp.zeros(done.shape, F32)
    for c in start_loads(vals, state, diff, mask, sv, sd, sm, sems, ENDS):
        c.wait()
    v0, v1, v30, v31 = (sv[k] for k in range(4))
    c0, c1, c30, c31 = (sd[k] * sm[k].astype(F32) for k in range(4))
    p0, p31 = rim_rows(v0, v1, v30, v31, c0, c1, c30, c31)
    write_pair("lat", m_1, m_2, (v0, c0, p0), (v31, c31, p31), mp)
    write_parts(rv, (v0, v31, p0, p31), vp)
    write_parts(rc, (c0, c1, c30, c31), vp)


def by_grid_row(x, dst, first):
    n = x.shape[0]
    if n < 8:
        x = jnp.concatenate([x, jnp.zeros((8 - n, *x.shape[1:]), x.dtype)], axis=0)
    y = jnp.swapaxes(x, 0, 1)
    v, i = first
    for k in range(8):
        dst[i + k, v : v + 8, :] = y[k]


def sweeps_kernel(vals, vp, state, diff, mask, after, field, out, east, west, south, pk, coef, mid):
    half = vals // 2
    for v in range(0, vp, 8):
        if v >= vals:
            for ref in (field, coef):
                ref[:, v : v + 8, :] = jnp.zeros((ROWS, 8, LANES), F32)
            continue
        end = min(v + 8, vals)
        for i in range(0, ROWS, 8):
            rows = slice(i, i + 8)
            if end <= half:
                m = mask[v:end, rows, :]
            elif v >= half:
                m = mask[v - half : end - half, rows, :]
            else:
                m = jnp.concatenate([mask[v:half, rows, :], mask[: end - half, rows, :]], axis=0)
            by_grid_row(state[v:end, rows, :], field, (v, i))
            by_grid_row(diff[v:end, rows, :] * m.astype(F32), coef, (v, i))
    lane = lax.broadcasted_iota(jnp.int32, (vp, LANES), 1)
    pv = jnp.zeros((vp, LANES), F32)
    pc = jnp.zeros((vp, LANES), F32)
    c = coef[0]
    for i in range(ROWS):
        if i < ROWS - 1:
            cn = coef[i + 1]
            south[i] = jnp.minimum(c, cn)
        else:
            south[i] = jnp.zeros_like(c)
        e = jnp.where(lane == LANES - 1, 0.0, jnp.minimum(c, roll(c, -1)))
        east[i] = e
        west[i] = roll(e, 1)
        here = (lane >> 2) == i
        pv = jnp.where(here, roll(field[i], 4 * i + 2), pv)
        pc = jnp.where(here, roll(c, 4 * i + 2), pc)
        c = cn
    write_parts(pk, (pv, pc, rim_pack(pv, pc)), vp)
    edges = (east, west, south)

    def keep(i, y):
        mid[i] = y

    def split(i, y):
        out[:, LANES * i : LANES * (i + 1)] = stacked(y)

    sweep(field, edges, keep)
    sweep(mid, edges, split)


def lon_kernel(vp, mp, g_1, g_2, coefs, pk, m_1, m_2):
    north, south = read_pair("lat", g_1, g_2, mp, vp)
    if coefs:
        pv, pc, pp = parts_of(pk, vp)
        north, south = north[:2], south[:2]
    else:
        pv, pp = parts_of(pk, vp)
        pc = pv
        north, south = (north[0], north[0]), (south[0], south[0])
    east, west = pack_messages(pv, pc, pp, north, south)
    write_pair("lon", m_1, m_2, (west,), (east,), mp)


def select_kernel(smooth, cells, out, hot):
    chunk = hot.shape[1]
    wide = 4 * LANES
    for base in range(0, cells.shape[1], chunk):
        for k in range(0, ROWS * LANES, wide):
            ids = lax.broadcasted_iota(jnp.int32, (wide, chunk), 0) + k
            hot[k : k + wide, :] = chosen(cells[:, base : base + chunk], ids)
        total = jnp.zeros((smooth.shape[0], chunk), F32)
        for k in range(0, ROWS * LANES, wide):
            total = total + dot(smooth[:, k : k + wide], hot[k : k + wide, :])
        out[:, base : base + chunk] = folded(total)


def weights_kernel(slots, weights, hi, lo):
    s = slots[...]
    place = s + 8 * jnp.floor((s.astype(F32) + 0.5) * (1.0 / (CAP * GROUPS))).astype(jnp.int32)
    taps = range(slots.shape[0])
    at = [place[k : k + 1] for k in taps]
    w = [weights[k : k + 1, :] for k in taps]
    for a in taps:
        for b in range(a + 1, len(taps)):
            same = at[a] == at[b]
            w[a] = w[a] + jnp.where(same, w[b], 0.0)
            at[b] = jnp.where(same, -1, at[b])
    at = [x.astype(jnp.int16) for x in at]
    parts = [halves(x) for x in w]
    shape = (LANES, hi.shape[1])
    for r in range(0, hi.shape[0], LANES):
        row = (lax.broadcasted_iota(jnp.int32, shape, 0) + r).astype(jnp.int16)
        h = l = jnp.zeros(shape, BF16)
        for k in taps:
            here = row == at[k]
            h, l = jnp.where(here, parts[k][0], h), jnp.where(here, parts[k][1], l)
        hi[r : r + LANES, :] = h
        lo[r : r + LANES, :] = l


def read_ghosts(vp, mp, lat, lon):
    north, south = read_pair("lat", *lat, mp, vp)
    west, east = read_pair("lon", *lon, mp, vp)
    return north, south, ghost_pack(west[0], east[0]), corner_pack(west[0], east[0])


def send_kernel(owners, vp, mp, g_1, g_2, h_1, h_2, rv, rc, pk, inner, cells, out):
    ghosts = read_ghosts(vp, mp, (g_1, g_2), (h_1, h_2))
    v0, v31, p0, p31 = parts_of(rv, vp)
    pv, pc, pp = parts_of(pk, vp)
    fix = rim_correction((v0, v31, p0, p31, pv, pp), parts_of(rc, vp) + [pc], ghosts)
    slots = cells.shape[1]
    total = folded(dot(stacked(jnp.concatenate(fix, axis=1)), chosen(cells[...], rim_ids(slots))))
    pack_payload(inner[...] + total, out, 0, owners)


def owner_kernel(vals, vp, owners, got, w_hi, w_lo, prec, equiv, back, r2, w2):
    r2[...] = stacked(unpack_payload(got, owners, r2.shape[1]))
    wide = min(512, equiv.shape[1])
    for q in range(0, equiv.shape[1], wide):
        at = slice(q, q + wide)
        e = (folded(dot(r2[...], w_hi[:, at])) + dot(r2[:vp, :], w_lo[:, at]))[:vals]
        equiv[:, at] = e
        w2[:, at] = stacked(tall(prec[:, at] * e, vp))
    for o in range(0, r2.shape[1], 7 * LANES):
        at = slice(o, o + 7 * LANES)
        x = folded(dot_nt(w2[...], w_hi[at, :])) + dot_nt(w2[:vp, :], w_lo[at, :])
        n = 7 * GROUPS * (o // (7 * LANES))
        pack_payload(x, back, n, min(owners, n + 7 * GROUPS))


def back_kernel(owners, vp, mp, got, cells, rc, pk, m_1, m_2, inc, ra, pa):
    slots = cells.shape[1]
    x = stacked(unpack_payload(got, owners, slots))
    inc[...] = x
    rims = folded(dot_nt(x, chosen(cells[...], rim_ids(slots))))
    v0, v1, v30, v31, pv = (rims[:, LANES * k : LANES * (k + 1)] for k in range(5))
    p0, p31 = rim_rows(v0, v1, v30, v31, *parts_of(rc, vp))
    write_pair("lat", m_1, m_2, (v0, p0), (v31, p31), mp)
    write_parts(ra, (v0, v31, p0, p31), vp)
    write_parts(pa, (pv, rim_pack(pv, pk[vp : 2 * vp, :])), vp)


def adjoint_kernel(vp, inc, cells, east, west, south, out, adj):
    wide = 2 * LANES
    slots = cells.shape[1]
    for k in range(ROWS // 2):
        ids = lax.broadcasted_iota(jnp.int32, (wide, slots), 0) + k * wide
        x = folded(dot_nt(inc[...], chosen(cells[...], ids)))
        for j in range(2):
            adj[2 * k + j] = x[:, LANES * j : LANES * (j + 1)]

    def keep(i, y):
        out[i] = y

    sweep(adj, (east, west, south), keep)


def second_kernel(mid, east, west, south, field, out):
    def add(i, y):
        out[i] = y + field[i]

    sweep(mid, (east, west, south), add)


def final_kernel(vals, vp, mp, g_1, g_2, h_1, h_2, a_1, a_2, b_1, b_2, ra, rc, pk, pa, part, out, buf, sems):
    gn, gs, (_, gc, _), (_, kc) = read_ghosts(vp, mp, (g_1, g_2), (h_1, h_2))
    an, az, (gv, _, gp), (kv, _) = read_ghosts(vp, mp, (a_1, a_2), (b_1, b_2))
    ghosts = (an[0], gn[1], an[1]), (az[0], gs[1], az[1]), (gv, gc, gp), (kv, kc)
    v0, v31, p0, p31 = parts_of(ra, vp)
    pv, pp = parts_of(pa, vp)
    r0, r1, r30, r31, fix = rim_correction((v0, v31, p0, p31, pv, pp), parts_of(rc, vp) + [pk[vp : 2 * vp, :]], ghosts)
    lane = lax.broadcasted_iota(jnp.int32, (vp, LANES), 1)
    outer = (lane < 2) | (lane >= LANES - 2)
    copies = []
    for i in range(ROWS):
        x = part[i] + jnp.where(outer, roll(fix, -(4 * i + 2)), 0.0)
        row = {0: r0, 1: r1, ROWS - 2: r30, ROWS - 1: r31}.get(i)
        buf[i] = x if row is None else x + row
        copies.append(pltpu.make_async_copy(buf.at[i, pl.ds(0, vals)], out.at[:, i], sems.at[i]))
        copies[-1].start()
    for c in copies:
        c.wait()


def swap(axis, x, first):
    n = lax.axis_size(axis)
    pairs = []
    for i in range(n):
        j = i + 1 if (i % 2 == 0) == first else i - 1
        if axis == "lon":
            j %= n
        if 0 <= j < n:
            pairs.append((i, j))
    return lax.ppermute(x, axis, pairs)


def exchange(axis, m_1, m_2):
    g_2 = swap(axis, m_2, False)
    g_1 = swap(axis, m_1, True)
    return g_1, g_2


def across(x):
    return lax.all_to_all(x, ("lon", "lat"), split_axis=0, concat_axis=0, tiled=True)


def on_device(state, diffusivity, sea_mask, send_cols, obs_slots, obs_weights, obs_precision):
    vals, taps, obs = state.shape[0], obs_slots.shape[0], obs_slots.shape[1]
    owners = send_cols.shape[1] // CAP
    vp, mp = up(vals, ROWS), up(vals, 8)
    tiles = up(owners, 7 * GROUPS) // GROUPS
    slots = tiles * LANES
    cell_count = ROWS * LANES
    cells = jnp.pad(send_cols, ((0, 0), (0, tiles * GROUPS * CAP - owners * CAP)), constant_values=cell_count)
    cells = jnp.pad(cells.reshape(tiles, GROUPS * CAP), ((0, 0), (0, LANES - GROUPS * CAP)), constant_values=cell_count)
    cells = cells.reshape(1, slots)
    lines = lambda n, rows, dtype=F32: ((n * rows, LANES), dtype)
    field = ((ROWS, vp, LANES), F32)

    def loads(n):
        block = (n, vp, LANES)
        return [pltpu.VMEM(block, F32), pltpu.VMEM(block, F32), pltpu.VMEM(block, jnp.int32), pltpu.SemaphoreType.DMA((4 * n,))]

    *lat_out, rv, rc, done = call(
        functools.partial(rows_kernel, vals, vp, mp),
        [lines(3, mp), lines(3, mp), lines(4, vp), lines(4, vp), lines(1, 8)],
        state, diffusivity, sea_mask,
        in_specs=[HBM] * 3,
        scratch=loads(len(ENDS)),
        vmem=62,
    )
    lat_in = exchange("lat", *lat_out)
    wide = min(obs, 1024 if slots <= 1024 else 512)
    obs_weights, done = lax.optimization_barrier((obs_weights, done))
    w_hi, w_lo = pl.pallas_call(
        weights_kernel,
        grid=(obs // wide,),
        out_shape=[jax.ShapeDtypeStruct((slots, obs), BF16)] * 2,
        in_specs=[pl.BlockSpec((taps, wide), lambda j: (0, j))] * 2,
        out_specs=[pl.BlockSpec((slots, wide), lambda j: (0, j))] * 2,
        compiler_params=pltpu.CompilerParams(vmem_limit_bytes=20 * MIB),
        cost_estimate=pl.CostEstimate(flops=int(4e9), bytes_accessed=int(80e6), transcendentals=0),
    )(obs_slots, obs_weights)
    whole, split, east, west, south, pk = call(
        functools.partial(sweeps_kernel, vals, vp),
        [field, ((2 * vp, cell_count), BF16), field, field, field, lines(3, vp)],
        state, diffusivity, sea_mask, w_hi,
        in_specs=[VMEM] * 3 + [HBM],
        scratch=[pltpu.VMEM((ROWS, vp, LANES), F32)] * 2,
        vmem=24,
        us=8,
    )
    lon_out = call(
        lambda g_1, g_2, *refs: lon_kernel(vp, mp, g_1, g_2, True, *refs),
        [lines(1, mp)] * 2, *lat_in, pk,
        vmem=8,
    )
    lon_in = exchange("lon", *lon_out)
    (inner,) = call(
        select_kernel,
        [((vp, slots), F32)],
        split, cells,
        scratch=[pltpu.VMEM((cell_count, 7 * LANES), BF16)],
        vmem=24,
        us=3,
    )
    (payload,) = call(
        functools.partial(send_kernel, owners, vp, mp),
        [((owners * ROWS, LANES), F32)],
        *lat_in, *lon_in, rv, rc, pk, inner, cells,
        vmem=24,
    )
    payload, w_hi, w_lo = lax.optimization_barrier((payload, w_hi, w_lo))
    received = across(payload)
    matrix = 4 * slots * obs // MIB
    equivalents, payload = call(
        functools.partial(owner_kernel, vals, vp, owners),
        [((vals, obs), F32), ((owners * ROWS, LANES), F32)],
        received, w_hi, w_lo, obs_precision,
        scratch=[pltpu.VMEM((2 * vp, slots), BF16), pltpu.VMEM((2 * vp, obs), BF16)],
        vmem=20 + matrix,
    )
    incoming = across(payload)
    *lat_out, inc, ra, pa = call(
        functools.partial(back_kernel, owners, vp, mp),
        [lines(2, mp)] * 2 + [((2 * vp, slots), BF16), lines(4, vp), lines(2, vp)],
        incoming, cells, rc, pk,
        vmem=24,
    )
    lat_back = exchange("lat", *lat_out)
    (mid,) = call(
        functools.partial(adjoint_kernel, vp),
        [field],
        inc, cells, east, west, south,
        scratch=[pltpu.VMEM((ROWS, vp, LANES), F32)],
        vmem=24,
        us=4,
    )
    lat_back, mid = lax.optimization_barrier((lat_back, mid))
    lon_out = call(
        lambda g_1, g_2, *refs: lon_kernel(vp, mp, g_1, g_2, False, *refs),
        [lines(1, mp)] * 2, *lat_back, pa,
        vmem=8,
    )
    lon_back = exchange("lon", *lon_out)
    (part,) = call(second_kernel, [field], mid, east, west, south, whole, vmem=20, us=2)
    (product,) = call(
        functools.partial(final_kernel, vals, vp, mp),
        [(state.shape, F32)],
        *lat_in, *lon_in, *lat_back, *lon_back, ra, rc, pk, pa, part,
        scratch=[pltpu.VMEM((ROWS, vp, LANES), F32), pltpu.SemaphoreType.DMA((ROWS,))],
        out_specs=[HBM],
        vmem=16,
    )
    return product, equivalents


def solution(mesh):
    placed = (
        P(None, "lat", "lon"),
        P(None, "lat", "lon"),
        P(None, "lat", "lon"),
        P(("lon", "lat"), None),
        P(None, ("lon", "lat")),
        P(None, ("lon", "lat")),
        P(None, ("lon", "lat")),
    )
    return jax.shard_map(
        on_device,
        mesh=mesh,
        in_specs=placed,
        out_specs=(P(None, "lat", "lon"), P(None, ("lon", "lat"))),
        check_vma=False,
    )
```

```python
import functools

import jax
import jax.numpy as jnp
from jax import lax
from jax.experimental import pallas as pl
from jax.experimental.pallas import tpu as pltpu
from jax.sharding import PartitionSpec as P

CAP = 24
LANES = 128
GROUPS = 5
CHUNK = 32 * CAP
ROWS = 32
SENT = 30
OBS_BLOCK = 256
F32, BF16 = jnp.float32, jnp.bfloat16
MIB = 1 << 20


def up(n, k):
    return -(-n // k) * k


def roll(x, k):
    k %= LANES
    return x if k == 0 else pltpu.roll(x, k, axis=1)


def lane_of(x):
    return lax.broadcasted_iota(jnp.int32, x.shape, 1)


def tall(x, rows):
    return jnp.concatenate([x, jnp.zeros((rows - x.shape[0], x.shape[1]), x.dtype)], axis=0)


def halves(x):
    hi = x.astype(BF16)
    return hi, (x - hi.astype(F32)).astype(BF16)


def dot(a, b):
    return lax.dot_general(a, b, (((1,), (0,)), ((), ())), preferred_element_type=F32)


def dot_nt(a, b):
    return lax.dot_general(a, b, (((1,), (1,)), ((), ())), preferred_element_type=F32)


def stacked(x):
    return jnp.concatenate(halves(x), axis=0)


def folded(x):
    n = x.shape[0] // 2
    return x[:n] + x[n:]


def row_edges(c):
    east = jnp.where(lane_of(c) == LANES - 1, 0.0, jnp.minimum(c, roll(c, -1)))
    return east, roll(east, 1)


def pack_edges(cp):
    lane = lane_of(cp)
    kind = lane & 3
    inner = jnp.where(kind == 1, roll(cp, 1), roll(cp, -1))
    inner = jnp.where((kind == 1) | (kind == 2), jnp.minimum(cp, inner), 0.0)
    south = jnp.where(lane >= LANES - 4, 0.0, jnp.minimum(cp, roll(cp, -4)))
    return kind, inner, south, roll(south, 4)


def rim_rows(v0, v1, v30, v31, c0, c1, c30, c31):
    out = []
    for v, w, c, d in ((v0, v1, c0, c1), (v31, v30, c31, c30)):
        east, west = row_edges(c)
        out.append(v + east * (roll(v, -1) - v) + west * (roll(v, 1) - v) + jnp.minimum(c, d) * (w - v))
    return out


def rim_pack(vp, cp):
    kind, inner, south, north = pack_edges(cp)
    beside = jnp.where(kind == 1, roll(vp, 1), roll(vp, -1))
    return vp + inner * (beside - vp) + south * (roll(vp, -4) - vp) + north * (roll(vp, 4) - vp)


def pack_messages(vp, cp, pp, north, south):
    lane = lane_of(vp)
    kind = lane & 3
    east = jnp.where(kind == 0, roll(vp, -1), jnp.where(kind == 1, cp, roll(pp, 1)))
    west = jnp.where(kind == 0, roll(vp, -2), jnp.where(kind == 1, roll(cp, -1), pp))
    for k, x in zip((3, 7, 11, 15), (*north, *south)):
        east = jnp.where(lane == k, roll(x, k + 1), east)
        west = jnp.where(lane == k, roll(x, k), west)
    return east, west


def ghost_pack(from_w, from_e):
    one = (lane_of(from_w) & 3) == 1
    v = jnp.where(one, roll(from_e, 1), roll(from_w, 2))
    c = jnp.where(one, from_e, roll(from_w, 1))
    p = jnp.where(one, roll(from_e, -1), from_w)
    return v, c, p


def corner_pack(from_w, from_e):
    lane = lane_of(from_w)
    out = []
    for n, s in ((3, 11), (7, 15)):
        x = jnp.zeros_like(from_w)
        for at, src, k in ((1, from_e, n), (2, from_w, n), (LANES - 3, from_e, s), (LANES - 2, from_w, s)):
            x = jnp.where(lane == at, roll(src, at - k), x)
        out.append(x)
    return out


def rim_correction(own, coef, ghosts):
    v0, v31, p0, p31, vp, pp = own
    c0, c1, c30, c31, cp = coef
    (gvn, gcn, gpn), (gvs, gcs, gps), (gv, gc, gp), (kv, kc) = ghosts
    lane = lane_of(v0)
    ends = (lane == 0) | (lane == LANES - 1)
    kind, inner, south, north = pack_edges(cp)
    mid = (kind == 1) | (kind == 2)
    mg = jnp.where(mid, jnp.minimum(cp, gc), 0.0)
    f = mg * (gv - vp)
    mn, ms = jnp.minimum(c0, gcn), jnp.minimum(c31, gcs)
    fn, fs = mn * (gvn - v0), ms * (gvs - v31)
    ghost = gp - f + jnp.where(mid, jnp.minimum(gc, kc), 0.0) * (kv - gv)
    ghost_n = gpn - fn + jnp.where(ends, jnp.minimum(gcn, roll(kc, -2)), 0.0) * (roll(kv, -2) - gvn)
    ghost_s = gps - fs + jnp.where(ends, jnp.minimum(gcs, roll(kc, 2)), 0.0) * (roll(kv, 2) - gvs)
    whole = pp + f + jnp.where((lane == 1) | (lane == 2), roll(fn, 2), 0.0)
    whole = whole + jnp.where((lane == LANES - 3) | (lane == LANES - 2), roll(fs, -2), 0.0)
    whole_n = p0 + fn + jnp.where(ends, roll(f, -2), 0.0)
    whole_s = p31 + fs + jnp.where(ends, roll(f, 2), 0.0)
    qf = inner * f
    rp = f - qf + south * (roll(f, -4) - f) + north * (roll(f, 4) - f) + mg * (ghost - whole)
    rp = jnp.where(mid, rp, jnp.where(kind == 0, roll(qf, -1), roll(qf, 1)))
    rows = []
    for c, d, m, g, w, x in ((c0, c1, mn, ghost_n, whole_n, fn), (c31, c30, ms, ghost_s, whole_s, fs)):
        east, west = row_edges(c)
        across = jnp.minimum(c, d)
        rows.append(x + east * (roll(x, -1) - x) + west * (roll(x, 1) - x) - across * x + m * (g - w))
        rows.append(across * x)
    return rows[0], rows[1], rows[3], rows[2], rp


def sweep(src, edges, emit):
    east, west, south = edges
    for i in range(ROWS):
        x = src[i]
        y = x + east[i] * (roll(x, -1) - x) + west[i] * (roll(x, 1) - x)
        if i < ROWS - 1:
            y = y + south[i] * (src[i + 1] - x)
        if i > 0:
            y = y + south[i - 1] * (src[i - 1] - x)
        emit(i, y)


def chosen(cells, ids):
    return jnp.where(ids == cells, 1.0, 0.0).astype(BF16)


def rim_ids(n):
    line = lax.broadcasted_iota(jnp.int32, (LANES, n), 0)
    rows = [line + i * LANES for i in (0, 1, ROWS - 2, ROWS - 1)]
    k = line & 3
    pack = (line >> 2) * LANES + jnp.where(k < 2, LANES - 2 + k, k - 2)
    return jnp.concatenate(rows + [pack], axis=0)


def spans(o):
    a, lane = divmod(CAP * o, LANES)
    if lane + CAP <= LANES:
        return [(a, lane, 0, CAP)]
    return [(a, lane, 0, LANES - lane), (a + 1, lane - LANES, LANES - lane, CAP)]


def pack_payload(columns, out_ref, first, last):
    lane = lax.broadcasted_iota(jnp.int32, (ROWS, LANES), 1)
    tail = ROWS - 2 * (GROUPS - 1) - 2
    tiles = []
    for o in range(first, last):
        while len(tiles) <= spans(o - first)[-1][0]:
            x = columns(len(tiles) // 2)
            rest = [x[ROWS * g + SENT : ROWS * (g + 1)] for g in range(GROUPS - 1)]
            groups = [x[ROWS * g : ROWS * (g + 1)] for g in range(GROUPS - 1)]
            groups.append(jnp.concatenate([x[ROWS * (GROUPS - 1) :][:tail], *rest, jnp.zeros((2, x.shape[1]), F32)], axis=0))
            tiles += [[g[:, :LANES] for g in groups], [g[:, LANES:] for g in groups]]
        block = jnp.zeros((ROWS, LANES), F32)
        for a, at, p, q in spans(o - first):
            for g in range(GROUPS):
                piece = roll(tiles[a][g], CAP * g - at)
                block = jnp.where((lane >= CAP * g + p) & (lane < CAP * g + q), piece, block)
        out_ref[SENT * o : SENT * (o + 1), :] = block[:SENT]


def unpack_payload(in_ref, owners, slots):
    lane = lax.broadcasted_iota(jnp.int32, (ROWS, LANES), 1)
    pieces = [[jnp.zeros((ROWS, LANES), F32) for _ in range(slots // LANES)] for _ in range(GROUPS)]
    for o in range(owners):
        if o < owners - 1:
            block = in_ref[SENT * o : SENT * o + ROWS, :]
        else:
            block = tall(in_ref[SENT * o :, :], ROWS)
        for a, at, p, q in spans(o):
            for g in range(GROUPS):
                here = (lane >= at + p) & (lane < at + q)
                pieces[g][a] = jnp.where(here, roll(block, at - CAP * g), pieces[g][a])
    groups = [jnp.concatenate(x, axis=1) for x in pieces]
    tail = ROWS - 2 * (GROUPS - 1) - 2
    out = []
    for g in range(GROUPS - 1):
        out += [groups[g][:SENT], groups[-1][tail + 2 * g : tail + 2 * (g + 1)]]
    out += [groups[-1][:tail], jnp.zeros((ROWS - tail, slots), F32)]
    return jnp.concatenate(out, axis=0)


def takes(us):
    return pl.CostEstimate(flops=MIB, bytes_accessed=int(us * 3.3e6), transcendentals=0)


def call(kernel, outs, *args, in_specs=None, scratch=(), vmem=48, us=1, **kw):
    any_spec = pl.BlockSpec(memory_space=pltpu.VMEM)
    return pl.pallas_call(
        kernel,
        out_shape=[jax.ShapeDtypeStruct(s, d) for s, d in outs],
        in_specs=in_specs or [any_spec] * len(args),
        scratch_shapes=list(scratch),
        compiler_params=pltpu.CompilerParams(vmem_limit_bytes=vmem * MIB),
        cost_estimate=takes(us),
        **kw,
    )(*args)


HBM = pl.BlockSpec(memory_space=pl.ANY)
VMEM = pl.BlockSpec(memory_space=pltpu.VMEM)


def even(axis):
    return lax.rem(lax.axis_index(axis), 2) == 0


def write_parts(ref, parts, rows):
    for k, x in enumerate(parts):
        ref[rows * k : rows * (k + 1), :] = x[:rows]


def parts_of(ref, rows, vp=None):
    out = [ref[rows * k : rows * (k + 1), :] for k in range(ref.shape[0] // rows)]
    return out if vp is None else [tall(x, vp) for x in out]


def write_pair(axis, first, second, up_parts, down_parts, rows):
    for ref, e, o in ((first, down_parts, up_parts), (second, up_parts, down_parts)):
        write_parts(ref, [jnp.where(even(axis), x, y) for x, y in zip(e, o)], rows)


def read_pair(axis, first, second, rows, vp):
    f, s = parts_of(first, rows, vp), parts_of(second, rows, vp)
    before = [jnp.where(even(axis), y, x) for x, y in zip(f, s)]
    after = [jnp.where(even(axis), x, y) for x, y in zip(f, s)]
    return before, after


def start_loads(vals, state, diff, mask, sv, sd, sm, sems, rows):
    half = vals // 2
    copies = []
    for k, i in enumerate(rows):
        for src, dst in (
            (state, sv.at[k, pl.ds(0, vals)]),
            (diff, sd.at[k, pl.ds(0, vals)]),
            (mask, sm.at[k, pl.ds(0, half)]),
            (mask, sm.at[k, pl.ds(half, half)]),
        ):
            copies.append(pltpu.make_async_copy(src.at[:, i], dst, sems.at[len(copies)]))
            copies[-1].start()
    for ref in (sv, sd, sm):
        ref[:, vals:, :] = jnp.zeros((ref.shape[0], ref.shape[1] - vals, LANES), ref.dtype)
    return copies


ENDS = (0, 1, ROWS - 2, ROWS - 1)


def rows_kernel(vals, vp, mp, state, diff, mask, m_1, m_2, rv, rc, done, sv, sd, sm, sems):
    done[...] = jnp.zeros(done.shape, F32)
    for c in start_loads(vals, state, diff, mask, sv, sd, sm, sems, ENDS):
        c.wait()
    v0, v1, v30, v31 = (sv[k] for k in range(4))
    c0, c1, c30, c31 = (sd[k] * sm[k].astype(F32) for k in range(4))
    p0, p31 = rim_rows(v0, v1, v30, v31, c0, c1, c30, c31)
    write_pair("lat", m_1, m_2, (v0, c0, p0), (v31, c31, p31), mp)
    write_parts(rv, (v0, v31, p0, p31), vp)
    write_parts(rc, (c0, c1, c30, c31), vp)


def by_grid_row(x, dst, first):
    n = x.shape[0]
    if n < 8:
        x = jnp.concatenate([x, jnp.zeros((8 - n, *x.shape[1:]), x.dtype)], axis=0)
    y = jnp.swapaxes(x, 0, 1)
    v, i = first
    for k in range(8):
        dst[i + k, v : v + 8, :] = y[k]


def sweeps_kernel(vals, vp, state, diff, mask, after, field, out, east, west, south, pk, coef, mid):
    half = vals // 2
    for v in range(0, vp, 8):
        if v >= vals:
            for ref in (field, coef):
                ref[:, v : v + 8, :] = jnp.zeros((ROWS, 8, LANES), F32)
            continue
        end = min(v + 8, vals)
        for i in range(0, ROWS, 8):
            rows = slice(i, i + 8)
            if end <= half:
                m = mask[v:end, rows, :]
            elif v >= half:
                m = mask[v - half : end - half, rows, :]
            else:
                m = jnp.concatenate([mask[v:half, rows, :], mask[: end - half, rows, :]], axis=0)
            by_grid_row(state[v:end, rows, :], field, (v, i))
            by_grid_row(diff[v:end, rows, :] * m.astype(F32), coef, (v, i))
    lane = lax.broadcasted_iota(jnp.int32, (vp, LANES), 1)
    pv = jnp.zeros((vp, LANES), F32)
    pc = jnp.zeros((vp, LANES), F32)
    c = coef[0]
    for i in range(ROWS):
        if i < ROWS - 1:
            cn = coef[i + 1]
            south[i] = jnp.minimum(c, cn)
        else:
            south[i] = jnp.zeros_like(c)
        e = jnp.where(lane == LANES - 1, 0.0, jnp.minimum(c, roll(c, -1)))
        east[i] = e
        west[i] = roll(e, 1)
        here = (lane >> 2) == i
        pv = jnp.where(here, roll(field[i], 4 * i + 2), pv)
        pc = jnp.where(here, roll(c, 4 * i + 2), pc)
        c = cn
    write_parts(pk, (pv, pc, rim_pack(pv, pc)), vp)
    edges = (east, west, south)

    def keep(i, y):
        mid[i] = y

    def split(i, y):
        out[:, LANES * i : LANES * (i + 1)] = stacked(y)

    sweep(field, edges, keep)
    sweep(mid, edges, split)


def lon_kernel(vp, mp, g_1, g_2, coefs, pk, m_1, m_2):
    north, south = read_pair("lat", g_1, g_2, mp, vp)
    if coefs:
        pv, pc, pp = parts_of(pk, vp)
        north, south = north[:2], south[:2]
    else:
        pv, pp = parts_of(pk, vp)
        pc = pv
        north, south = (north[0], north[0]), (south[0], south[0])
    east, west = pack_messages(pv, pc, pp, north, south)
    write_pair("lon", m_1, m_2, (west,), (east,), mp)


def select_kernel(smooth, cells, out, hot):
    chunk = hot.shape[1]
    wide = 4 * LANES
    for base in range(0, cells.shape[1], chunk):
        for k in range(0, ROWS * LANES, wide):
            ids = lax.broadcasted_iota(jnp.int32, (wide, chunk), 0) + k
            hot[k : k + wide, :] = chosen(cells[:, base : base + chunk], ids)
        total = jnp.zeros((smooth.shape[0], chunk), F32)
        for k in range(0, ROWS * LANES, wide):
            total = total + dot(smooth[:, k : k + wide], hot[k : k + wide, :])
        out[:, base : base + chunk] = folded(total)


def weights_kernel(slots, weights, hi, lo):
    taps = range(slots.shape[0])
    at = [slots[k : k + 1, :] for k in taps]
    w = [weights[k : k + 1, :] for k in taps]
    for a in taps:
        for b in range(a + 1, len(taps)):
            same = at[a] == at[b]
            w[a] = w[a] + jnp.where(same, w[b], 0.0)
            at[b] = jnp.where(same, -1, at[b])
    at = [x.astype(jnp.int16) for x in at]
    parts = [halves(x) for x in w]
    shape = (LANES, hi.shape[1])
    for r in range(0, hi.shape[0], LANES):
        row = (lax.broadcasted_iota(jnp.int32, shape, 0) + r).astype(jnp.int16)
        h = l = jnp.zeros(shape, BF16)
        for k in taps:
            here = row == at[k]
            h, l = jnp.where(here, parts[k][0], h), jnp.where(here, parts[k][1], l)
        hi[r : r + LANES, :] = h
        lo[r : r + LANES, :] = l


def read_ghosts(vp, mp, lat, lon):
    north, south = read_pair("lat", *lat, mp, vp)
    west, east = read_pair("lon", *lon, mp, vp)
    return north, south, ghost_pack(west[0], east[0]), corner_pack(west[0], east[0])


def send_kernel(owners, vp, mp, g_1, g_2, h_1, h_2, rv, rc, pk, inner, cells, out):
    ghosts = read_ghosts(vp, mp, (g_1, g_2), (h_1, h_2))
    v0, v31, p0, p31 = parts_of(rv, vp)
    pv, pc, pp = parts_of(pk, vp)
    fix = rim_correction((v0, v31, p0, p31, pv, pp), parts_of(rc, vp) + [pc], ghosts)
    wide = 2 * LANES
    fix = stacked(jnp.concatenate(fix, axis=1))
    ids = rim_ids(wide)

    def columns(k):
        at = slice(wide * k, wide * (k + 1))
        return inner[:, at] + folded(dot(fix, chosen(cells[:, at], ids)))

    pack_payload(columns, out, 0, owners)


def owner_kernel(vals, vp, owners, got, w_hi, w_lo, prec, equiv, back, r2, w2):
    r2[...] = stacked(unpack_payload(got, owners, r2.shape[1]))
    wide = min(512, equiv.shape[1])
    for q in range(0, equiv.shape[1], wide):
        at = slice(q, q + wide)
        e = (folded(dot(r2[...], w_hi[:, at])) + dot(r2[:vp, :], w_lo[:, at]))[:vals]
        equiv[:, at] = e
        w2[:, at] = stacked(tall(prec[:, at] * e, vp))
    for o in range(0, r2.shape[1], CHUNK):

        def columns(k):
            at = slice(o + 2 * LANES * k, o + 2 * LANES * (k + 1))
            return folded(dot_nt(w2[...], w_hi[at, :])) + dot_nt(w2[:vp, :], w_lo[at, :])

        pack_payload(columns, back, o // CAP, (o + CHUNK) // CAP)


def back_kernel(owners, vp, mp, got, cells, rc, pk, m_1, m_2, inc, ra, pa):
    slots = cells.shape[1]
    x = stacked(unpack_payload(got, owners, slots))
    inc[...] = x
    rims = folded(dot_nt(x, chosen(cells[...], rim_ids(slots))))
    v0, v1, v30, v31, pv = (rims[:, LANES * k : LANES * (k + 1)] for k in range(5))
    p0, p31 = rim_rows(v0, v1, v30, v31, *parts_of(rc, vp))
    write_pair("lat", m_1, m_2, (v0, p0), (v31, p31), mp)
    write_parts(ra, (v0, v31, p0, p31), vp)
    write_parts(pa, (pv, rim_pack(pv, pk[vp : 2 * vp, :])), vp)


def adjoint_kernel(vp, inc, cells, east, west, south, out, adj):
    wide = 2 * LANES
    slots = cells.shape[1]
    for k in range(ROWS // 2):
        ids = lax.broadcasted_iota(jnp.int32, (wide, slots), 0) + k * wide
        x = folded(dot_nt(inc[...], chosen(cells[...], ids)))
        for j in range(2):
            adj[2 * k + j] = x[:, LANES * j : LANES * (j + 1)]

    def keep(i, y):
        out[i] = y

    sweep(adj, (east, west, south), keep)


def second_kernel(mid, east, west, south, field, out):
    def add(i, y):
        out[i] = y + field[i]

    sweep(mid, (east, west, south), add)


def final_kernel(vals, vp, mp, g_1, g_2, h_1, h_2, a_1, a_2, b_1, b_2, ra, rc, pk, pa, part, out, buf, sems):
    gn, gs, (_, gc, _), (_, kc) = read_ghosts(vp, mp, (g_1, g_2), (h_1, h_2))
    an, az, (gv, _, gp), (kv, _) = read_ghosts(vp, mp, (a_1, a_2), (b_1, b_2))
    ghosts = (an[0], gn[1], an[1]), (az[0], gs[1], az[1]), (gv, gc, gp), (kv, kc)
    v0, v31, p0, p31 = parts_of(ra, vp)
    pv, pp = parts_of(pa, vp)
    r0, r1, r30, r31, fix = rim_correction((v0, v31, p0, p31, pv, pp), parts_of(rc, vp) + [pk[vp : 2 * vp, :]], ghosts)
    lane = lax.broadcasted_iota(jnp.int32, (vp, LANES), 1)
    outer = (lane < 2) | (lane >= LANES - 2)
    copies = []
    for i in range(ROWS):
        x = part[i] + jnp.where(outer, roll(fix, -(4 * i + 2)), 0.0)
        row = {0: r0, 1: r1, ROWS - 2: r30, ROWS - 1: r31}.get(i)
        buf[i] = x if row is None else x + row
        copies.append(pltpu.make_async_copy(buf.at[i, pl.ds(0, vals)], out.at[:, i], sems.at[i]))
        copies[-1].start()
    for c in copies:
        c.wait()


def swap(axis, x, first):
    n = lax.axis_size(axis)
    pairs = []
    for i in range(n):
        j = i + 1 if (i % 2 == 0) == first else i - 1
        if axis == "lon":
            j %= n
        if 0 <= j < n:
            pairs.append((i, j))
    return lax.ppermute(x, axis, pairs)


def exchange(axis, m_1, m_2):
    g_2 = swap(axis, m_2, False)
    g_1 = swap(axis, m_1, True)
    return g_1, g_2


def across(x):
    flat = x.reshape(lax.axis_size(("lon", "lat")), 1, SENT * LANES)
    return lax.all_to_all(flat, ("lon", "lat"), split_axis=0, concat_axis=0, tiled=True).reshape(x.shape)


def on_device(state, diffusivity, sea_mask, send_cols, obs_slots, obs_weights, obs_precision):
    vals, taps, obs = state.shape[0], obs_slots.shape[0], obs_slots.shape[1]
    owners = send_cols.shape[1] // CAP
    vp, mp = up(vals, ROWS), up(vals, 8)
    slots = owners * CAP
    cell_count = ROWS * LANES
    cells = send_cols
    blocks = ((owners * SENT, LANES), F32)
    lines = lambda n, rows, dtype=F32: ((n * rows, LANES), dtype)
    field = ((ROWS, vp, LANES), F32)

    def loads(n):
        block = (n, vp, LANES)
        return [pltpu.VMEM(block, F32), pltpu.VMEM(block, F32), pltpu.VMEM(block, jnp.int32), pltpu.SemaphoreType.DMA((4 * n,))]

    *lat_out, rv, rc, done = call(
        functools.partial(rows_kernel, vals, vp, mp),
        [lines(3, mp), lines(3, mp), lines(4, vp), lines(4, vp), lines(1, 8)],
        state, diffusivity, sea_mask,
        in_specs=[HBM] * 3,
        scratch=loads(len(ENDS)),
        vmem=62,
    )
    lat_in = exchange("lat", *lat_out)
    wide = obs if slots <= 1024 else 512
    obs_weights, done = lax.optimization_barrier((obs_weights, done))
    w_hi, w_lo = pl.pallas_call(
        weights_kernel,
        grid=(obs // wide,),
        out_shape=[jax.ShapeDtypeStruct((slots, obs), BF16)] * 2,
        in_specs=[pl.BlockSpec((taps, wide), lambda j: (0, j))] * 2,
        out_specs=[pl.BlockSpec((slots, wide), lambda j: (0, j))] * 2,
        compiler_params=pltpu.CompilerParams(vmem_limit_bytes=20 * MIB),
        cost_estimate=pl.CostEstimate(flops=int(4e9), bytes_accessed=int(80e6), transcendentals=0),
    )(obs_slots, obs_weights)
    whole, split, east, west, south, pk = call(
        functools.partial(sweeps_kernel, vals, vp),
        [field, ((2 * vp, cell_count), BF16), field, field, field, lines(3, vp)],
        state, diffusivity, sea_mask, w_hi,
        in_specs=[VMEM] * 3 + [HBM],
        scratch=[pltpu.VMEM((ROWS, vp, LANES), F32)] * 2,
        vmem=24,
        us=8,
    )
    lon_out = call(
        lambda g_1, g_2, *refs: lon_kernel(vp, mp, g_1, g_2, True, *refs),
        [lines(1, mp)] * 2, *lat_in, pk,
        vmem=8,
    )
    lon_in = exchange("lon", *lon_out)
    (inner,) = call(
        select_kernel,
        [((vp, slots), F32)],
        split, cells,
        scratch=[pltpu.VMEM((cell_count, CHUNK), BF16)],
        vmem=24,
        us=3,
    )
    (payload,) = call(
        functools.partial(send_kernel, owners, vp, mp),
        [blocks],
        *lat_in, *lon_in, rv, rc, pk, inner, cells,
        vmem=24,
    )
    payload, w_hi, w_lo = lax.optimization_barrier((payload, w_hi, w_lo))
    received = across(payload)
    matrix = 4 * slots * obs // MIB
    equivalents, payload = call(
        functools.partial(owner_kernel, vals, vp, owners),
        [((vals, obs), F32), blocks],
        received, w_hi, w_lo, obs_precision,
        scratch=[pltpu.VMEM((2 * vp, slots), BF16), pltpu.VMEM((2 * vp, obs), BF16)],
        vmem=20 + matrix,
    )
    incoming = across(payload)
    *lat_out, inc, ra, pa = call(
        functools.partial(back_kernel, owners, vp, mp),
        [lines(2, mp)] * 2 + [((2 * vp, slots), BF16), lines(4, vp), lines(2, vp)],
        incoming, cells, rc, pk,
        vmem=24,
    )
    lat_back = exchange("lat", *lat_out)
    (mid,) = call(
        functools.partial(adjoint_kernel, vp),
        [field],
        inc, cells, east, west, south,
        scratch=[pltpu.VMEM((ROWS, vp, LANES), F32)],
        vmem=24,
        us=4,
    )
    lat_back, mid = lax.optimization_barrier((lat_back, mid))
    lon_out = call(
        lambda g_1, g_2, *refs: lon_kernel(vp, mp, g_1, g_2, False, *refs),
        [lines(1, mp)] * 2, *lat_back, pa,
        vmem=8,
    )
    lon_back = exchange("lon", *lon_out)
    (part,) = call(second_kernel, [field], mid, east, west, south, whole, vmem=20, us=2)
    (product,) = call(
        functools.partial(final_kernel, vals, vp, mp),
        [(state.shape, F32)],
        *lat_in, *lon_in, *lat_back, *lon_back, ra, rc, pk, pa, part,
        scratch=[pltpu.VMEM((ROWS, vp, LANES), F32), pltpu.SemaphoreType.DMA((ROWS,))],
        out_specs=[HBM],
        vmem=16,
    )
    return product, equivalents


def solution(mesh):
    placed = (
        P(None, "lat", "lon"),
        P(None, "lat", "lon"),
        P(None, "lat", "lon"),
        P(("lon", "lat"), None),
        P(None, ("lon", "lat")),
        P(None, ("lon", "lat")),
        P(None, ("lon", "lat")),
    )
    return jax.shard_map(
        on_device,
        mesh=mesh,
        in_specs=placed,
        out_specs=(P(None, "lat", "lon"), P(None, ("lon", "lat"))),
        check_vma=False,
    )
```

```python
import functools

import jax
import jax.numpy as jnp
from jax import lax
from jax.experimental import pallas as pl
from jax.experimental.pallas import tpu as pltpu
from jax.sharding import PartitionSpec as P

CAP = 24
LANES = 128
GROUPS = 5
CHUNK = 32 * CAP
ROWS = 32
SENT = 30
OBS_BLOCK = 256
F32, BF16 = jnp.float32, jnp.bfloat16
MIB = 1 << 20


def up(n, k):
    return -(-n // k) * k


def roll(x, k):
    k %= LANES
    return x if k == 0 else pltpu.roll(x, k, axis=1)


def lane_of(x):
    return lax.broadcasted_iota(jnp.int32, x.shape, 1)


def tall(x, rows):
    if x.shape[0] == rows:
        return x
    return jnp.concatenate([x, jnp.zeros((rows - x.shape[0], x.shape[1]), x.dtype)], axis=0)


def halves(x):
    hi = x.astype(BF16)
    return hi, (x - hi.astype(F32)).astype(BF16)


def dot(a, b):
    return lax.dot_general(a, b, (((1,), (0,)), ((), ())), preferred_element_type=F32)


def dot_nt(a, b):
    return lax.dot_general(a, b, (((1,), (1,)), ((), ())), preferred_element_type=F32)


def stacked(x):
    return jnp.concatenate(halves(x), axis=0)


def folded(x):
    n = x.shape[0] // 2
    return x[:n] + x[n:]


def row_edges(c):
    east = jnp.where(lane_of(c) == LANES - 1, 0.0, jnp.minimum(c, roll(c, -1)))
    return east, roll(east, 1)


def pack_edges(cp):
    lane = lane_of(cp)
    kind = lane & 3
    inner = jnp.where(kind == 1, roll(cp, 1), roll(cp, -1))
    inner = jnp.where((kind == 1) | (kind == 2), jnp.minimum(cp, inner), 0.0)
    south = jnp.where(lane >= LANES - 4, 0.0, jnp.minimum(cp, roll(cp, -4)))
    return kind, inner, south, roll(south, 4)


def rim_rows(v0, v1, v30, v31, c0, c1, c30, c31):
    out = []
    for v, w, c, d in ((v0, v1, c0, c1), (v31, v30, c31, c30)):
        east, west = row_edges(c)
        out.append(v + east * (roll(v, -1) - v) + west * (roll(v, 1) - v) + jnp.minimum(c, d) * (w - v))
    return out


def rim_pack(vp, cp):
    kind, inner, south, north = pack_edges(cp)
    beside = jnp.where(kind == 1, roll(vp, 1), roll(vp, -1))
    return vp + inner * (beside - vp) + south * (roll(vp, -4) - vp) + north * (roll(vp, 4) - vp)


def pack_messages(vp, cp, pp, north=(), south=()):
    lane = lane_of(vp)
    kind = lane & 3
    east = jnp.where(kind == 0, roll(vp, -1), jnp.where(kind == 1, cp, roll(pp, 1)))
    west = jnp.where(kind == 0, roll(vp, -2), jnp.where(kind == 1, roll(cp, -1), pp))
    for k, x in zip((3, 7, 11, 15), (*north, *south)):
        east = jnp.where(lane == k, roll(x, k + 1), east)
        west = jnp.where(lane == k, roll(x, k), west)
    return east, west


def ghost_pack(from_w, from_e):
    one = (lane_of(from_w) & 3) == 1
    v = jnp.where(one, roll(from_e, 1), roll(from_w, 2))
    c = jnp.where(one, from_e, roll(from_w, 1))
    p = jnp.where(one, roll(from_e, -1), from_w)
    return v, c, p


def corner_pack(from_w, from_e):
    lane = lane_of(from_w)
    out = []
    for n, s in ((3, 11), (7, 15)):
        x = jnp.zeros_like(from_w)
        for at, src, k in ((1, from_e, n), (2, from_w, n), (LANES - 3, from_e, s), (LANES - 2, from_w, s)):
            x = jnp.where(lane == at, roll(src, at - k), x)
        out.append(x)
    return out


def pack_correction(vp, pp, cp, gv, gc, gp, more_ghost=0.0, more_whole=0.0):
    kind, inner, south, north = pack_edges(cp)
    mid = (kind == 1) | (kind == 2)
    mg = jnp.where(mid, jnp.minimum(cp, gc), 0.0)
    f = mg * (gv - vp)
    qf = inner * f
    again = mg * (gp - f + more_ghost - (pp + f + more_whole))
    rp = f - qf + south * (roll(f, -4) - f) + north * (roll(f, 4) - f) + again
    return jnp.where(mid, rp, jnp.where(kind == 0, roll(qf, -1), roll(qf, 1))), f


def rim_correction(own, coef, ghosts, complete=False):
    v0, v31, p0, p31, vp, pp = own
    c0, c1, c30, c31, cp = coef
    (gvn, gcn, gpn), (gvs, gcs, gps), (gv, gc, gp), (kv, kc) = ghosts
    lane = lane_of(v0)
    ends = (lane == 0) | (lane == LANES - 1)
    mn, ms = jnp.minimum(c0, gcn), jnp.minimum(c31, gcs)
    fn, fs = mn * (gvn - v0), ms * (gvs - v31)
    more_ghost = jnp.where(((lane & 3) == 1) | ((lane & 3) == 2), jnp.minimum(gc, kc), 0.0) * (kv - gv)
    more_whole = jnp.where((lane == 1) | (lane == 2), roll(fn, 2), 0.0)
    more_whole = more_whole + jnp.where((lane == LANES - 3) | (lane == LANES - 2), roll(fs, -2), 0.0)
    rp, f = pack_correction(vp, pp, cp, gv, gc, gp, more_ghost, more_whole)
    ghost_n, ghost_s = gpn - fn, gps - fs
    if not complete:
        ghost_n = ghost_n + jnp.where(ends, jnp.minimum(gcn, roll(kc, -2)), 0.0) * (roll(kv, -2) - gvn)
        ghost_s = ghost_s + jnp.where(ends, jnp.minimum(gcs, roll(kc, 2)), 0.0) * (roll(kv, 2) - gvs)
    whole_n = p0 + fn + jnp.where(ends, roll(f, -2), 0.0)
    whole_s = p31 + fs + jnp.where(ends, roll(f, 2), 0.0)
    rows = []
    for c, d, m, g, w, x in ((c0, c1, mn, ghost_n, whole_n, fn), (c31, c30, ms, ghost_s, whole_s, fs)):
        east, west = row_edges(c)
        across = jnp.minimum(c, d)
        rows.append(x + east * (roll(x, -1) - x) + west * (roll(x, 1) - x) - across * x + m * (g - w))
        rows.append(across * x)
    return rows[0], rows[1], rows[3], rows[2], rp


def sweep(src, edges, emit):
    east, west, south = edges
    for i in range(ROWS):
        x = src[i]
        y = x + east[i] * (roll(x, -1) - x) + west[i] * (roll(x, 1) - x)
        if i < ROWS - 1:
            y = y + south[i] * (src[i + 1] - x)
        if i > 0:
            y = y + south[i - 1] * (src[i - 1] - x)
        emit(i, y)


def chosen(cells, ids):
    return jnp.where(ids == cells, 1.0, 0.0).astype(BF16)


def rim_ids(n):
    line = lax.broadcasted_iota(jnp.int32, (LANES, n), 0)
    rows = [line + i * LANES for i in (0, 1, ROWS - 2, ROWS - 1)]
    k = line & 3
    pack = (line >> 2) * LANES + jnp.where(k < 2, LANES - 2 + k, k - 2)
    return jnp.concatenate(rows + [pack], axis=0)


def spans(o):
    a, lane = divmod(CAP * o, LANES)
    if lane + CAP <= LANES:
        return [(a, lane, 0, CAP)]
    return [(a, lane, 0, LANES - lane), (a + 1, lane - LANES, LANES - lane, CAP)]


def merged(old, new, lo, hi):
    if old is None:
        return new
    lane = lane_of(new)
    return jnp.where((lane >= lo) & (lane < hi), new, old)


def by_shift(pairs, a):
    out = {}
    for o in pairs:
        for tile, at, p, q in spans(o):
            if tile == a:
                for g in range(GROUPS):
                    out.setdefault(g - o, []).append((o, g, at + p, CAP * g + p, q - p))
    return out


def pack_payload(columns, out_ref, first, last):
    tail = ROWS - 2 * (GROUPS - 1) - 2
    pairs = range(last - first)
    blocks = [None for _ in pairs]
    for a in range(spans(pairs[-1])[-1][0] + 1):
        if a % 2 == 0:
            both = columns(a // 2)
        x = both[:, LANES * (a % 2) : LANES * (a % 2 + 1)]
        rest = [x[ROWS * g + SENT : ROWS * (g + 1)] for g in range(GROUPS - 1)]
        groups = [x[ROWS * g : ROWS * (g + 1)] for g in range(GROUPS - 1)]
        groups.append(jnp.concatenate([x[ROWS * (GROUPS - 1) :][:tail], *rest, jnp.zeros((2, LANES), F32)], axis=0))
        for d, moves in by_shift(pairs, a).items():
            z = None
            for o, g, src, dst, n in moves:
                z = merged(z, groups[g], src, src + n)
            z = roll(z, CAP * d)
            for o, g, src, dst, n in moves:
                blocks[o] = merged(blocks[o], z, dst, dst + n)
        for o in pairs:
            if spans(o)[-1][0] == a:
                at = SENT * (first + o)
                out_ref[at : at + SENT, :] = blocks[o][:SENT]


def unpack_payload(in_ref, owners, slots):
    pairs = range(owners)
    blocks = [in_ref[SENT * o : SENT * o + ROWS, :] if o < owners - 1 else tall(in_ref[SENT * o :, :], ROWS) for o in pairs]
    pieces = [[None for _ in range(slots // LANES)] for _ in range(GROUPS)]
    for a in range(slots // LANES):
        for d, moves in by_shift(pairs, a).items():
            z = None
            for o, g, dst, src, n in moves:
                z = merged(z, blocks[o], src, src + n)
            z = roll(z, -CAP * d)
            for o, g, dst, src, n in moves:
                pieces[g][a] = merged(pieces[g][a], z, dst, dst + n)
    groups = [jnp.concatenate(x, axis=1) for x in pieces]
    tail = ROWS - 2 * (GROUPS - 1) - 2
    out = []
    for g in range(GROUPS - 1):
        out += [groups[g][:SENT], groups[-1][tail + 2 * g : tail + 2 * (g + 1)]]
    out += [groups[-1][:tail], jnp.zeros((ROWS - tail, slots), F32)]
    return jnp.concatenate(out, axis=0)


def takes(us):
    return pl.CostEstimate(flops=MIB, bytes_accessed=int(us * 3.3e6), transcendentals=0)


def call(kernel, outs, *args, in_specs=None, scratch=(), vmem=48, us=1, **kw):
    any_spec = pl.BlockSpec(memory_space=pltpu.VMEM)
    return pl.pallas_call(
        kernel,
        out_shape=[jax.ShapeDtypeStruct(s, d) for s, d in outs],
        in_specs=in_specs or [any_spec] * len(args),
        scratch_shapes=list(scratch),
        compiler_params=pltpu.CompilerParams(vmem_limit_bytes=vmem * MIB),
        cost_estimate=takes(us),
        **kw,
    )(*args)


HBM = pl.BlockSpec(memory_space=pl.ANY)
VMEM = pl.BlockSpec(memory_space=pltpu.VMEM)


def even(axis):
    return lax.rem(lax.axis_index(axis), 2) == 0


def write_parts(ref, parts, rows):
    for k, x in enumerate(parts):
        ref[rows * k : rows * (k + 1), :] = x[:rows]


def parts_of(ref, rows, vp=None):
    out = [ref[rows * k : rows * (k + 1), :] for k in range(ref.shape[0] // rows)]
    return out if vp is None else [tall(x, vp) for x in out]


def write_pair(axis, first, second, up_parts, down_parts, rows):
    for ref, e, o in ((first, down_parts, up_parts), (second, up_parts, down_parts)):
        write_parts(ref, [jnp.where(even(axis), x, y) for x, y in zip(e, o)], rows)


def read_pair(axis, first, second, rows, vp):
    f, s = parts_of(first, rows, vp), parts_of(second, rows, vp)
    before = [jnp.where(even(axis), y, x) for x, y in zip(f, s)]
    after = [jnp.where(even(axis), x, y) for x, y in zip(f, s)]
    return before, after


def start_loads(vals, state, diff, mask, sv, sd, sm, sems, rows):
    half = vals // 2
    copies = []
    for k, i in enumerate(rows):
        for src, dst in (
            (state, sv.at[k, pl.ds(0, vals)]),
            (diff, sd.at[k, pl.ds(0, vals)]),
            (mask, sm.at[k, pl.ds(0, half)]),
            (mask, sm.at[k, pl.ds(half, half)]),
        ):
            copies.append(pltpu.make_async_copy(src.at[:, i], dst, sems.at[len(copies)]))
            copies[-1].start()
    for ref in (sv, sd, sm):
        ref[:, vals:, :] = jnp.zeros((ref.shape[0], ref.shape[1] - vals, LANES), ref.dtype)
    return copies


ENDS = (0, 1, ROWS - 2, ROWS - 1)


def rows_kernel(vals, vp, mp, state, diff, mask, m_1, m_2, rv, rc, done, sv, sd, sm, sems):
    done[...] = jnp.zeros(done.shape, F32)
    for c in start_loads(vals, state, diff, mask, sv, sd, sm, sems, ENDS):
        c.wait()
    v0, v1, v30, v31 = (sv[k] for k in range(4))
    c0, c1, c30, c31 = (sd[k] * sm[k].astype(F32) for k in range(4))
    p0, p31 = rim_rows(v0, v1, v30, v31, c0, c1, c30, c31)
    write_pair("lat", m_1, m_2, (v0, c0, p0), (v31, c31, p31), mp)
    write_parts(rv, (v0, v31, p0, p31), vp)
    write_parts(rc, (c0, c1, c30, c31), vp)


def by_grid_row(x, dst, first):
    n = x.shape[0]
    if n < 8:
        x = jnp.concatenate([x, jnp.zeros((8 - n, *x.shape[1:]), x.dtype)], axis=0)
    y = jnp.swapaxes(x, 0, 1)
    v, i = first
    for k in range(8):
        dst[i + k, v : v + 8, :] = y[k]


def outer_columns(ref):
    total = jnp.zeros((2 * ref.shape[1], LANES), F32)
    r = lax.broadcasted_iota(jnp.int32, (2 * LANES, LANES), 0)
    lane = lax.broadcasted_iota(jnp.int32, (2 * LANES, LANES), 1)
    source = (lane >> 2) * LANES + jnp.where((lane & 3) < 2, LANES - 2 + (lane & 3), (lane & 3) - 2)
    for i in range(0, ROWS, 2):
        take = jnp.where(r == source - i * LANES, 1.0, 0.0).astype(BF16)
        total = total + dot(stacked(jnp.concatenate([ref[i], ref[i + 1]], axis=1)), take)
    return folded(total)


def sweeps_kernel(vals, vp, state, diff, mask, after, field, out, east, west, south, pk, coef, mid):
    half = vals // 2
    for v in range(0, vp, 8):
        if v >= vals:
            for ref in (field, coef):
                ref[:, v : v + 8, :] = jnp.zeros((ROWS, 8, LANES), F32)
            continue
        end = min(v + 8, vals)
        for i in range(0, ROWS, 8):
            rows = slice(i, i + 8)
            if end <= half:
                m = mask[v:end, rows, :]
            elif v >= half:
                m = mask[v - half : end - half, rows, :]
            else:
                m = jnp.concatenate([mask[v:half, rows, :], mask[: end - half, rows, :]], axis=0)
            by_grid_row(state[v:end, rows, :], field, (v, i))
            by_grid_row(diff[v:end, rows, :] * m.astype(F32), coef, (v, i))
    lane = lax.broadcasted_iota(jnp.int32, (vp, LANES), 1)
    c = coef[0]
    for i in range(ROWS):
        if i < ROWS - 1:
            cn = coef[i + 1]
            south[i] = jnp.minimum(c, cn)
        else:
            south[i] = jnp.zeros_like(c)
        e = jnp.where(lane == LANES - 1, 0.0, jnp.minimum(c, roll(c, -1)))
        east[i] = e
        west[i] = roll(e, 1)
        c = cn
    pv, pc = outer_columns(field), outer_columns(coef)
    write_parts(pk, (pv, pc, rim_pack(pv, pc)), vp)
    edges = (east, west, south)

    def keep(i, y):
        mid[i] = y

    def split(i, y):
        out[:, LANES * i : LANES * (i + 1)] = stacked(y)

    sweep(field, edges, keep)
    sweep(mid, edges, split)


def lon_kernel(vp, mp, g_1, g_2, pk, m_1, m_2):
    north, south = read_pair("lat", g_1, g_2, mp, vp)
    east, west = pack_messages(*parts_of(pk, vp), north[:2], south[:2])
    write_pair("lon", m_1, m_2, (west,), (east,), mp)


def select_kernel(smooth, cells, out, hot):
    chunk = hot.shape[1]
    wide = 4 * LANES
    for base in range(0, cells.shape[1], chunk):
        for k in range(0, ROWS * LANES, wide):
            ids = lax.broadcasted_iota(jnp.int32, (wide, chunk), 0) + k
            hot[k : k + wide, :] = chosen(cells[:, base : base + chunk], ids)
        total = jnp.zeros((smooth.shape[0], chunk), F32)
        for k in range(0, ROWS * LANES, wide):
            total = total + dot(smooth[:, k : k + wide], hot[k : k + wide, :])
        out[:, base : base + chunk] = folded(total)


def weights_kernel(slots, weights, hi, lo):
    taps = range(slots.shape[0])
    at = [slots[k : k + 1, :] for k in taps]
    w = [weights[k : k + 1, :] for k in taps]
    for a in taps:
        for b in range(a + 1, len(taps)):
            same = at[a] == at[b]
            w[a] = w[a] + jnp.where(same, w[b], 0.0)
            at[b] = jnp.where(same, -1, at[b])
    at = [x.astype(jnp.int16) for x in at]
    parts = [halves(x) for x in w]
    shape = (LANES, hi.shape[1])
    for r in range(0, hi.shape[0], LANES):
        row = (lax.broadcasted_iota(jnp.int32, shape, 0) + r).astype(jnp.int16)
        h = l = jnp.zeros(shape, BF16)
        for k in taps:
            here = row == at[k]
            h, l = jnp.where(here, parts[k][0], h), jnp.where(here, parts[k][1], l)
        hi[r : r + LANES, :] = h
        lo[r : r + LANES, :] = l


def read_ghosts(vp, mp, lat, lon):
    north, south = read_pair("lat", *lat, mp, vp)
    west, east = read_pair("lon", *lon, mp, vp)
    return north, south, ghost_pack(west[0], east[0]), corner_pack(west[0], east[0])


def send_kernel(owners, vp, mp, g_1, g_2, h_1, h_2, rv, rc, pk, inner, cells, out):
    ghosts = read_ghosts(vp, mp, (g_1, g_2), (h_1, h_2))
    v0, v31, p0, p31 = parts_of(rv, vp)
    pv, pc, pp = parts_of(pk, vp)
    fix = rim_correction((v0, v31, p0, p31, pv, pp), parts_of(rc, vp) + [pc], ghosts)
    wide = 2 * LANES
    fix = stacked(jnp.concatenate(fix, axis=1))
    ids = rim_ids(wide)

    def columns(k):
        at = slice(wide * k, wide * (k + 1))
        return inner[:, at] + folded(dot(fix, chosen(cells[:, at], ids)))

    pack_payload(columns, out, 0, owners)


def owner_kernel(vals, vp, owners, got, w_hi, w_lo, prec, equiv, back, r2, w2):
    r2[...] = stacked(unpack_payload(got, owners, r2.shape[1]))
    wide = min(512, equiv.shape[1])
    for q in range(0, equiv.shape[1], wide):
        at = slice(q, q + wide)
        e = (folded(dot(r2[...], w_hi[:, at])) + dot(r2[:vp, :], w_lo[:, at]))[:vals]
        equiv[:, at] = e
        w2[:, at] = stacked(tall(prec[:, at] * e, vp))
    for o in range(0, r2.shape[1], CHUNK):

        def columns(k):
            at = slice(o + 2 * LANES * k, o + 2 * LANES * (k + 1))
            return folded(dot_nt(w2[...], w_hi[at, :])) + dot_nt(w2[:vp, :], w_lo[at, :])

        pack_payload(columns, back, o // CAP, (o + CHUNK) // CAP)


def back_kernel(owners, vp, mp, got, cells, rc, pk, m_1, m_2, inc, ra, pa):
    slots = cells.shape[1]
    x = stacked(unpack_payload(got, owners, slots))
    inc[...] = x
    rims = folded(dot_nt(x, chosen(cells[...], rim_ids(slots))))
    v0, v1, v30, v31, pv = (rims[:, LANES * k : LANES * (k + 1)] for k in range(5))
    pc = pk[vp : 2 * vp, :]
    pp = rim_pack(pv, pc)
    east, west = pack_messages(pv, pc, pp)
    write_pair("lon", m_1, m_2, (west,), (east,), mp)
    write_parts(ra, (v0, v31, *rim_rows(v0, v1, v30, v31, *parts_of(rc, vp))), vp)
    write_parts(pa, (pv, pp), vp)


def back_ghosts(vp, mp, lon, lon_back):
    west, east = read_pair("lon", *lon, mp, vp)
    _, gc, _ = ghost_pack(west[0], east[0])
    west, east = read_pair("lon", *lon_back, mp, vp)
    gv, _, gp = ghost_pack(west[0], east[0])
    return gv, gc, gp


def lat_kernel(vals, vp, mp, h_1, h_2, b_1, b_2, pk, ra, pa, m_1, m_2):
    ghosts = back_ghosts(vp, mp, (h_1, h_2), (b_1, b_2))
    pv, pp = parts_of(pa, vp)
    v0, v31, p0, p31 = parts_of(ra, vp)
    _, f = pack_correction(pv, pp, pk[vp : 2 * vp, :], *ghosts)
    lane = lane_of(f)
    ends = (lane == 0) | (lane == LANES - 1)
    t = tall(ghosts[0], 2 * LANES).T

    def part(x, k):
        return tall(jnp.concatenate([x[:vals], t[k : k + 1, :LANES], t[k : k + 1, LANES:]], axis=0), mp)

    north = part(v0, 2), part(p0 + jnp.where(ends, roll(f, -2), 0.0), 1)
    south = part(v31, LANES - 2), part(p31 + jnp.where(ends, roll(f, 2), 0.0), LANES - 3)
    write_pair("lat", m_1, m_2, north, south, mp)


def lat_corners(vals, vp, north, south):
    row = lax.broadcasted_iota(jnp.int32, (LANES, 2 * LANES), 0)
    t = jnp.zeros((LANES, 2 * LANES), F32)
    for k, x in ((2, north[0]), (1, north[1]), (LANES - 2, south[0]), (LANES - 3, south[1])):
        t = jnp.where(row == k, jnp.concatenate([x[vals : vals + 1], x[vals + 1 : vals + 2]], axis=1), t)
    return t.T[:vp]


def adjoint_kernel(vp, inc, cells, east, west, south, out, adj):
    wide = 2 * LANES
    slots = cells.shape[1]
    for k in range(ROWS // 2):
        ids = lax.broadcasted_iota(jnp.int32, (wide, slots), 0) + k * wide
        x = folded(dot_nt(inc[...], chosen(cells[...], ids)))
        for j in range(2):
            adj[2 * k + j] = x[:, LANES * j : LANES * (j + 1)]

    def keep(i, y):
        out[i] = y

    sweep(adj, (east, west, south), keep)


def second_kernel(vals, vp, mp, mid, east, west, south, field, h_1, h_2, b_1, b_2, pk, pa, out, part, buf, sems):
    pv, pp = parts_of(pa, vp)
    fix, _ = pack_correction(pv, pp, pk[vp : 2 * vp, :], *back_ghosts(vp, mp, (h_1, h_2), (b_1, b_2)))
    lane = lane_of(fix)
    outer = (lane < 2) | (lane >= LANES - 2)
    copies = []

    def add(i, y):
        x = y + field[i]
        if i in ENDS:
            part[ENDS.index(i)] = x
            return
        buf[i] = x + jnp.where(outer, roll(fix, -(4 * i + 2)), 0.0)
        copies.append(pltpu.make_async_copy(buf.at[i, pl.ds(0, vals)], out.at[:, i], sems.at[i]))
        copies[-1].start()

    sweep(mid, (east, west, south), add)
    for c in copies:
        c.wait()


def final_kernel(vals, vp, mp, most, g_1, g_2, h_1, h_2, a_1, a_2, b_1, b_2, ra, rc, pk, pa, part, out, buf, sems):
    gn, gs, _, (_, kc) = read_ghosts(vp, mp, (g_1, g_2), (h_1, h_2))
    an, az = read_pair("lat", a_1, a_2, mp, vp)
    beside = back_ghosts(vp, mp, (h_1, h_2), (b_1, b_2))
    ghosts = (an[0], gn[1], an[1]), (az[0], gs[1], az[1]), beside, (lat_corners(vals, vp, an, az), kc)
    v0, v31, p0, p31 = parts_of(ra, vp)
    pv, pp = parts_of(pa, vp)
    coef = parts_of(rc, vp) + [pk[vp : 2 * vp, :]]
    *rows, fix = rim_correction((v0, v31, p0, p31, pv, pp), coef, ghosts, complete=True)
    lane = lane_of(fix)
    outer = (lane < 2) | (lane >= LANES - 2)
    copies = []
    for k, i in enumerate(ENDS):
        buf[k] = part[k] + rows[k] + jnp.where(outer, roll(fix, -(4 * i + 2)), 0.0)
        copies.append(pltpu.make_async_copy(buf.at[k, pl.ds(0, vals)], out.at[:, i], sems.at[k]))
        copies[-1].start()
    for c in copies:
        c.wait()


def swap(axis, x, first):
    n = lax.axis_size(axis)
    pairs = []
    for i in range(n):
        j = i + 1 if (i % 2 == 0) == first else i - 1
        if axis == "lon":
            j %= n
        if 0 <= j < n:
            pairs.append((i, j))
    return lax.ppermute(x, axis, pairs)


def exchange(axis, m_1, m_2):
    g_2 = swap(axis, m_2, False)
    g_1 = swap(axis, m_1, True)
    return g_1, g_2


def across(x):
    flat = x.reshape(lax.axis_size(("lon", "lat")), 1, SENT * LANES)
    return lax.all_to_all(flat, ("lon", "lat"), split_axis=0, concat_axis=0, tiled=True).reshape(x.shape)


def on_device(state, diffusivity, sea_mask, send_cols, obs_slots, obs_weights, obs_precision):
    vals, taps, obs = state.shape[0], obs_slots.shape[0], obs_slots.shape[1]
    owners = send_cols.shape[1] // CAP
    vp, mp = up(vals, ROWS), up(vals + 2, 8)
    slots = owners * CAP
    cell_count = ROWS * LANES
    cells = send_cols
    blocks = ((owners * SENT, LANES), F32)
    lines = lambda n, rows, dtype=F32: ((n * rows, LANES), dtype)
    field = ((ROWS, vp, LANES), F32)

    def loads(n):
        block = (n, vp, LANES)
        return [pltpu.VMEM(block, F32), pltpu.VMEM(block, F32), pltpu.VMEM(block, jnp.int32), pltpu.SemaphoreType.DMA((4 * n,))]

    *lat_out, rv, rc, done = call(
        functools.partial(rows_kernel, vals, vp, mp),
        [lines(3, mp), lines(3, mp), lines(4, vp), lines(4, vp), lines(1, 8)],
        state, diffusivity, sea_mask,
        in_specs=[HBM] * 3,
        scratch=loads(len(ENDS)),
        vmem=62,
    )
    lat_in = exchange("lat", *lat_out)
    wide = obs if slots <= 1024 else 512
    obs_weights, done = lax.optimization_barrier((obs_weights, done))
    w_hi, w_lo = pl.pallas_call(
        weights_kernel,
        grid=(obs // wide,),
        out_shape=[jax.ShapeDtypeStruct((slots, obs), BF16)] * 2,
        in_specs=[pl.BlockSpec((taps, wide), lambda j: (0, j))] * 2,
        out_specs=[pl.BlockSpec((slots, wide), lambda j: (0, j))] * 2,
        compiler_params=pltpu.CompilerParams(vmem_limit_bytes=20 * MIB),
        cost_estimate=pl.CostEstimate(flops=int(4e9), bytes_accessed=int(80e6), transcendentals=0),
    )(obs_slots, obs_weights)
    whole, split, east, west, south, pk = call(
        functools.partial(sweeps_kernel, vals, vp),
        [field, ((2 * vp, cell_count), BF16), field, field, field, lines(3, vp)],
        state, diffusivity, sea_mask, w_hi,
        in_specs=[VMEM] * 3 + [HBM],
        scratch=[pltpu.VMEM((ROWS, vp, LANES), F32)] * 2,
        vmem=24,
        us=8,
    )
    lon_out = call(
        functools.partial(lon_kernel, vp, mp),
        [lines(1, mp)] * 2, *lat_in, pk,
        vmem=8,
    )
    lon_in = exchange("lon", *lon_out)
    (inner,) = call(
        select_kernel,
        [((vp, slots), F32)],
        split, cells,
        scratch=[pltpu.VMEM((cell_count, CHUNK), BF16)],
        vmem=24,
        us=3,
    )
    (payload,) = call(
        functools.partial(send_kernel, owners, vp, mp),
        [blocks],
        *lat_in, *lon_in, rv, rc, pk, inner, cells,
        vmem=24,
    )
    payload, w_hi, w_lo = lax.optimization_barrier((payload, w_hi, w_lo))
    received = across(payload)
    matrix = 4 * slots * obs // MIB
    equivalents, payload = call(
        functools.partial(owner_kernel, vals, vp, owners),
        [((vals, obs), F32), blocks],
        received, w_hi, w_lo, obs_precision,
        scratch=[pltpu.VMEM((2 * vp, slots), BF16), pltpu.VMEM((2 * vp, obs), BF16)],
        vmem=20 + matrix,
    )
    incoming = across(payload)
    *lon_out, inc, ra, pa = call(
        functools.partial(back_kernel, owners, vp, mp),
        [lines(1, mp)] * 2 + [((2 * vp, slots), BF16), lines(4, vp), lines(2, vp)],
        incoming, cells, rc, pk,
        vmem=24,
    )
    lon_back = exchange("lon", *lon_out)
    (mid,) = call(
        functools.partial(adjoint_kernel, vp),
        [field],
        inc, cells, east, west, south,
        scratch=[pltpu.VMEM((ROWS, vp, LANES), F32)],
        vmem=24,
        us=4,
    )
    lon_back, mid = lax.optimization_barrier((lon_back, mid))
    lat_out = call(
        functools.partial(lat_kernel, vals, vp, mp),
        [lines(2, mp)] * 2, *lon_in, *lon_back, pk, ra, pa,
        vmem=8,
    )
    lat_back = exchange("lat", *lat_out)
    most, part = call(
        functools.partial(second_kernel, vals, vp, mp),
        [(state.shape, F32), ((len(ENDS), vp, LANES), F32)],
        mid, east, west, south, whole, *lon_in, *lon_back, pk, pa,
        scratch=[pltpu.VMEM((ROWS, vp, LANES), F32), pltpu.SemaphoreType.DMA((ROWS,))],
        out_specs=[HBM, VMEM],
        vmem=20,
        us=4,
    )
    (product,) = call(
        functools.partial(final_kernel, vals, vp, mp),
        [(state.shape, F32)],
        most, *lat_in, *lon_in, *lat_back, *lon_back, ra, rc, pk, pa, part,
        in_specs=[HBM] + [VMEM] * 13,
        scratch=[pltpu.VMEM((len(ENDS), vp, LANES), F32), pltpu.SemaphoreType.DMA((len(ENDS),))],
        out_specs=[HBM],
        input_output_aliases={0: 0},
        vmem=16,
    )
    return product, equivalents


def solution(mesh):
    placed = (
        P(None, "lat", "lon"),
        P(None, "lat", "lon"),
        P(None, "lat", "lon"),
        P(("lon", "lat"), None),
        P(None, ("lon", "lat")),
        P(None, ("lon", "lat")),
        P(None, ("lon", "lat")),
    )
    return jax.shard_map(
        on_device,
        mesh=mesh,
        in_specs=placed,
        out_specs=(P(None, "lat", "lon"), P(None, ("lon", "lat"))),
        check_vma=False,
    )
```

```python
import functools

import jax
import jax.numpy as jnp
from jax import lax
from jax.experimental import pallas as pl
from jax.experimental.pallas import tpu as pltpu
from jax.sharding import PartitionSpec as P

CAP = 24
LANES = 128
GROUPS = 5
CHUNK = 32 * CAP
ROWS = 32
SENT = 30
OBS_BLOCK = 256
F32, BF16 = jnp.float32, jnp.bfloat16
MIB = 1 << 20


def up(n, k):
    return -(-n // k) * k


def roll(x, k):
    k %= LANES
    return x if k == 0 else pltpu.roll(x, k, axis=1)


def lane_of(x):
    return lax.broadcasted_iota(jnp.int32, x.shape, 1)


def tall(x, rows):
    if x.shape[0] == rows:
        return x
    return jnp.concatenate([x, jnp.zeros((rows - x.shape[0], x.shape[1]), x.dtype)], axis=0)


def halves(x):
    hi = x.astype(BF16)
    return hi, (x - hi.astype(F32)).astype(BF16)


def dot(a, b):
    return lax.dot_general(a, b, (((1,), (0,)), ((), ())), preferred_element_type=F32)


def dot_nt(a, b):
    return lax.dot_general(a, b, (((1,), (1,)), ((), ())), preferred_element_type=F32)


def stacked(x):
    return jnp.concatenate(halves(x), axis=0)


def folded(x):
    n = x.shape[0] // 2
    return x[:n] + x[n:]


def row_edges(c):
    east = jnp.where(lane_of(c) == LANES - 1, 0.0, jnp.minimum(c, roll(c, -1)))
    return east, roll(east, 1)


def pack_edges(cp):
    lane = lane_of(cp)
    kind = lane & 3
    inner = jnp.where(kind == 1, roll(cp, 1), roll(cp, -1))
    inner = jnp.where((kind == 1) | (kind == 2), jnp.minimum(cp, inner), 0.0)
    south = jnp.where(lane >= LANES - 4, 0.0, jnp.minimum(cp, roll(cp, -4)))
    return kind, inner, south, roll(south, 4)


def rim_rows(v0, v1, v30, v31, c0, c1, c30, c31):
    out = []
    for v, w, c, d in ((v0, v1, c0, c1), (v31, v30, c31, c30)):
        east, west = row_edges(c)
        out.append(v + east * (roll(v, -1) - v) + west * (roll(v, 1) - v) + jnp.minimum(c, d) * (w - v))
    return out


def rim_pack(vp, cp):
    kind, inner, south, north = pack_edges(cp)
    beside = jnp.where(kind == 1, roll(vp, 1), roll(vp, -1))
    return vp + inner * (beside - vp) + south * (roll(vp, -4) - vp) + north * (roll(vp, 4) - vp)


def pack_messages(vp, cp, pp, north=(), south=()):
    lane = lane_of(vp)
    kind = lane & 3
    east = jnp.where(kind == 0, roll(vp, -1), jnp.where(kind == 1, cp, roll(pp, 1)))
    west = jnp.where(kind == 0, roll(vp, -2), jnp.where(kind == 1, roll(cp, -1), pp))
    for k, x in zip((3, 7, 11, 15), (*north, *south)):
        east = jnp.where(lane == k, roll(x, k + 1), east)
        west = jnp.where(lane == k, roll(x, k), west)
    return east, west


def ghost_pack(from_w, from_e):
    one = (lane_of(from_w) & 3) == 1
    v = jnp.where(one, roll(from_e, 1), roll(from_w, 2))
    c = jnp.where(one, from_e, roll(from_w, 1))
    p = jnp.where(one, roll(from_e, -1), from_w)
    return v, c, p


def corner_pack(from_w, from_e):
    lane = lane_of(from_w)
    out = []
    for n, s in ((3, 11), (7, 15)):
        x = jnp.zeros_like(from_w)
        for at, src, k in ((1, from_e, n), (2, from_w, n), (LANES - 3, from_e, s), (LANES - 2, from_w, s)):
            x = jnp.where(lane == at, roll(src, at - k), x)
        out.append(x)
    return out


def pack_correction(vp, pp, cp, gv, gc, gp, more_ghost=0.0, more_whole=0.0):
    kind, inner, south, north = pack_edges(cp)
    mid = (kind == 1) | (kind == 2)
    mg = jnp.where(mid, jnp.minimum(cp, gc), 0.0)
    f = mg * (gv - vp)
    qf = inner * f
    again = mg * (gp - f + more_ghost - (pp + f + more_whole))
    rp = f - qf + south * (roll(f, -4) - f) + north * (roll(f, 4) - f) + again
    return jnp.where(mid, rp, jnp.where(kind == 0, roll(qf, -1), roll(qf, 1))), f


def rim_correction(own, coef, ghosts, complete=False):
    v0, v31, p0, p31, vp, pp = own
    c0, c1, c30, c31, cp = coef
    (gvn, gcn, gpn), (gvs, gcs, gps), (gv, gc, gp), (kv, kc) = ghosts
    lane = lane_of(v0)
    ends = (lane == 0) | (lane == LANES - 1)
    mn, ms = jnp.minimum(c0, gcn), jnp.minimum(c31, gcs)
    fn, fs = mn * (gvn - v0), ms * (gvs - v31)
    more_ghost = jnp.where(((lane & 3) == 1) | ((lane & 3) == 2), jnp.minimum(gc, kc), 0.0) * (kv - gv)
    more_whole = jnp.where((lane == 1) | (lane == 2), roll(fn, 2), 0.0)
    more_whole = more_whole + jnp.where((lane == LANES - 3) | (lane == LANES - 2), roll(fs, -2), 0.0)
    rp, f = pack_correction(vp, pp, cp, gv, gc, gp, more_ghost, more_whole)
    ghost_n, ghost_s = gpn - fn, gps - fs
    if not complete:
        ghost_n = ghost_n + jnp.where(ends, jnp.minimum(gcn, roll(kc, -2)), 0.0) * (roll(kv, -2) - gvn)
        ghost_s = ghost_s + jnp.where(ends, jnp.minimum(gcs, roll(kc, 2)), 0.0) * (roll(kv, 2) - gvs)
    whole_n = p0 + fn + jnp.where(ends, roll(f, -2), 0.0)
    whole_s = p31 + fs + jnp.where(ends, roll(f, 2), 0.0)
    rows = []
    for c, d, m, g, w, x in ((c0, c1, mn, ghost_n, whole_n, fn), (c31, c30, ms, ghost_s, whole_s, fs)):
        east, west = row_edges(c)
        across = jnp.minimum(c, d)
        rows.append(x + east * (roll(x, -1) - x) + west * (roll(x, 1) - x) - across * x + m * (g - w))
        rows.append(across * x)
    return rows[0], rows[1], rows[3], rows[2], rp


def sweep(src, edges, emit):
    east, west, south = edges
    for i in range(ROWS):
        x = src[i]
        y = x + east[i] * (roll(x, -1) - x) + west[i] * (roll(x, 1) - x)
        if i < ROWS - 1:
            y = y + south[i] * (src[i + 1] - x)
        if i > 0:
            y = y + south[i - 1] * (src[i - 1] - x)
        emit(i, y)


def chosen(cells, ids):
    return jnp.where(ids == cells, 1.0, 0.0).astype(BF16)


def rim_ids(n):
    line = lax.broadcasted_iota(jnp.int32, (LANES, n), 0)
    rows = [line + i * LANES for i in (0, 1, ROWS - 2, ROWS - 1)]
    k = line & 3
    pack = (line >> 2) * LANES + jnp.where(k < 2, LANES - 2 + k, k - 2)
    return jnp.concatenate(rows + [pack], axis=0)


def spans(o):
    a, lane = divmod(CAP * o, LANES)
    if lane + CAP <= LANES:
        return [(a, lane, 0, CAP)]
    return [(a, lane, 0, LANES - lane), (a + 1, lane - LANES, LANES - lane, CAP)]


def merged(old, new, lo, hi):
    if old is None:
        return new
    lane = lane_of(new)
    return jnp.where((lane >= lo) & (lane < hi), new, old)


def by_shift(pairs, a):
    out = {}
    for o in pairs:
        for tile, at, p, q in spans(o):
            if tile == a:
                for g in range(GROUPS):
                    out.setdefault(g - o, []).append((o, g, at + p, CAP * g + p, q - p))
    return out


def pack_payload(columns, out_ref, first, last):
    tail = ROWS - 2 * (GROUPS - 1) - 2
    pairs = range(last - first)
    blocks = [None for _ in pairs]
    for a in range(spans(pairs[-1])[-1][0] + 1):
        if a % 2 == 0:
            both = columns(a // 2)
        x = both[:, LANES * (a % 2) : LANES * (a % 2 + 1)]
        rest = [x[ROWS * g + SENT : ROWS * (g + 1)] for g in range(GROUPS - 1)]
        groups = [x[ROWS * g : ROWS * (g + 1)] for g in range(GROUPS - 1)]
        groups.append(jnp.concatenate([x[ROWS * (GROUPS - 1) :][:tail], *rest, jnp.zeros((2, LANES), F32)], axis=0))
        for d, moves in by_shift(pairs, a).items():
            z = None
            for o, g, src, dst, n in moves:
                z = merged(z, groups[g], src, src + n)
            z = roll(z, CAP * d)
            for o, g, src, dst, n in moves:
                blocks[o] = merged(blocks[o], z, dst, dst + n)
        for o in pairs:
            if spans(o)[-1][0] == a:
                at = SENT * (first + o)
                out_ref[at : at + SENT, :] = blocks[o][:SENT]


def unpack_payload(in_ref, owners, slots):
    pairs = range(owners)
    blocks = [in_ref[SENT * o : SENT * o + ROWS, :] if o < owners - 1 else tall(in_ref[SENT * o :, :], ROWS) for o in pairs]
    pieces = [[None for _ in range(slots // LANES)] for _ in range(GROUPS)]
    for a in range(slots // LANES):
        for d, moves in by_shift(pairs, a).items():
            z = None
            for o, g, dst, src, n in moves:
                z = merged(z, blocks[o], src, src + n)
            z = roll(z, -CAP * d)
            for o, g, dst, src, n in moves:
                pieces[g][a] = merged(pieces[g][a], z, dst, dst + n)
    groups = [jnp.concatenate(x, axis=1) for x in pieces]
    tail = ROWS - 2 * (GROUPS - 1) - 2
    out = []
    for g in range(GROUPS - 1):
        out += [groups[g][:SENT], groups[-1][tail + 2 * g : tail + 2 * (g + 1)]]
    out += [groups[-1][:tail], jnp.zeros((ROWS - tail, slots), F32)]
    return jnp.concatenate(out, axis=0)


def takes(us):
    return pl.CostEstimate(flops=MIB, bytes_accessed=int(us * 3.3e6), transcendentals=0)


def call(kernel, outs, *args, in_specs=None, scratch=(), vmem=48, us=1, **kw):
    any_spec = pl.BlockSpec(memory_space=pltpu.VMEM)
    return pl.pallas_call(
        kernel,
        out_shape=[jax.ShapeDtypeStruct(s, d) for s, d in outs],
        in_specs=in_specs or [any_spec] * len(args),
        scratch_shapes=list(scratch),
        compiler_params=pltpu.CompilerParams(vmem_limit_bytes=vmem * MIB),
        cost_estimate=takes(us),
        **kw,
    )(*args)


HBM = pl.BlockSpec(memory_space=pl.ANY)
VMEM = pl.BlockSpec(memory_space=pltpu.VMEM)


def even(axis):
    return lax.rem(lax.axis_index(axis), 2) == 0


def write_parts(ref, parts, rows):
    for k, x in enumerate(parts):
        ref[rows * k : rows * (k + 1), :] = x[:rows]


def parts_of(ref, rows, vp=None):
    out = [ref[rows * k : rows * (k + 1), :] for k in range(ref.shape[0] // rows)]
    return out if vp is None else [tall(x, vp) for x in out]


def write_pair(axis, first, second, up_parts, down_parts, rows):
    for ref, e, o in ((first, down_parts, up_parts), (second, up_parts, down_parts)):
        write_parts(ref, [jnp.where(even(axis), x, y) for x, y in zip(e, o)], rows)


def read_pair(axis, first, second, rows, vp):
    f, s = parts_of(first, rows, vp), parts_of(second, rows, vp)
    before = [jnp.where(even(axis), y, x) for x, y in zip(f, s)]
    after = [jnp.where(even(axis), x, y) for x, y in zip(f, s)]
    return before, after


ENDS = (0, 1, ROWS - 2, ROWS - 1)


def mask_of(mask, vals, v, rows):
    half, end = vals // 2, min(v + 8, vals)
    if end <= half:
        return mask[v:end, rows, :]
    if v >= half:
        return mask[v - half : end - half, rows, :]
    return jnp.concatenate([mask[v:half, rows, :], mask[: end - half, rows, :]], axis=0)


def eight(x):
    n = x.shape[0]
    return x if n == 8 else jnp.concatenate([x, jnp.zeros((8 - n, *x.shape[1:]), x.dtype)], axis=0)


def rows_kernel(vals, vp, mp, state, diff, mask, m_1, m_2, rv, rc, done, sv, sd, sm, sems):
    done[...] = jnp.zeros(done.shape, F32)
    copies = []
    for src, dst, n in ((state, sv, vals), (diff, sd, vals), (mask, sm, vals // 2)):
        for k, i in enumerate((0, ROWS - 2)):
            at = dst.at[pl.ds(0, n), pl.ds(2 * k, 2)]
            copies.append(pltpu.make_async_copy(src.at[:, pl.ds(i, 2)], at, sems.at[len(copies)]))
            copies[-1].start()
    for c in copies:
        c.wait()
    v_tiles, c_tiles = [], []
    for v in range(0, vals, 8):
        end = min(v + 8, vals)
        c = sd[v:end] * mask_of(sm, vals, v, slice(0, 8)).astype(F32)
        for tiles, x in ((v_tiles, sv[v:end]), (c_tiles, c)):
            y = jnp.swapaxes(eight(x), 0, 1)
            tiles.append([y[k] for k in range(4)])
    v0, v1, v30, v31 = (tall(jnp.concatenate([t[k] for t in v_tiles], axis=0), vp) for k in range(4))
    c0, c1, c30, c31 = (tall(jnp.concatenate([t[k] for t in c_tiles], axis=0), vp) for k in range(4))
    p0, p31 = rim_rows(v0, v1, v30, v31, c0, c1, c30, c31)
    write_pair("lat", m_1, m_2, (v0, c0, p0), (v31, c31, p31), mp)
    write_parts(rv, (v0, v31, p0, p31), vp)
    write_parts(rc, (c0, c1, c30, c31), vp)


def by_grid_row(x, dst, first):
    y = jnp.swapaxes(eight(x), 0, 1)
    v, i = first
    for k in range(8):
        dst[i + k, v : v + 8, :] = y[k]


def outer_columns(ref):
    total = jnp.zeros((2 * ref.shape[1], LANES), F32)
    r = lax.broadcasted_iota(jnp.int32, (2 * LANES, LANES), 0)
    lane = lax.broadcasted_iota(jnp.int32, (2 * LANES, LANES), 1)
    source = (lane >> 2) * LANES + jnp.where((lane & 3) < 2, LANES - 2 + (lane & 3), (lane & 3) - 2)
    for i in range(0, ROWS, 2):
        take = jnp.where(r == source - i * LANES, 1.0, 0.0).astype(BF16)
        total = total + dot(stacked(jnp.concatenate([ref[i], ref[i + 1]], axis=1)), take)
    return folded(total)


def sweeps_kernel(vals, vp, state, diff, mask, after, field, out, east, west, south, pk, coef, mid):
    half = vals // 2
    for v in range(0, vp, 8):
        if v >= vals:
            for ref in (field, coef):
                ref[:, v : v + 8, :] = jnp.zeros((ROWS, 8, LANES), F32)
            continue
        end = min(v + 8, vals)
        for i in range(0, ROWS, 8):
            rows = slice(i, i + 8)
            m = mask_of(mask, vals, v, rows)
            by_grid_row(state[v:end, rows, :], field, (v, i))
            by_grid_row(diff[v:end, rows, :] * m.astype(F32), coef, (v, i))
    lane = lax.broadcasted_iota(jnp.int32, (vp, LANES), 1)
    c = coef[0]
    for i in range(ROWS):
        if i < ROWS - 1:
            cn = coef[i + 1]
            south[i] = jnp.minimum(c, cn)
        else:
            south[i] = jnp.zeros_like(c)
        e = jnp.where(lane == LANES - 1, 0.0, jnp.minimum(c, roll(c, -1)))
        w = roll(e, 1)
        east[i], west[i] = e, w
        x = field[i]
        y = x + e * (roll(x, -1) - x) + w * (roll(x, 1) - x)
        if i < ROWS - 1:
            y = y + south[i] * (field[i + 1] - x)
        if i > 0:
            y = y + south[i - 1] * (field[i - 1] - x)
        mid[i] = y
        c = cn
    pv, pc = outer_columns(field), outer_columns(coef)
    write_parts(pk, (pv, pc, rim_pack(pv, pc)), vp)
    edges = (east, west, south)

    def split(i, y):
        out[:, LANES * i : LANES * (i + 1)] = stacked(y)

    sweep(mid, edges, split)


def lon_kernel(vp, mp, g_1, g_2, pk, m_1, m_2):
    north, south = read_pair("lat", g_1, g_2, mp, vp)
    east, west = pack_messages(*parts_of(pk, vp), north[:2], south[:2])
    write_pair("lon", m_1, m_2, (west,), (east,), mp)


def select_kernel(smooth, cells, out, hot):
    chunk = hot.shape[1]
    wide = 4 * LANES
    for base in range(0, cells.shape[1], chunk):
        for k in range(0, ROWS * LANES, wide):
            ids = lax.broadcasted_iota(jnp.int32, (wide, chunk), 0) + k
            hot[k : k + wide, :] = chosen(cells[:, base : base + chunk], ids)
        total = jnp.zeros((smooth.shape[0], chunk), F32)
        for k in range(0, ROWS * LANES, wide):
            total = total + dot(smooth[:, k : k + wide], hot[k : k + wide, :])
        out[:, base : base + chunk] = folded(total)


def weights_kernel(slots, weights, hi, lo):
    taps = range(slots.shape[0])
    at = [slots[k : k + 1, :] for k in taps]
    w = [weights[k : k + 1, :] for k in taps]
    for a in taps:
        for b in range(a + 1, len(taps)):
            same = at[a] == at[b]
            w[a] = w[a] + jnp.where(same, w[b], 0.0)
            at[b] = jnp.where(same, -1, at[b])
    at = [x.astype(jnp.int16) for x in at]
    parts = [halves(x) for x in w]
    shape = (LANES, hi.shape[1])
    for r in range(0, hi.shape[0], LANES):
        row = (lax.broadcasted_iota(jnp.int32, shape, 0) + r).astype(jnp.int16)
        h = l = jnp.zeros(shape, BF16)
        for k in taps:
            here = row == at[k]
            h, l = jnp.where(here, parts[k][0], h), jnp.where(here, parts[k][1], l)
        hi[r : r + LANES, :] = h
        lo[r : r + LANES, :] = l


def read_ghosts(vp, mp, lat, lon):
    north, south = read_pair("lat", *lat, mp, vp)
    west, east = read_pair("lon", *lon, mp, vp)
    return north, south, ghost_pack(west[0], east[0]), corner_pack(west[0], east[0])


def send_kernel(owners, vp, mp, g_1, g_2, h_1, h_2, rv, rc, pk, inner, cells, out):
    ghosts = read_ghosts(vp, mp, (g_1, g_2), (h_1, h_2))
    v0, v31, p0, p31 = parts_of(rv, vp)
    pv, pc, pp = parts_of(pk, vp)
    fix = rim_correction((v0, v31, p0, p31, pv, pp), parts_of(rc, vp) + [pc], ghosts)
    wide = 2 * LANES
    fix = stacked(jnp.concatenate(fix, axis=1))
    ids = rim_ids(wide)

    def columns(k):
        at = slice(wide * k, wide * (k + 1))
        return inner[:, at] + folded(dot(fix, chosen(cells[:, at], ids)))

    pack_payload(columns, out, 0, owners)


def owner_kernel(vals, vp, owners, got, w_hi, w_lo, prec, equiv, back, r2, w2):
    r2[...] = stacked(unpack_payload(got, owners, r2.shape[1]))
    wide = min(512, equiv.shape[1])
    for q in range(0, equiv.shape[1], wide):
        at = slice(q, q + wide)
        e = (folded(dot(r2[...], w_hi[:, at])) + dot(r2[:vp, :], w_lo[:, at]))[:vals]
        equiv[:, at] = e
        w2[:, at] = stacked(tall(prec[:, at] * e, vp))
    for o in range(0, r2.shape[1], CHUNK):

        def columns(k):
            at = slice(o + 2 * LANES * k, o + 2 * LANES * (k + 1))
            return folded(dot_nt(w2[...], w_hi[at, :])) + dot_nt(w2[:vp, :], w_lo[at, :])

        pack_payload(columns, back, o // CAP, (o + CHUNK) // CAP)


def back_kernel(owners, vp, mp, got, cells, rc, pk, m_1, m_2, inc, ra, pa):
    slots = cells.shape[1]
    x = stacked(unpack_payload(got, owners, slots))
    inc[...] = x
    rims = folded(dot_nt(x, chosen(cells[...], rim_ids(slots))))
    v0, v1, v30, v31, pv = (rims[:, LANES * k : LANES * (k + 1)] for k in range(5))
    pc = pk[vp : 2 * vp, :]
    pp = rim_pack(pv, pc)
    east, west = pack_messages(pv, pc, pp)
    write_pair("lon", m_1, m_2, (west,), (east,), mp)
    write_parts(ra, (v0, v31, *rim_rows(v0, v1, v30, v31, *parts_of(rc, vp))), vp)
    write_parts(pa, (pv, pp), vp)


def back_ghosts(vp, mp, lon, lon_back):
    west, east = read_pair("lon", *lon, mp, vp)
    _, gc, _ = ghost_pack(west[0], east[0])
    west, east = read_pair("lon", *lon_back, mp, vp)
    gv, _, gp = ghost_pack(west[0], east[0])
    return gv, gc, gp


def lat_kernel(vals, vp, mp, h_1, h_2, b_1, b_2, pk, ra, pa, m_1, m_2):
    ghosts = back_ghosts(vp, mp, (h_1, h_2), (b_1, b_2))
    pv, pp = parts_of(pa, vp)
    v0, v31, p0, p31 = parts_of(ra, vp)
    _, f = pack_correction(pv, pp, pk[vp : 2 * vp, :], *ghosts)
    lane = lane_of(f)
    ends = (lane == 0) | (lane == LANES - 1)
    t = tall(ghosts[0], 2 * LANES).T

    def part(x, k):
        return tall(jnp.concatenate([x[:vals], t[k : k + 1, :LANES], t[k : k + 1, LANES:]], axis=0), mp)

    north = part(v0, 2), part(p0 + jnp.where(ends, roll(f, -2), 0.0), 1)
    south = part(v31, LANES - 2), part(p31 + jnp.where(ends, roll(f, 2), 0.0), LANES - 3)
    write_pair("lat", m_1, m_2, north, south, mp)


def lat_corners(vals, vp, north, south):
    row = lax.broadcasted_iota(jnp.int32, (LANES, 2 * LANES), 0)
    t = jnp.zeros((LANES, 2 * LANES), F32)
    for k, x in ((2, north[0]), (1, north[1]), (LANES - 2, south[0]), (LANES - 3, south[1])):
        t = jnp.where(row == k, jnp.concatenate([x[vals : vals + 1], x[vals + 1 : vals + 2]], axis=1), t)
    return t.T[:vp]


def adjoint_kernel(vp, inc, cells, east, west, south, out, adj):
    wide = 2 * LANES
    slots = cells.shape[1]
    for k in range(ROWS // 2):
        ids = lax.broadcasted_iota(jnp.int32, (wide, slots), 0) + k * wide
        x = folded(dot_nt(inc[...], chosen(cells[...], ids)))
        for j in range(2):
            adj[2 * k + j] = x[:, LANES * j : LANES * (j + 1)]

    def keep(i, y):
        out[i] = y

    sweep(adj, (east, west, south), keep)


def second_kernel(vals, vp, mp, mid, east, west, south, field, h_1, h_2, b_1, b_2, pk, pa, out, part, buf, sems):
    pv, pp = parts_of(pa, vp)
    fix, _ = pack_correction(pv, pp, pk[vp : 2 * vp, :], *back_ghosts(vp, mp, (h_1, h_2), (b_1, b_2)))
    lane = lane_of(fix)
    outer = (lane < 2) | (lane >= LANES - 2)
    copies = []

    def add(i, y):
        x = y + field[i]
        if i in ENDS:
            part[ENDS.index(i)] = x
            return
        buf[i] = x + jnp.where(outer, roll(fix, -(4 * i + 2)), 0.0)
        copies.append(pltpu.make_async_copy(buf.at[i, pl.ds(0, vals)], out.at[:, i], sems.at[i]))
        copies[-1].start()

    sweep(mid, (east, west, south), add)
    for c in copies:
        c.wait()


def final_kernel(vals, vp, mp, most, g_1, g_2, h_1, h_2, a_1, a_2, b_1, b_2, ra, rc, pk, pa, part, out, buf, sems):
    gn, gs, _, (_, kc) = read_ghosts(vp, mp, (g_1, g_2), (h_1, h_2))
    an, az = read_pair("lat", a_1, a_2, mp, vp)
    beside = back_ghosts(vp, mp, (h_1, h_2), (b_1, b_2))
    ghosts = (an[0], gn[1], an[1]), (az[0], gs[1], az[1]), beside, (lat_corners(vals, vp, an, az), kc)
    v0, v31, p0, p31 = parts_of(ra, vp)
    pv, pp = parts_of(pa, vp)
    coef = parts_of(rc, vp) + [pk[vp : 2 * vp, :]]
    *rows, fix = rim_correction((v0, v31, p0, p31, pv, pp), coef, ghosts, complete=True)
    lane = lane_of(fix)
    outer = (lane < 2) | (lane >= LANES - 2)
    copies = []
    for k, i in enumerate(ENDS):
        buf[k] = part[k] + rows[k] + jnp.where(outer, roll(fix, -(4 * i + 2)), 0.0)
        copies.append(pltpu.make_async_copy(buf.at[k, pl.ds(0, vals)], out.at[:, i], sems.at[k]))
        copies[-1].start()
    for c in copies:
        c.wait()


def swap(axis, x, first):
    n = lax.axis_size(axis)
    pairs = []
    for i in range(n):
        j = i + 1 if (i % 2 == 0) == first else i - 1
        if axis == "lon":
            j %= n
        if 0 <= j < n:
            pairs.append((i, j))
    return lax.ppermute(x, axis, pairs)


def exchange(axis, m_1, m_2):
    g_2 = swap(axis, m_2, False)
    g_1 = swap(axis, m_1, True)
    return g_1, g_2


def across(x):
    flat = x.reshape(lax.axis_size(("lon", "lat")), 1, SENT * LANES)
    return lax.all_to_all(flat, ("lon", "lat"), split_axis=0, concat_axis=0, tiled=True).reshape(x.shape)


def on_device(state, diffusivity, sea_mask, send_cols, obs_slots, obs_weights, obs_precision):
    vals, taps, obs = state.shape[0], obs_slots.shape[0], obs_slots.shape[1]
    owners = send_cols.shape[1] // CAP
    vp, mp = up(vals, ROWS), up(vals + 2, 8)
    slots = owners * CAP
    cell_count = ROWS * LANES
    cells = send_cols
    blocks = ((owners * SENT, LANES), F32)
    lines = lambda n, rows, dtype=F32: ((n * rows, LANES), dtype)
    field = ((ROWS, vp, LANES), F32)

    *lat_out, rv, rc, done = call(
        functools.partial(rows_kernel, vals, vp, mp),
        [lines(3, mp), lines(3, mp), lines(4, vp), lines(4, vp), lines(1, 8)],
        state, diffusivity, sea_mask,
        in_specs=[HBM] * 3,
        scratch=[pltpu.VMEM((n, 8, LANES), d) for n, d in ((vp, F32), (vp, F32), (vp // 2, jnp.int32))]
        + [pltpu.SemaphoreType.DMA((6,))],
        vmem=62,
    )
    lat_in = exchange("lat", *lat_out)
    wide = obs if slots <= 1024 else 512
    obs_weights, done = lax.optimization_barrier((obs_weights, done))
    w_hi, w_lo = pl.pallas_call(
        weights_kernel,
        grid=(obs // wide,),
        out_shape=[jax.ShapeDtypeStruct((slots, obs), BF16)] * 2,
        in_specs=[pl.BlockSpec((taps, wide), lambda j: (0, j))] * 2,
        out_specs=[pl.BlockSpec((slots, wide), lambda j: (0, j))] * 2,
        compiler_params=pltpu.CompilerParams(vmem_limit_bytes=20 * MIB),
        cost_estimate=pl.CostEstimate(flops=int(4e9), bytes_accessed=int(80e6), transcendentals=0),
    )(obs_slots, obs_weights)
    whole, split, east, west, south, pk = call(
        functools.partial(sweeps_kernel, vals, vp),
        [field, ((2 * vp, cell_count), BF16), field, field, field, lines(3, vp)],
        state, diffusivity, sea_mask, w_hi,
        in_specs=[VMEM] * 3 + [HBM],
        scratch=[pltpu.VMEM((ROWS, vp, LANES), F32)] * 2,
        vmem=24,
        us=8,
    )
    lon_out = call(
        functools.partial(lon_kernel, vp, mp),
        [lines(1, mp)] * 2, *lat_in, pk,
        vmem=8,
    )
    lon_in = exchange("lon", *lon_out)
    (inner,) = call(
        select_kernel,
        [((vp, slots), F32)],
        split, cells,
        scratch=[pltpu.VMEM((cell_count, CHUNK), BF16)],
        vmem=24,
        us=3,
    )
    (payload,) = call(
        functools.partial(send_kernel, owners, vp, mp),
        [blocks],
        *lat_in, *lon_in, rv, rc, pk, inner, cells,
        vmem=24,
    )
    payload, w_hi, w_lo = lax.optimization_barrier((payload, w_hi, w_lo))
    received = across(payload)
    matrix = 4 * slots * obs // MIB
    equivalents, payload = call(
        functools.partial(owner_kernel, vals, vp, owners),
        [((vals, obs), F32), blocks],
        received, w_hi, w_lo, obs_precision,
        scratch=[pltpu.VMEM((2 * vp, slots), BF16), pltpu.VMEM((2 * vp, obs), BF16)],
        vmem=20 + matrix,
    )
    incoming = across(payload)
    *lon_out, inc, ra, pa = call(
        functools.partial(back_kernel, owners, vp, mp),
        [lines(1, mp)] * 2 + [((2 * vp, slots), BF16), lines(4, vp), lines(2, vp)],
        incoming, cells, rc, pk,
        vmem=24,
    )
    lon_back = exchange("lon", *lon_out)
    (mid,) = call(
        functools.partial(adjoint_kernel, vp),
        [field],
        inc, cells, east, west, south,
        scratch=[pltpu.VMEM((ROWS, vp, LANES), F32)],
        vmem=24,
        us=4,
    )
    lon_back, mid = lax.optimization_barrier((lon_back, mid))
    lat_out = call(
        functools.partial(lat_kernel, vals, vp, mp),
        [lines(2, mp)] * 2, *lon_in, *lon_back, pk, ra, pa,
        vmem=8,
    )
    lat_back = exchange("lat", *lat_out)
    most, part = call(
        functools.partial(second_kernel, vals, vp, mp),
        [(state.shape, F32), ((len(ENDS), vp, LANES), F32)],
        mid, east, west, south, whole, *lon_in, *lon_back, pk, pa,
        scratch=[pltpu.VMEM((ROWS, vp, LANES), F32), pltpu.SemaphoreType.DMA((ROWS,))],
        out_specs=[HBM, VMEM],
        vmem=20,
        us=4,
    )
    (product,) = call(
        functools.partial(final_kernel, vals, vp, mp),
        [(state.shape, F32)],
        most, *lat_in, *lon_in, *lat_back, *lon_back, ra, rc, pk, pa, part,
        in_specs=[HBM] + [VMEM] * 13,
        scratch=[pltpu.VMEM((len(ENDS), vp, LANES), F32), pltpu.SemaphoreType.DMA((len(ENDS),))],
        out_specs=[HBM],
        input_output_aliases={0: 0},
        vmem=16,
    )
    return product, equivalents


def solution(mesh):
    placed = (
        P(None, "lat", "lon"),
        P(None, "lat", "lon"),
        P(None, "lat", "lon"),
        P(("lon", "lat"), None),
        P(None, ("lon", "lat")),
        P(None, ("lon", "lat")),
        P(None, ("lon", "lat")),
    )
    return jax.shard_map(
        on_device,
        mesh=mesh,
        in_specs=placed,
        out_specs=(P(None, "lat", "lon"), P(None, ("lon", "lat"))),
        check_vma=False,
    )
```

```python
import functools

import jax
import jax.numpy as jnp
from jax import lax
from jax.experimental import pallas as pl
from jax.experimental.pallas import tpu as pltpu
from jax.sharding import PartitionSpec as P

CAP = 24
LANES = 128
GROUPS = 5
CHUNK = 32 * CAP
ROWS = 32
SENT = 30
OBS_BLOCK = 256
F32, BF16 = jnp.float32, jnp.bfloat16
MIB = 1 << 20


def up(n, k):
    return -(-n // k) * k


def roll(x, k):
    k %= LANES
    return x if k == 0 else pltpu.roll(x, k, axis=1)


def lane_of(x):
    return lax.broadcasted_iota(jnp.int32, x.shape, 1)


def tall(x, rows):
    if x.shape[0] == rows:
        return x
    return jnp.concatenate([x, jnp.zeros((rows - x.shape[0], x.shape[1]), x.dtype)], axis=0)


def halves(x):
    hi = x.astype(BF16)
    return hi, (x - hi.astype(F32)).astype(BF16)


def dot(a, b):
    return lax.dot_general(a, b, (((1,), (0,)), ((), ())), preferred_element_type=F32)


def dot_nt(a, b):
    return lax.dot_general(a, b, (((1,), (1,)), ((), ())), preferred_element_type=F32)


def stacked(x):
    return jnp.concatenate(halves(x), axis=0)


def folded(x):
    n = x.shape[0] // 2
    return x[:n] + x[n:]


def row_edges(c):
    east = jnp.where(lane_of(c) == LANES - 1, 0.0, jnp.minimum(c, roll(c, -1)))
    return east, roll(east, 1)


def pack_edges(cp):
    lane = lane_of(cp)
    kind = lane & 3
    inner = jnp.where(kind == 1, roll(cp, 1), roll(cp, -1))
    inner = jnp.where((kind == 1) | (kind == 2), jnp.minimum(cp, inner), 0.0)
    south = jnp.where(lane >= LANES - 4, 0.0, jnp.minimum(cp, roll(cp, -4)))
    return kind, inner, south, roll(south, 4)


def rim_rows(v0, v1, v30, v31, c0, c1, c30, c31):
    out = []
    for v, w, c, d in ((v0, v1, c0, c1), (v31, v30, c31, c30)):
        east, west = row_edges(c)
        out.append(v + east * (roll(v, -1) - v) + west * (roll(v, 1) - v) + jnp.minimum(c, d) * (w - v))
    return out


def rim_pack(vp, cp):
    kind, inner, south, north = pack_edges(cp)
    beside = jnp.where(kind == 1, roll(vp, 1), roll(vp, -1))
    return vp + inner * (beside - vp) + south * (roll(vp, -4) - vp) + north * (roll(vp, 4) - vp)


def pack_messages(vp, cp, pp, north=(), south=()):
    lane = lane_of(vp)
    kind = lane & 3
    east = jnp.where(kind == 0, roll(vp, -1), jnp.where(kind == 1, cp, roll(pp, 1)))
    west = jnp.where(kind == 0, roll(vp, -2), jnp.where(kind == 1, roll(cp, -1), pp))
    for k, x in zip((3, 7, 11, 15), (*north, *south)):
        east = jnp.where(lane == k, roll(x, k + 1), east)
        west = jnp.where(lane == k, roll(x, k), west)
    return east, west


def ghost_pack(from_w, from_e):
    one = (lane_of(from_w) & 3) == 1
    v = jnp.where(one, roll(from_e, 1), roll(from_w, 2))
    c = jnp.where(one, from_e, roll(from_w, 1))
    p = jnp.where(one, roll(from_e, -1), from_w)
    return v, c, p


def corner_pack(from_w, from_e):
    lane = lane_of(from_w)
    out = []
    for n, s in ((3, 11), (7, 15)):
        x = jnp.zeros_like(from_w)
        for at, src, k in ((1, from_e, n), (2, from_w, n), (LANES - 3, from_e, s), (LANES - 2, from_w, s)):
            x = jnp.where(lane == at, roll(src, at - k), x)
        out.append(x)
    return out


def pack_correction(vp, pp, cp, gv, gc, gp, more_ghost=0.0, more_whole=0.0):
    kind, inner, south, north = pack_edges(cp)
    mid = (kind == 1) | (kind == 2)
    mg = jnp.where(mid, jnp.minimum(cp, gc), 0.0)
    f = mg * (gv - vp)
    qf = inner * f
    again = mg * (gp - f + more_ghost - (pp + f + more_whole))
    rp = f - qf + south * (roll(f, -4) - f) + north * (roll(f, 4) - f) + again
    return jnp.where(mid, rp, jnp.where(kind == 0, roll(qf, -1), roll(qf, 1))), f


def rim_correction(own, coef, ghosts, complete=False):
    v0, v31, p0, p31, vp, pp = own
    c0, c1, c30, c31, cp = coef
    (gvn, gcn, gpn), (gvs, gcs, gps), (gv, gc, gp), (kv, kc) = ghosts
    lane = lane_of(v0)
    ends = (lane == 0) | (lane == LANES - 1)
    mn, ms = jnp.minimum(c0, gcn), jnp.minimum(c31, gcs)
    fn, fs = mn * (gvn - v0), ms * (gvs - v31)
    more_ghost = jnp.where(((lane & 3) == 1) | ((lane & 3) == 2), jnp.minimum(gc, kc), 0.0) * (kv - gv)
    more_whole = jnp.where((lane == 1) | (lane == 2), roll(fn, 2), 0.0)
    more_whole = more_whole + jnp.where((lane == LANES - 3) | (lane == LANES - 2), roll(fs, -2), 0.0)
    rp, f = pack_correction(vp, pp, cp, gv, gc, gp, more_ghost, more_whole)
    ghost_n, ghost_s = gpn - fn, gps - fs
    if not complete:
        ghost_n = ghost_n + jnp.where(ends, jnp.minimum(gcn, roll(kc, -2)), 0.0) * (roll(kv, -2) - gvn)
        ghost_s = ghost_s + jnp.where(ends, jnp.minimum(gcs, roll(kc, 2)), 0.0) * (roll(kv, 2) - gvs)
    whole_n = p0 + fn + jnp.where(ends, roll(f, -2), 0.0)
    whole_s = p31 + fs + jnp.where(ends, roll(f, 2), 0.0)
    rows = []
    for c, d, m, g, w, x in ((c0, c1, mn, ghost_n, whole_n, fn), (c31, c30, ms, ghost_s, whole_s, fs)):
        east, west = row_edges(c)
        across = jnp.minimum(c, d)
        rows.append(x + east * (roll(x, -1) - x) + west * (roll(x, 1) - x) - across * x + m * (g - w))
        rows.append(across * x)
    return rows[0], rows[1], rows[3], rows[2], rp


def sweep(src, edges, emit):
    east, west, south = edges
    for i in range(ROWS):
        x = src[i]
        y = x + east[i] * (roll(x, -1) - x) + west[i] * (roll(x, 1) - x)
        if i < ROWS - 1:
            y = y + south[i] * (src[i + 1] - x)
        if i > 0:
            y = y + south[i - 1] * (src[i - 1] - x)
        emit(i, y)


def chosen(cells, ids):
    return jnp.where(ids == cells, 1.0, 0.0).astype(BF16)


def rim_ids(n):
    line = lax.broadcasted_iota(jnp.int32, (LANES, n), 0)
    rows = [line + i * LANES for i in (0, 1, ROWS - 2, ROWS - 1)]
    k = line & 3
    pack = (line >> 2) * LANES + jnp.where(k < 2, LANES - 2 + k, k - 2)
    return jnp.concatenate(rows + [pack], axis=0)


def spans(o):
    a, lane = divmod(CAP * o, LANES)
    if lane + CAP <= LANES:
        return [(a, lane, 0, CAP)]
    return [(a, lane, 0, LANES - lane), (a + 1, lane - LANES, LANES - lane, CAP)]


def merged(old, new, lo, hi):
    if old is None:
        return new
    lane = lane_of(new)
    return jnp.where((lane >= lo) & (lane < hi), new, old)


def by_shift(pairs, a):
    out = {}
    for o in pairs:
        for tile, at, p, q in spans(o):
            if tile == a:
                for g in range(GROUPS):
                    out.setdefault(g - o, []).append((o, g, at + p, CAP * g + p, q - p))
    return out


def pack_payload(columns, out_ref, first, last):
    tail = ROWS - 2 * (GROUPS - 1) - 2
    pairs = range(last - first)
    blocks = [None for _ in pairs]
    for a in range(spans(pairs[-1])[-1][0] + 1):
        if a % 2 == 0:
            both = columns(a // 2)
        x = both[:, LANES * (a % 2) : LANES * (a % 2 + 1)]
        rest = [x[ROWS * g + SENT : ROWS * (g + 1)] for g in range(GROUPS - 1)]
        groups = [x[ROWS * g : ROWS * (g + 1)] for g in range(GROUPS - 1)]
        groups.append(jnp.concatenate([x[ROWS * (GROUPS - 1) :][:tail], *rest, jnp.zeros((2, LANES), F32)], axis=0))
        for d, moves in by_shift(pairs, a).items():
            z = None
            for o, g, src, dst, n in moves:
                z = merged(z, groups[g], src, src + n)
            z = roll(z, CAP * d)
            for o, g, src, dst, n in moves:
                blocks[o] = merged(blocks[o], z, dst, dst + n)
        for o in pairs:
            if spans(o)[-1][0] == a:
                at = SENT * (first + o)
                out_ref[at : at + SENT, :] = blocks[o][:SENT]


def unpack_payload(in_ref, owners, slots):
    pairs = range(owners)
    blocks = [in_ref[SENT * o : SENT * o + ROWS, :] if o < owners - 1 else tall(in_ref[SENT * o :, :], ROWS) for o in pairs]
    pieces = [[None for _ in range(slots // LANES)] for _ in range(GROUPS)]
    for a in range(slots // LANES):
        for d, moves in by_shift(pairs, a).items():
            z = None
            for o, g, dst, src, n in moves:
                z = merged(z, blocks[o], src, src + n)
            z = roll(z, -CAP * d)
            for o, g, dst, src, n in moves:
                pieces[g][a] = merged(pieces[g][a], z, dst, dst + n)
    groups = [jnp.concatenate(x, axis=1) for x in pieces]
    tail = ROWS - 2 * (GROUPS - 1) - 2
    out = []
    for g in range(GROUPS - 1):
        out += [groups[g][:SENT], groups[-1][tail + 2 * g : tail + 2 * (g + 1)]]
    out += [groups[-1][:tail], jnp.zeros((ROWS - tail, slots), F32)]
    return jnp.concatenate(out, axis=0)


def takes(us):
    return pl.CostEstimate(flops=MIB, bytes_accessed=int(us * 3.3e6), transcendentals=0)


def call(kernel, outs, *args, in_specs=None, scratch=(), vmem=48, us=1, **kw):
    any_spec = pl.BlockSpec(memory_space=pltpu.VMEM)
    return pl.pallas_call(
        kernel,
        out_shape=[jax.ShapeDtypeStruct(s, d) for s, d in outs],
        in_specs=in_specs or [any_spec] * len(args),
        scratch_shapes=list(scratch),
        compiler_params=pltpu.CompilerParams(vmem_limit_bytes=vmem * MIB),
        cost_estimate=takes(us),
        **kw,
    )(*args)


HBM = pl.BlockSpec(memory_space=pl.ANY)
VMEM = pl.BlockSpec(memory_space=pltpu.VMEM)


def even(axis):
    return lax.rem(lax.axis_index(axis), 2) == 0


def write_parts(ref, parts, rows):
    for k, x in enumerate(parts):
        ref[rows * k : rows * (k + 1), :] = x[:rows]


def parts_of(ref, rows, vp=None):
    out = [ref[rows * k : rows * (k + 1), :] for k in range(ref.shape[0] // rows)]
    return out if vp is None else [tall(x, vp) for x in out]


def write_pair(axis, first, second, up_parts, down_parts, rows):
    for ref, e, o in ((first, down_parts, up_parts), (second, up_parts, down_parts)):
        write_parts(ref, [jnp.where(even(axis), x, y) for x, y in zip(e, o)], rows)


def read_pair(axis, first, second, rows, vp):
    f, s = parts_of(first, rows, vp), parts_of(second, rows, vp)
    before = [jnp.where(even(axis), y, x) for x, y in zip(f, s)]
    after = [jnp.where(even(axis), x, y) for x, y in zip(f, s)]
    return before, after


ENDS = (0, 1, ROWS - 2, ROWS - 1)


def mask_of(mask, vals, v, rows):
    half, end = vals // 2, min(v + 8, vals)
    if end <= half:
        return mask[v:end, rows, :]
    if v >= half:
        return mask[v - half : end - half, rows, :]
    return jnp.concatenate([mask[v:half, rows, :], mask[: end - half, rows, :]], axis=0)


def eight(x):
    n = x.shape[0]
    return x if n == 8 else jnp.concatenate([x, jnp.zeros((8 - n, *x.shape[1:]), x.dtype)], axis=0)


def rows_kernel(vals, vp, mp, state, diff, mask, m_1, m_2, rv, rc, done, sv, sd, sm, sems):
    done[...] = jnp.zeros(done.shape, F32)
    copies = []
    for src, dst, n in ((state, sv, vals), (diff, sd, vals), (mask, sm, vals // 2)):
        for k, i in enumerate((0, ROWS - 2)):
            at = dst.at[pl.ds(0, n), pl.ds(2 * k, 2)]
            copies.append(pltpu.make_async_copy(src.at[:, pl.ds(i, 2)], at, sems.at[len(copies)]))
            copies[-1].start()
    for c in copies:
        c.wait()
    v_tiles, c_tiles = [], []
    for v in range(0, vals, 8):
        end = min(v + 8, vals)
        c = sd[v:end] * mask_of(sm, vals, v, slice(0, 8)).astype(F32)
        for tiles, x in ((v_tiles, sv[v:end]), (c_tiles, c)):
            y = jnp.swapaxes(eight(x), 0, 1)
            tiles.append([y[k] for k in range(4)])
    v0, v1, v30, v31 = (tall(jnp.concatenate([t[k] for t in v_tiles], axis=0), vp) for k in range(4))
    c0, c1, c30, c31 = (tall(jnp.concatenate([t[k] for t in c_tiles], axis=0), vp) for k in range(4))
    p0, p31 = rim_rows(v0, v1, v30, v31, c0, c1, c30, c31)
    write_pair("lat", m_1, m_2, (v0, c0, p0), (v31, c31, p31), mp)
    write_parts(rv, (v0, v31, p0, p31), vp)
    write_parts(rc, (c0, c1, c30, c31), vp)


def by_grid_row(x, dst, first):
    y = jnp.swapaxes(eight(x), 0, 1)
    v, i = first
    for k in range(8):
        dst[i + k, v : v + 8, :] = y[k]


def outer_columns(ref):
    total = jnp.zeros((2 * ref.shape[1], LANES), F32)
    r = lax.broadcasted_iota(jnp.int32, (2 * LANES, LANES), 0)
    lane = lax.broadcasted_iota(jnp.int32, (2 * LANES, LANES), 1)
    source = (lane >> 2) * LANES + jnp.where((lane & 3) < 2, LANES - 2 + (lane & 3), (lane & 3) - 2)
    for i in range(0, ROWS, 2):
        take = jnp.where(r == source - i * LANES, 1.0, 0.0).astype(BF16)
        total = total + dot(stacked(jnp.concatenate([ref[i], ref[i + 1]], axis=1)), take)
    return folded(total)


def sweeps_kernel(vals, vp, state, diff, mask, after, field, mid, east, west, south, pk, coef):
    half = vals // 2
    for v in range(0, vp, 8):
        if v >= vals:
            for ref in (field, coef):
                ref[:, v : v + 8, :] = jnp.zeros((ROWS, 8, LANES), F32)
            continue
        end = min(v + 8, vals)
        for i in range(0, ROWS, 8):
            rows = slice(i, i + 8)
            m = mask_of(mask, vals, v, rows)
            by_grid_row(state[v:end, rows, :], field, (v, i))
            by_grid_row(diff[v:end, rows, :] * m.astype(F32), coef, (v, i))
    lane = lax.broadcasted_iota(jnp.int32, (vp, LANES), 1)
    c = coef[0]
    for i in range(ROWS):
        if i < ROWS - 1:
            cn = coef[i + 1]
            south[i] = jnp.minimum(c, cn)
        else:
            south[i] = jnp.zeros_like(c)
        e = jnp.where(lane == LANES - 1, 0.0, jnp.minimum(c, roll(c, -1)))
        w = roll(e, 1)
        east[i], west[i] = e, w
        x = field[i]
        y = x + e * (roll(x, -1) - x) + w * (roll(x, 1) - x)
        if i < ROWS - 1:
            y = y + south[i] * (field[i + 1] - x)
        if i > 0:
            y = y + south[i - 1] * (field[i - 1] - x)
        mid[i] = y
        c = cn
    pv, pc = outer_columns(field), outer_columns(coef)
    write_parts(pk, (pv, pc, rim_pack(pv, pc)), vp)


def lon_kernel(vp, mp, g_1, g_2, pk, m_1, m_2):
    north, south = read_pair("lat", g_1, g_2, mp, vp)
    east, west = pack_messages(*parts_of(pk, vp), north[:2], south[:2])
    write_pair("lon", m_1, m_2, (west,), (east,), mp)


def select_kernel(mid, east, west, south, cells, out, smooth, hot):
    def split(i, y):
        smooth[:, LANES * i : LANES * (i + 1)] = stacked(y)

    sweep(mid, (east, west, south), split)
    chunk = hot.shape[1]
    wide = 4 * LANES
    for base in range(0, cells.shape[1], chunk):
        for k in range(0, ROWS * LANES, wide):
            ids = lax.broadcasted_iota(jnp.int32, (wide, chunk), 0) + k
            hot[k : k + wide, :] = chosen(cells[:, base : base + chunk], ids)
        total = jnp.zeros((smooth.shape[0], chunk), F32)
        for k in range(0, ROWS * LANES, wide):
            total = total + dot(smooth[:, k : k + wide], hot[k : k + wide, :])
        out[:, base : base + chunk] = folded(total)


def weights_kernel(slots, weights, hi, lo):
    taps = range(slots.shape[0])
    at = [slots[k : k + 1, :] for k in taps]
    w = [weights[k : k + 1, :] for k in taps]
    for a in taps:
        for b in range(a + 1, len(taps)):
            same = at[a] == at[b]
            w[a] = w[a] + jnp.where(same, w[b], 0.0)
            at[b] = jnp.where(same, -1, at[b])
    at = [x.astype(jnp.int16) for x in at]
    parts = [halves(x) for x in w]
    shape = (LANES, hi.shape[1])
    for r in range(0, hi.shape[0], LANES):
        row = (lax.broadcasted_iota(jnp.int32, shape, 0) + r).astype(jnp.int16)
        h = l = jnp.zeros(shape, BF16)
        for k in taps:
            here = row == at[k]
            h, l = jnp.where(here, parts[k][0], h), jnp.where(here, parts[k][1], l)
        hi[r : r + LANES, :] = h
        lo[r : r + LANES, :] = l


def read_ghosts(vp, mp, lat, lon):
    north, south = read_pair("lat", *lat, mp, vp)
    west, east = read_pair("lon", *lon, mp, vp)
    return north, south, ghost_pack(west[0], east[0]), corner_pack(west[0], east[0])


def send_kernel(owners, vp, mp, g_1, g_2, h_1, h_2, rv, rc, pk, inner, cells, out):
    ghosts = read_ghosts(vp, mp, (g_1, g_2), (h_1, h_2))
    v0, v31, p0, p31 = parts_of(rv, vp)
    pv, pc, pp = parts_of(pk, vp)
    fix = rim_correction((v0, v31, p0, p31, pv, pp), parts_of(rc, vp) + [pc], ghosts)
    wide = 2 * LANES
    fix = stacked(jnp.concatenate(fix, axis=1))
    ids = rim_ids(wide)

    def columns(k):
        at = slice(wide * k, wide * (k + 1))
        return inner[:, at] + folded(dot(fix, chosen(cells[:, at], ids)))

    pack_payload(columns, out, 0, owners)


def owner_kernel(vals, vp, owners, got, w_hi, w_lo, prec, equiv, back, r2, w2):
    r2[...] = stacked(unpack_payload(got, owners, r2.shape[1]))
    wide = min(512, equiv.shape[1])
    for q in range(0, equiv.shape[1], wide):
        at = slice(q, q + wide)
        e = (folded(dot(r2[...], w_hi[:, at])) + dot(r2[:vp, :], w_lo[:, at]))[:vals]
        equiv[:, at] = e
        w2[:, at] = stacked(tall(prec[:, at] * e, vp))
    for o in range(0, r2.shape[1], CHUNK):

        def columns(k):
            at = slice(o + 2 * LANES * k, o + 2 * LANES * (k + 1))
            return folded(dot_nt(w2[...], w_hi[at, :])) + dot_nt(w2[:vp, :], w_lo[at, :])

        pack_payload(columns, back, o // CAP, (o + CHUNK) // CAP)


def back_kernel(owners, vp, mp, got, cells, rc, pk, m_1, m_2, inc, ra, pa):
    slots = cells.shape[1]
    x = stacked(unpack_payload(got, owners, slots))
    inc[...] = x
    rims = folded(dot_nt(x, chosen(cells[...], rim_ids(slots))))
    v0, v1, v30, v31, pv = (rims[:, LANES * k : LANES * (k + 1)] for k in range(5))
    pc = pk[vp : 2 * vp, :]
    pp = rim_pack(pv, pc)
    east, west = pack_messages(pv, pc, pp)
    write_pair("lon", m_1, m_2, (west,), (east,), mp)
    write_parts(ra, (v0, v31, *rim_rows(v0, v1, v30, v31, *parts_of(rc, vp))), vp)
    write_parts(pa, (pv, pp), vp)


def back_ghosts(vp, mp, lon, lon_back):
    west, east = read_pair("lon", *lon, mp, vp)
    _, gc, _ = ghost_pack(west[0], east[0])
    west, east = read_pair("lon", *lon_back, mp, vp)
    gv, _, gp = ghost_pack(west[0], east[0])
    return gv, gc, gp


def lat_kernel(vals, vp, mp, h_1, h_2, b_1, b_2, pk, ra, pa, m_1, m_2):
    ghosts = back_ghosts(vp, mp, (h_1, h_2), (b_1, b_2))
    pv, pp = parts_of(pa, vp)
    v0, v31, p0, p31 = parts_of(ra, vp)
    _, f = pack_correction(pv, pp, pk[vp : 2 * vp, :], *ghosts)
    lane = lane_of(f)
    ends = (lane == 0) | (lane == LANES - 1)
    t = tall(ghosts[0], 2 * LANES).T

    def part(x, k):
        return tall(jnp.concatenate([x[:vals], t[k : k + 1, :LANES], t[k : k + 1, LANES:]], axis=0), mp)

    north = part(v0, 2), part(p0 + jnp.where(ends, roll(f, -2), 0.0), 1)
    south = part(v31, LANES - 2), part(p31 + jnp.where(ends, roll(f, 2), 0.0), LANES - 3)
    write_pair("lat", m_1, m_2, north, south, mp)


def lat_corners(vals, vp, north, south):
    row = lax.broadcasted_iota(jnp.int32, (LANES, 2 * LANES), 0)
    t = jnp.zeros((LANES, 2 * LANES), F32)
    for k, x in ((2, north[0]), (1, north[1]), (LANES - 2, south[0]), (LANES - 3, south[1])):
        t = jnp.where(row == k, jnp.concatenate([x[vals : vals + 1], x[vals + 1 : vals + 2]], axis=1), t)
    return t.T[:vp]


def adjoint_kernel(vp, inc, cells, east, west, south, out, adj):
    wide = 2 * LANES
    slots = cells.shape[1]
    for k in range(ROWS // 2):
        ids = lax.broadcasted_iota(jnp.int32, (wide, slots), 0) + k * wide
        x = folded(dot_nt(inc[...], chosen(cells[...], ids)))
        for j in range(2):
            adj[2 * k + j] = x[:, LANES * j : LANES * (j + 1)]

    def keep(i, y):
        out[i] = y

    sweep(adj, (east, west, south), keep)


def second_kernel(vals, vp, mp, mid, east, west, south, field, h_1, h_2, b_1, b_2, pk, pa, out, part, buf, sems):
    pv, pp = parts_of(pa, vp)
    fix, _ = pack_correction(pv, pp, pk[vp : 2 * vp, :], *back_ghosts(vp, mp, (h_1, h_2), (b_1, b_2)))
    lane = lane_of(fix)
    outer = (lane < 2) | (lane >= LANES - 2)
    copies = []

    def add(i, y):
        x = y + field[i]
        if i in ENDS:
            part[ENDS.index(i)] = x
            return
        buf[i] = x + jnp.where(outer, roll(fix, -(4 * i + 2)), 0.0)
        copies.append(pltpu.make_async_copy(buf.at[i, pl.ds(0, vals)], out.at[:, i], sems.at[i]))
        copies[-1].start()

    sweep(mid, (east, west, south), add)
    for c in copies:
        c.wait()


def final_kernel(vals, vp, mp, most, g_1, g_2, h_1, h_2, a_1, a_2, b_1, b_2, ra, rc, pk, pa, part, out, buf, sems):
    gn, gs, _, (_, kc) = read_ghosts(vp, mp, (g_1, g_2), (h_1, h_2))
    an, az = read_pair("lat", a_1, a_2, mp, vp)
    beside = back_ghosts(vp, mp, (h_1, h_2), (b_1, b_2))
    ghosts = (an[0], gn[1], an[1]), (az[0], gs[1], az[1]), beside, (lat_corners(vals, vp, an, az), kc)
    v0, v31, p0, p31 = parts_of(ra, vp)
    pv, pp = parts_of(pa, vp)
    coef = parts_of(rc, vp) + [pk[vp : 2 * vp, :]]
    *rows, fix = rim_correction((v0, v31, p0, p31, pv, pp), coef, ghosts, complete=True)
    lane = lane_of(fix)
    outer = (lane < 2) | (lane >= LANES - 2)
    copies = []
    for k, i in enumerate(ENDS):
        buf[k] = part[k] + rows[k] + jnp.where(outer, roll(fix, -(4 * i + 2)), 0.0)
        copies.append(pltpu.make_async_copy(buf.at[k, pl.ds(0, vals)], out.at[:, i], sems.at[k]))
        copies[-1].start()
    for c in copies:
        c.wait()


def swap(axis, x, first):
    n = lax.axis_size(axis)
    pairs = []
    for i in range(n):
        j = i + 1 if (i % 2 == 0) == first else i - 1
        if axis == "lon":
            j %= n
        if 0 <= j < n:
            pairs.append((i, j))
    return lax.ppermute(x, axis, pairs)


def exchange(axis, m_1, m_2):
    g_2 = swap(axis, m_2, False)
    g_1 = swap(axis, m_1, True)
    return g_1, g_2


def across(x):
    flat = x.reshape(lax.axis_size(("lon", "lat")), 1, SENT * LANES)
    return lax.all_to_all(flat, ("lon", "lat"), split_axis=0, concat_axis=0, tiled=True).reshape(x.shape)


def on_device(state, diffusivity, sea_mask, send_cols, obs_slots, obs_weights, obs_precision):
    vals, taps, obs = state.shape[0], obs_slots.shape[0], obs_slots.shape[1]
    owners = send_cols.shape[1] // CAP
    vp, mp = up(vals, ROWS), up(vals + 2, 8)
    slots = owners * CAP
    cell_count = ROWS * LANES
    cells = send_cols
    blocks = ((owners * SENT, LANES), F32)
    lines = lambda n, rows, dtype=F32: ((n * rows, LANES), dtype)
    field = ((ROWS, vp, LANES), F32)

    *lat_out, rv, rc, done = call(
        functools.partial(rows_kernel, vals, vp, mp),
        [lines(3, mp), lines(3, mp), lines(4, vp), lines(4, vp), lines(1, 8)],
        state, diffusivity, sea_mask,
        in_specs=[HBM] * 3,
        scratch=[pltpu.VMEM((n, 8, LANES), d) for n, d in ((vp, F32), (vp, F32), (vp // 2, jnp.int32))]
        + [pltpu.SemaphoreType.DMA((6,))],
        vmem=62,
    )
    lat_in = exchange("lat", *lat_out)
    wide = obs if slots <= 1024 else 512
    obs_weights, done = lax.optimization_barrier((obs_weights, done))
    w_hi, w_lo = pl.pallas_call(
        weights_kernel,
        grid=(obs // wide,),
        out_shape=[jax.ShapeDtypeStruct((slots, obs), BF16)] * 2,
        in_specs=[pl.BlockSpec((taps, wide), lambda j: (0, j))] * 2,
        out_specs=[pl.BlockSpec((slots, wide), lambda j: (0, j))] * 2,
        compiler_params=pltpu.CompilerParams(vmem_limit_bytes=20 * MIB),
        cost_estimate=pl.CostEstimate(flops=int(4e9), bytes_accessed=int(80e6), transcendentals=0),
    )(obs_slots, obs_weights)
    whole, once, east, west, south, pk = call(
        functools.partial(sweeps_kernel, vals, vp),
        [field, field, field, field, field, lines(3, vp)],
        state, diffusivity, sea_mask, w_hi,
        in_specs=[VMEM] * 3 + [HBM],
        scratch=[pltpu.VMEM((ROWS, vp, LANES), F32)],
        vmem=24,
        us=8,
    )
    lon_out = call(
        functools.partial(lon_kernel, vp, mp),
        [lines(1, mp)] * 2, *lat_in, pk,
        vmem=8,
    )
    lon_in = exchange("lon", *lon_out)
    (inner,) = call(
        select_kernel,
        [((vp, slots), F32)],
        once, east, west, south, cells,
        scratch=[pltpu.VMEM((2 * vp, cell_count), BF16), pltpu.VMEM((cell_count, CHUNK), BF16)],
        vmem=24,
        us=3,
    )
    (payload,) = call(
        functools.partial(send_kernel, owners, vp, mp),
        [blocks],
        *lat_in, *lon_in, rv, rc, pk, inner, cells,
        vmem=24,
    )
    payload, w_hi, w_lo = lax.optimization_barrier((payload, w_hi, w_lo))
    received = across(payload)
    matrix = 4 * slots * obs // MIB
    equivalents, payload = call(
        functools.partial(owner_kernel, vals, vp, owners),
        [((vals, obs), F32), blocks],
        received, w_hi, w_lo, obs_precision,
        scratch=[pltpu.VMEM((2 * vp, slots), BF16), pltpu.VMEM((2 * vp, obs), BF16)],
        vmem=20 + matrix,
    )
    incoming = across(payload)
    *lon_out, inc, ra, pa = call(
        functools.partial(back_kernel, owners, vp, mp),
        [lines(1, mp)] * 2 + [((2 * vp, slots), BF16), lines(4, vp), lines(2, vp)],
        incoming, cells, rc, pk,
        vmem=24,
    )
    lon_back = exchange("lon", *lon_out)
    (mid,) = call(
        functools.partial(adjoint_kernel, vp),
        [field],
        inc, cells, east, west, south,
        scratch=[pltpu.VMEM((ROWS, vp, LANES), F32)],
        vmem=24,
        us=4,
    )
    lon_back, mid = lax.optimization_barrier((lon_back, mid))
    lat_out = call(
        functools.partial(lat_kernel, vals, vp, mp),
        [lines(2, mp)] * 2, *lon_in, *lon_back, pk, ra, pa,
        vmem=8,
    )
    lat_back = exchange("lat", *lat_out)
    most, part = call(
        functools.partial(second_kernel, vals, vp, mp),
        [(state.shape, F32), ((len(ENDS), vp, LANES), F32)],
        mid, east, west, south, whole, *lon_in, *lon_back, pk, pa,
        scratch=[pltpu.VMEM((ROWS, vp, LANES), F32), pltpu.SemaphoreType.DMA((ROWS,))],
        out_specs=[HBM, VMEM],
        vmem=20,
        us=4,
    )
    (product,) = call(
        functools.partial(final_kernel, vals, vp, mp),
        [(state.shape, F32)],
        most, *lat_in, *lon_in, *lat_back, *lon_back, ra, rc, pk, pa, part,
        in_specs=[HBM] + [VMEM] * 13,
        scratch=[pltpu.VMEM((len(ENDS), vp, LANES), F32), pltpu.SemaphoreType.DMA((len(ENDS),))],
        out_specs=[HBM],
        input_output_aliases={0: 0},
        vmem=16,
    )
    return product, equivalents


def solution(mesh):
    placed = (
        P(None, "lat", "lon"),
        P(None, "lat", "lon"),
        P(None, "lat", "lon"),
        P(("lon", "lat"), None),
        P(None, ("lon", "lat")),
        P(None, ("lon", "lat")),
        P(None, ("lon", "lat")),
    )
    return jax.shard_map(
        on_device,
        mesh=mesh,
        in_specs=placed,
        out_specs=(P(None, "lat", "lon"), P(None, ("lon", "lat"))),
        check_vma=False,
    )
```
